32 devices in a mesh: dp: 2 (over x), blk: 4 (over z), tensor: 4 (over y, core).
Axes of the slice: x: 2, y: 2, z: 4, core: 2. Of those that a mesh axis runs over, the one named last changes fastest.
Arguments:
- block_input: bfloat16 [4, 2048, 2048], P('dp', 'blk', 'tensor'), may hold values from -6 to 6
- segment_ids: int32 [4, 2048], P('dp'), may hold values from 0 to 7, as said below
- layer_norm_gain: float32 [2048], replicated, may hold values from 0.5 to 1.5
- layer_norm_bias: float32 [2048], replicated, may hold values from -4 to 4
- qkv_weight: bfloat16 [2048, 3, 2048], P(None, None, 'tensor'), may hold values from -0.125 to 0.125
- qkv_bias: float32 [3, 2048], P(None, 'tensor'), may hold values from -0.4375 to 0.4375
- out_weight: bfloat16 [2048, 2048], P('tensor'), may hold values from -2 to 2
- out_bias: float32 [2048], P('tensor'), may hold values from -4 to 4
- up_weight: bfloat16 [2048, 8192], P(None, 'tensor'), may hold values from -0.125 to 0.125
- up_bias: float32 [8192], P('tensor'), may hold values from -4 to 4
- down_weight: bfloat16 [8192, 2048], P('tensor'), may hold values from -0.0625 to 0.0625
- down_bias: float32 [2048], P('tensor'), may hold values from -4 to 4
- grad_output: bfloat16 [4, 2048, 2048], P('dp', 'blk', 'tensor'), may hold values from -6 to 6
Outputs:
- block_output: bfloat16 [4, 2048, 2048], P('dp', 'blk', 'tensor')
- input_grad: bfloat16 [4, 2048, 2048], P('dp', 'blk', 'tensor')
- norm_gain_grad: float32 [2048], P('tensor')
- norm_bias_grad: float32 [2048], P('tensor')
- qkv_weight_grad: float32 [2048, 3, 2048], P(None, None, 'tensor')
- qkv_bias_grad: float32 [3, 2048], P(None, 'tensor')
- out_weight_grad: float32 [2048, 2048], P('tensor')
- out_bias_grad: float32 [2048], P('tensor')
- up_weight_grad: float32 [2048, 8192], P(None, 'tensor')
- up_bias_grad: float32 [8192], P('tensor')
- down_weight_grad: float32 [8192, 2048], P('tensor')
- down_bias_grad: float32 [2048], P('tensor')
The draws below stay inside these ranges and needn't reach their ends.
Inputs may be any that keep to these rules, and one draw needn't show every extreme that they name: `segment_ids`: segment ids never fall along a row; each row uses every id from 0 to 7, and in each row one document holds every position from 256 to 1792.
All inputs are finite; a program needn't handle non-finite values.
Results may differ from the reference program's by a relative error of at most 0.02.
Values may be sent and summed in bfloat16 or wider, within the bound.
A program may use at most 320 MiB of HBM per device.

```python
import math
import jax
import jax.numpy as jnp
from jax import lax

D = 2048
H = 32
HD = 64
ROT = 32
FF = 8192
SEQ = 2048
ROWS = 4
BLOCK_LEN = 512


def draw_segment_ids(key, part):
    key = jax.random.fold_in(key, 11)
    row_keys = jax.random.split(key, ROWS)

    def one_row(row_key):
        pieces = jax.random.split(row_key, 4)
        head_end = jax.random.randint(pieces[0], (), 8, BLOCK_LEN // 2)
        tail_len = jax.random.randint(pieces[1], (), 8, BLOCK_LEN // 2)
        long_stop = SEQ - tail_len
        counter = jnp.arange(3).astype(jnp.int32)
        early_cuts = jax.random.randint(pieces[2], (3,), counter * head_end // 4 + 1, (counter + 1) * head_end // 4)
        pair = jnp.arange(2).astype(jnp.int32)
        late_cuts = jax.random.randint(pieces[3], (2,), long_stop + pair * tail_len // 3 + 1, long_stop + (pair + 1) * tail_len // 3)
        all_cuts = jnp.concatenate([early_cuts, head_end[None], long_stop[None], late_cuts])
        places = jnp.arange(SEQ).astype(jnp.int32)
        return jnp.sum((places[:, None] >= all_cuts[None, :]).astype(jnp.int32), axis=1)
    return jax.vmap(one_row)(row_keys).astype(jnp.int32)


def steps_of(own_key, extent, cuts, smallest, high):
    level, own = 1.0, jax.random.fold_in(own_key, 6)
    for axis_at, shards_of in cuts:
        steps = jnp.exp(jax.random.uniform(jax.random.fold_in(own, axis_at), (shards_of,), jnp.float32, smallest / len(cuts), high / len(cuts)))
        level = level * jnp.repeat(steps, extent[axis_at] // shards_of).reshape([-1 if axis == axis_at else 1 for axis in range(len(extent))])
    return level


def noise(key, extent, deviation, bound, cuts=(), kind=jnp.bfloat16):
    gain = steps_of(key, extent, cuts, -0.22, 0.18) if cuts else 1.0
    entries = jax.random.normal(key, extent, jnp.float32) * deviation * gain
    return jnp.minimum(jnp.maximum(entries, -bound), bound).astype(kind)


def setup_inputs(seed: int = 0) -> dict:
    key_of = jax.random.split(jax.random.key(seed), 14)
    block_input = noise(key_of[0], (ROWS, SEQ, D), 1.0, 6.0, ((0, 2), (1, 4), (2, 4)))
    segment_ids = draw_segment_ids(jax.random.fold_in(key_of[13], 71), 0)
    layer_norm_gain = jnp.clip(1.0 + 0.1 * jax.random.normal(key_of[2], (D,), jnp.float32), 0.5, 1.5)
    layer_norm_bias = noise(key_of[3], (D,), 0.3, 4.0, (), jnp.float32)
    qkv_weight = noise(key_of[4], (D, 3, H * HD), D ** -0.5, 0.125, ((2, 4),))
    qkv_bias = noise(key_of[5], (3, H * HD), 0.03, 0.4375, ((1, 4),), jnp.float32)
    out_weight = noise(key_of[6], (H * HD, D), (max(H * HD // 256, 1)) ** -0.5, 2.0, ((0, 4),))
    out_bias = noise(key_of[7], (D,), 0.3, 4.0, ((0, 4),), jnp.float32)
    up_weight = noise(key_of[8], (D, FF), D ** -0.5, 0.125, ((1, 4),))
    up_bias = noise(key_of[9], (FF,), 0.3, 4.0, ((0, 4),), jnp.float32)
    down_weight = noise(key_of[10], (FF, D), FF ** -0.5, 0.0625, ((0, 4),))
    down_bias = noise(key_of[11], (D,), 0.3, 4.0, ((0, 4),), jnp.float32)
    grad_output = noise(key_of[12], (ROWS, SEQ, D), 1.0, 6.0, ((0, 2), (1, 4), (2, 4)))
    return {"block_input": block_input, "segment_ids": segment_ids, "layer_norm_gain": layer_norm_gain, "layer_norm_bias": layer_norm_bias, "qkv_weight": qkv_weight, "qkv_bias": qkv_bias, "out_weight": out_weight, "out_bias": out_bias, "up_weight": up_weight, "up_bias": up_bias, "down_weight": down_weight, "down_bias": down_bias, "grad_output": grad_output}


@jax.custom_vjp
def low(v):
    return lax.optimization_barrier(v.astype(jnp.bfloat16)).astype(jnp.float32)

@jax.custom_vjp
def low_back(v):
    return v

def low_keep(v):
    return (low(v), None)

def low_pass(kept, grad):
    return (grad,)

def back_keep(v):
    return (v, None)

def back_low(kept, grad):
    return (low(grad),)
low.defvjp(low_keep, low_pass)
low_back.defvjp(back_keep, back_low)
EPSILON = 1e-05
ROPE_LOG_BASE = math.log(10000.0)
PRECISE = lax.Precision.HIGHEST
NEGATIVE = -1e+30

def both_ways(source):
    return low_back(low(source))

def document_offsets(segment_ids):
    places = jnp.arange(segment_ids.shape[1]).astype(jnp.int32)
    changed = jnp.concatenate([jnp.ones((segment_ids.shape[0], 1), dtype=bool), segment_ids[:, 1:] != segment_ids[:, :-1]], axis=1)
    starts = lax.cummax(jnp.where(changed, places[None, :], jnp.zeros_like(segment_ids)), axis=1)
    return (places[None, :] - starts).astype(jnp.float32)

def rotary_tables(positions):
    half_rot = ROT // 2
    steps_float = jnp.arange(half_rot).astype(jnp.float32)
    inverse_freq = jnp.exp(steps_float * (-2.0 / ROT) * ROPE_LOG_BASE)
    angles = positions[..., None] * inverse_freq
    return (jnp.cos(angles), jnp.sin(angles))

def rotate(source, cos_t, sin_t):
    half_rot = ROT // 2
    front_half = source[..., :half_rot]
    back_half = source[..., half_rot:ROT]
    cos_b = cos_t[..., None, :]
    sin_b = sin_t[..., None, :]
    return jnp.concatenate([front_half * cos_b - back_half * sin_b, back_half * cos_b + front_half * sin_b, source[..., ROT:]], axis=-1)

def one_head(query, keys, values, segment):
    scores = low_back(jnp.dot(query, keys.T, precision=PRECISE) * HD ** (-0.5))
    places = jnp.arange(SEQ)
    allowed = (segment[:, None] == segment[None, :]) & (places[:, None] >= places[None, :])
    probs = low(jax.nn.softmax(jnp.where(allowed, scores, NEGATIVE), axis=-1))
    return jnp.dot(probs, values, precision=PRECISE)

def attention(queries, keys, values, segment_ids):
    checked = jax.checkpoint(one_head)

    def per_row(row_items):
        query_row, key_row, value_row, segment_row = row_items

        def per_head(head_items):
            return checked(head_items[0], head_items[1], head_items[2], segment_row)
        heads_out = lax.map(per_head, (jnp.swapaxes(query_row, 0, 1), jnp.swapaxes(key_row, 0, 1), jnp.swapaxes(value_row, 0, 1)))
        return jnp.swapaxes(heads_out, 0, 1)
    return lax.map(per_row, (queries, keys, values, segment_ids))

def forward(block_input, layer_norm_gain, layer_norm_bias, qkv_weight, qkv_bias, out_weight, out_bias, up_weight, up_bias, down_weight, down_bias, segment_ids):
    row_mean = lax.optimization_barrier(jnp.mean(block_input, axis=-1, keepdims=True))
    mean_centered = block_input - row_mean
    variance = lax.optimization_barrier(jnp.mean(mean_centered * mean_centered, axis=-1, keepdims=True))
    normalized_rows = low(mean_centered * lax.rsqrt(variance + EPSILON) * layer_norm_gain + layer_norm_bias)
    qkv_all = low_back(jnp.einsum('rsd,dke->rske', normalized_rows, qkv_weight, precision=PRECISE) + qkv_bias)
    qkv_split = qkv_all.reshape(ROWS, SEQ, 3, H, HD)
    cos_t, sin_t = rotary_tables(document_offsets(segment_ids))
    queries = low(rotate(qkv_split[:, :, 0], cos_t, sin_t))
    keys = low(rotate(qkv_split[:, :, 1], cos_t, sin_t))
    values = low(qkv_split[:, :, 2])
    attended = both_ways(attention(queries, keys, values, segment_ids)).reshape(ROWS, SEQ, H * HD)
    hidden = low_back(jnp.einsum('rsd,df->rsf', normalized_rows, up_weight, precision=PRECISE) + up_bias)
    active = low(jax.nn.gelu(hidden, approximate=True))
    branch = jnp.einsum('rse,ed->rsd', attended, out_weight, precision=PRECISE) + out_bias
    branch = branch + jnp.einsum('rsf,fd->rsd', active, down_weight, precision=PRECISE) + down_bias
    return block_input + branch

def reference(block_input, segment_ids, layer_norm_gain, layer_norm_bias, qkv_weight, qkv_bias, out_weight, out_bias, up_weight, up_bias, down_weight, down_bias, grad_output):
    primals = (block_input.astype(jnp.float32), layer_norm_gain, layer_norm_bias, qkv_weight.astype(jnp.float32), qkv_bias, out_weight.astype(jnp.float32), out_bias, up_weight.astype(jnp.float32), up_bias, down_weight.astype(jnp.float32), down_bias)

    def layer(*params):
        return forward(*params, segment_ids)
    result, pullback = jax.vjp(layer, *primals)
    grads = pullback(grad_output.astype(jnp.float32))
    return (result.astype(jnp.bfloat16), grads[0].astype(jnp.bfloat16), grads[1], grads[2], grads[3], grads[4], grads[5], grads[6], grads[7], grads[8], grads[9], grads[10])
```

```python
import functools
import math

import jax
import jax.numpy as jnp
from jax import lax
from jax.experimental import pallas as pl
from jax.experimental.pallas import tpu as pltpu
from jax.sharding import PartitionSpec as P

HD = 64
ROT = 32
EPSILON = 1e-05
ROPE_LOG_BASE = math.log(10000.0)
NEGATIVE = -1e30
F32 = jnp.float32
BF = jnp.bfloat16
MESH = pl.DeviceIdType.MESH
dot32 = functools.partial(jnp.dot, preferred_element_type=F32)


def swap(value, axis, size, mask):
    return lax.ppermute(value, axis, [(i, i ^ mask) for i in range(size)])


def turn(source, cos_t, sin_t):
    half = ROT // 2
    front, back = source[:half], source[half:ROT]
    return jnp.concatenate(
        [front * cos_t - back * sin_t, back * cos_t + front * sin_t, source[ROT:]], axis=0
    )


def attention_kernel(
    nz, heads, tile, z_ref, pieces, grads, cos_ref, sin_ref, start_ref, out_ref,
    q_t, k_t, v_t, g_t, q_n, k_n, v_n, g_n, probs, dk_acc, dv_acc,
):
    z = z_ref[0]
    length = pieces[0].shape[0]
    width = heads * HD
    scale = HD**-0.5
    hs = range(heads)

    for m in range(nz):
        place = pl.ds(pl.multiple_of(jnp.bitwise_xor(z, m) * length, length), length)
        cos_t, sin_t = cos_ref[:, place], sin_ref[:, place]
        for h in hs:
            low = h * HD
            x = turn(pieces[m][:, low : low + HD].astype(F32).T, cos_t, sin_t) * scale
            q_t[h, :, place] = x.astype(BF)
            q_n[h, place, :] = x.T.astype(BF)
            low = width + h * HD
            x = turn(pieces[m][:, low : low + HD].astype(F32).T, cos_t, sin_t)
            k_t[h, :, place] = x.astype(BF)
            k_n[h, place, :] = x.T.astype(BF)
            low = 2 * width + h * HD
            x = pieces[m][:, low : low + HD]
            v_n[h, place, :] = x
            v_t[h, :, place] = x.astype(F32).T.astype(BF)
            x = grads[m][:, h * HD : h * HD + HD]
            g_n[h, place, :] = x
            g_t[h, :, place] = x.astype(F32).T.astype(BF)
    dk_acc[...] = jnp.zeros_like(dk_acc)
    dv_acc[...] = jnp.zeros_like(dv_acc)

    def one_tile(i, _):
        qs = pl.ds(pl.multiple_of(i * tile, tile), tile)
        start = start_ref[:, qs]
        queries = [q_t[h, :, qs] for h in hs]
        queries_n = [q_n[h, qs, :] for h in hs]
        cots = [g_t[h, :, qs] for h in hs]
        cots_n = [g_n[h, qs, :] for h in hs]
        key_at = lax.broadcasted_iota(jnp.int32, (tile, tile), 0)
        query_at = lax.broadcasted_iota(jnp.int32, (tile, tile), 1)

        def score(j, tops, diagonal):
            first = pl.multiple_of(j * tile, tile)
            allowed = key_at >= (start - first)
            if diagonal:
                allowed = allowed & (key_at <= query_at)
            result = []
            for h in hs:
                s = dot32(k_n[h, pl.ds(first, tile), :], queries[h])
                s = jnp.where(allowed, s, NEGATIVE)
                probs[h, pl.ds(first, tile), :] = s
                result.append(jnp.maximum(tops[h], jnp.max(s, axis=0, keepdims=True)))
            return tuple(result)

        tops = tuple(jnp.full((1, tile), NEGATIVE, F32) for _ in hs)
        tops = lax.fori_loop(0, i, lambda j, c: score(j, c, False), tops)
        tops = score(i, tops, True)

        def mix(j, carry):
            sums, mixed = carry
            ks = pl.ds(pl.multiple_of(j * tile, tile), tile)
            new_sums, new_mixed = [], []
            for h in hs:
                p = jnp.exp(probs[h, ks, :] - tops[h])
                probs[h, ks, :] = p
                new_sums.append(sums[h] + jnp.sum(p, axis=0, keepdims=True))
                new_mixed.append(mixed[h] + dot32(v_t[h, :, ks], p.astype(BF)))
            return tuple(new_sums), tuple(new_mixed)

        zeros = tuple(jnp.zeros((1, tile), F32) for _ in hs)
        wide_zeros = tuple(jnp.zeros((HD, tile), F32) for _ in hs)
        sums, mixed = lax.fori_loop(0, i + 1, mix, (zeros, wide_zeros))
        inverse = [1.0 / sums[h] for h in hs]
        mixed = [mixed[h] * inverse[h] for h in hs]
        delta = [jnp.sum(mixed[h] * cots[h].astype(F32), axis=0, keepdims=True) for h in hs]

        def back(j, carry):
            ks = pl.ds(pl.multiple_of(j * tile, tile), tile)
            result = []
            for h in hs:
                p = probs[h, ks, :] * inverse[h]
                dp = dot32(v_n[h, ks, :], cots[h])
                ds = (p * (dp - delta[h])).astype(BF)
                dv_acc[h, ks, :] += dot32(p.astype(BF), cots_n[h])
                dk_acc[h, ks, :] += dot32(ds, queries_n[h])
                result.append(carry[h] + dot32(k_t[h, :, ks], ds))
            return tuple(result)

        dq = lax.fori_loop(0, i + 1, back, wide_zeros)
        cos_t, sin_t = cos_ref[:, qs], sin_ref[:, qs]
        slot = jnp.bitwise_xor(i, z)
        for h in hs:
            low = h * HD
            out_ref[slot, :, low : low + HD] = turn(dq[h] * scale, cos_t, -sin_t).T.astype(BF)
            low = 3 * width + h * HD
            out_ref[slot, :, low : low + HD] = mixed[h].T.astype(BF)
        return 0

    lax.fori_loop(0, nz, one_tile, 0)
    for m in range(nz):
        place = pl.ds(pl.multiple_of(jnp.bitwise_xor(z, m) * length, length), length)
        cos_t, sin_t = cos_ref[:, place], sin_ref[:, place]
        for h in hs:
            low = width + h * HD
            x = turn(dk_acc[h, place, :].T, cos_t, -sin_t).T
            out_ref[m, :, low : low + HD] = x.astype(BF)
            low = 2 * width + h * HD
            out_ref[m, :, low : low + HD] = dv_acc[h, place, :].astype(BF)


def attention(z, pieces, grads, cos_t, sin_t, start):
    nz = len(pieces)
    length, width = grads[0].shape
    heads = width // HD
    total = nz * length

    def body(z_ref, *refs):
        attention_kernel(
            nz, heads, length, z_ref, refs[:nz], refs[nz : 2 * nz], *refs[2 * nz :]
        )

    vmem = pl.BlockSpec(memory_space=pltpu.VMEM)
    return pl.pallas_call(
        body,
        out_shape=jax.ShapeDtypeStruct((nz, length, 4 * width), BF),
        in_specs=[pl.BlockSpec(memory_space=pltpu.SMEM)] + [vmem] * (2 * nz + 3),
        out_specs=vmem,
        scratch_shapes=[pltpu.VMEM((heads, HD, total), BF)] * 4
        + [pltpu.VMEM((heads, total, HD), BF)] * 4
        + [pltpu.VMEM((heads, total, length), F32)]
        + [pltpu.VMEM((heads, total, HD), F32)] * 2,
        compiler_params=pltpu.CompilerParams(vmem_limit_bytes=56 << 20),
        cost_estimate=pl.CostEstimate(
            flops=heads * total * total * HD * 2 * 6 * 2,
            bytes_accessed=8 * total * width * 2,
            transcendentals=heads * total * total,
        ),
        name="attention",
    )(z, *pieces, *grads, cos_t, sin_t, start)


def add_rows(target, one, two):
    rows = target.shape[0]

    @pl.loop(0, rows, step=16)
    def _(r):
        at = pl.ds(pl.multiple_of(r, 16), 16)
        target[at] = (one[at].astype(F32) + two[at].astype(F32)).astype(BF)


def chain_kernel(chunks, count, *refs):
    own, refs = refs[:count], refs[count:]
    outs, refs = refs[:count], refs[count:]
    landed, refs = refs[:count], refs[count:]
    crossed, refs = refs[:count], refs[count:]
    stage, refs = refs[:count], refs[count:]
    sems, stage_sem, keep_sem = refs
    n = len(chunks)
    x, z = lax.axis_index("dp"), lax.axis_index("blk")
    at_end = (z == 0) | (z == 3)
    inner = jnp.where(z == 0, 1, 2)
    outer = jnp.where(z == 1, 0, 3)

    def send(kind, c, src, dst, device):
        return pltpu.make_async_remote_copy(
            src, dst, sems.at[2 * kind, c], sems.at[2 * kind + 1, c],
            device_id=device, device_id_type=MESH,
        )

    def rows(ref, c):
        a, first, size = chunks[c]
        return ref[a].at[pl.ds(first, size)]

    def final(c, half):
        a, first, size = chunks[c]
        return outs[a].at[half, pl.ds(first, size)]

    def go_in(c):
        return send(0, c, rows(own, c), rows(landed, c), {"blk": inner})

    def go_mid(c):
        return send(1, c, rows(landed, c), rows(crossed, c), {"blk": 3 - z})

    def go_out(c):
        return send(2, c, rows(crossed, c), final(c, x), {"blk": outer})

    def go_x_end(c):
        return send(3, c, final(c, x), final(c, x), {"dp": 1 - x})

    def go_x_mid(c):
        return send(3, c, rows(crossed, c), final(c, x), {"dp": 1 - x})

    def arrive_x(c):
        return send(3, c, final(c, 1 - x), final(c, 1 - x), {"dp": 1 - x})

    def arrive_out(c):
        return send(2, c, final(c, x), final(c, x), {"blk": inner})

    def load(c):
        a, first, size = chunks[c]
        return pltpu.make_async_copy(
            own[a].at[pl.ds(first, size)], stage[a].at[c % 3], stage_sem.at[c % 3]
        )

    def keep(c):
        return pltpu.make_async_copy(rows(crossed, c), final(c, x), keep_sem.at[c])

    barrier = pltpu.get_barrier_semaphore()
    pl.semaphore_signal(barrier, inc=1, device_id={"dp": 1 - x}, device_id_type=MESH)

    @pl.when(at_end)
    def _():
        pl.semaphore_signal(barrier, inc=1, device_id={"blk": inner}, device_id_type=MESH)
        pl.semaphore_wait(barrier, 2)
        lag = 4
        for c in range(n + lag):
            if c < n:
                if c >= 2:
                    go_in(c - 2).wait_send()
                go_in(c).start()
            if c >= lag:
                d = c - lag
                arrive_out(d).wait_recv()
                if d >= 2:
                    go_x_end(d - 2).wait_send()
                go_x_end(d).start()
        for c in range(n - 2, n):
            go_in(c).wait_send()
            go_x_end(c).wait_send()
        for c in range(n):
            arrive_x(c).wait_recv()

    @pl.when(jnp.logical_not(at_end))
    def _():
        pl.semaphore_signal(barrier, inc=1, device_id={"blk": outer}, device_id_type=MESH)
        pl.semaphore_signal(barrier, inc=1, device_id={"blk": 3 - z}, device_id_type=MESH)
        pl.semaphore_wait(barrier, 3)
        lag = 2
        for c in range(min(2, n)):
            load(c).start()
        for c in range(n + lag):
            if c < n:
                if c + 2 < n:
                    load(c + 2).start()
                load(c).wait()
                go_in(c).wait_recv()
                add_rows(rows(landed, c), rows(landed, c), stage[chunks[c][0]].at[c % 3])
                go_mid(c).start()
            if c >= lag:
                d = c - lag
                go_mid(d).wait_recv()
                add_rows(rows(crossed, d), rows(crossed, d), rows(landed, d))
                go_out(d).start()
                go_x_mid(d).start()
                keep(d).start()
        for c in range(n):
            go_mid(c).wait_send()
            go_out(c).wait_send()
            go_x_mid(c).wait_send()
            keep(c).wait()
        for c in range(n):
            arrive_x(c).wait_recv()


def chain(arrays, collective_id, chunk_bytes=1 << 19):
    chunks, stages = [], []
    for a, array in enumerate(arrays):
        rows, columns = array.shape
        size = min(rows, 1 << (chunk_bytes // (2 * columns)).bit_length() - 1)
        stages.append(pltpu.VMEM((3, size, columns), BF))
        chunks += [(a, first, size) for first in range(0, rows, size)]
    count = len(arrays)
    hbm = pl.BlockSpec(memory_space=pl.ANY)
    return pl.pallas_call(
        functools.partial(chain_kernel, chunks, count),
        out_shape=[jax.ShapeDtypeStruct((2,) + a.shape, BF) for a in arrays],
        in_specs=[hbm] * count,
        out_specs=[hbm] * count,
        scratch_shapes=[pltpu.VMEM(a.shape, BF) for a in arrays] * 2
        + stages
        + [
            pltpu.SemaphoreType.DMA((8, len(chunks))),
            pltpu.SemaphoreType.DMA((3,)),
            pltpu.SemaphoreType.DMA((len(chunks),)),
        ],
        compiler_params=pltpu.CompilerParams(
            collective_id=collective_id, has_side_effects=True, vmem_limit_bytes=56 << 20
        ),
        cost_estimate=pl.CostEstimate(
            flops=0, bytes_accessed=sum(a.size for a in arrays) * 60, transcendentals=0
        ),
        name="weight_sums",
    )(*arrays)


def place_blocks(blocks, order, count):
    width = blocks[0].shape[-1]
    out = jnp.zeros(blocks[0].shape[:-1] + (count * width,), blocks[0].dtype)
    for block, at in zip(blocks, order):
        out = lax.dynamic_update_slice_in_dim(out, block, at * width, out.ndim - 1)
    return out


def gather_all(part, nt):
    rows, tokens, width = part.shape
    x, t = lax.axis_index("dp"), lax.axis_index("tensor")
    if nt != 4:
        whole = lax.all_gather(part, "tensor", axis=2, tiled=True)
        return lax.all_gather(whole, "dp", axis=0, tiled=True)
    over_x = swap(part, "dp", 2, 1)
    over_y = swap(part, "tensor", 4, 2)
    half = tokens // 2
    corner = jnp.concatenate(
        [swap(over_y[:, :half], "dp", 2, 1), swap(over_x[:, half:], "tensor", 4, 2)], axis=1
    )
    mine = [(part, 0, 0), (over_x, 1, 0), (over_y, 0, 2), (corner, 1, 2)]
    blocks = mine + [(swap(b, "tensor", 4, 1), dx, dt + 1) for b, dx, dt in mine]
    out = jnp.zeros((2 * rows, tokens, nt * width), part.dtype)
    for block, dx, dt in blocks:
        at = (jnp.bitwise_xor(x, dx) * rows, 0, jnp.bitwise_xor(t, dt) * width)
        out = lax.dynamic_update_slice(out, block, at)
    return out


def scatter_sum(make, rows, tokens, width, nt):
    x, t = lax.axis_index("dp"), lax.axis_index("tensor")
    if nt != 4:
        whole = make(None).astype(BF)
        whole = lax.psum_scatter(whole, "dp", scatter_dimension=0, tiled=True)
        return lax.psum_scatter(whole, "tensor", scatter_dimension=2, tiled=True).astype(F32)
    core = t % 2
    other = swap(make(1 - core).astype(BF), "tensor", 4, 1)
    both = (make(core) + other.astype(F32)).astype(BF).reshape(2 * rows, tokens, 2, width)
    y = t // 2
    there = lax.dynamic_index_in_dim(both, 1 - y, 2, False)
    here = lax.dynamic_index_in_dim(both, y, 2, False)
    four = (here.astype(F32) + swap(there, "tensor", 4, 2).astype(F32)).astype(BF)
    away = lax.dynamic_slice_in_dim(four, (1 - x) * rows, rows, 0)
    near = lax.dynamic_slice_in_dim(four, x * rows, rows, 0)
    return near.astype(F32) + swap(away, "dp", 2, 1).astype(F32)


def core_columns(weight, nt, core):
    k, features = weight.shape
    cut = weight.reshape(k, 2, 2, features // 4)
    return lax.dynamic_index_in_dim(cut, core, 2, False).reshape(k, features // 2)


def butterfly(value, axes):
    for axis, size in axes:
        mask = 1
        while mask < size:
            value = value + swap(value, axis, size, mask)
            mask *= 2
    return value


def local(
    nx, nz, nt, block_input, segment_ids, layer_norm_gain, layer_norm_bias, qkv_weight, qkv_bias, out_weight, out_bias,
    up_weight, up_bias, down_weight, down_bias, grad_output,
):
    rows, tokens, width = block_input.shape
    all_rows = nx * rows
    features = nt * width
    many = all_rows * tokens
    x, z, t = lax.axis_index("dp"), lax.axis_index("blk"), lax.axis_index("tensor")
    att = qkv_weight.shape[2] // nx
    lanes = min(128, att)
    groups = att // lanes
    ff = up_weight.shape[1] // nx

    qkv_half = lax.dynamic_slice_in_dim(qkv_weight, x * att, att, 2)
    qkv_half_bias = lax.dynamic_slice_in_dim(qkv_bias, x * att, att, 1)
    out_half = lax.dynamic_slice_in_dim(out_weight, x * att, att, 0)
    up_half = lax.dynamic_slice_in_dim(up_weight, x * ff, ff, 1)
    up_half_bias = lax.dynamic_slice_in_dim(up_bias, x * ff, ff, 0)
    down_half = lax.dynamic_slice_in_dim(down_weight, x * ff, ff, 0)

    segments = lax.ppermute(segment_ids, "dp", [(0, 1), (1, 0)])
    segments = jnp.where(z // rows == x, segment_ids, segments)
    segments = lax.dynamic_slice_in_dim(segments, z % rows, 1, 0)
    length = segments.shape[1]
    places = jnp.arange(length, dtype=jnp.int32)[None]
    changed = jnp.concatenate(
        [jnp.ones((1, 1), dtype=bool), segments[:, 1:] != segments[:, :-1]], axis=1
    )
    start = lax.cummax(jnp.where(changed, places, 0), axis=1)
    half_rot = ROT // 2
    frequency = jnp.exp(jnp.arange(half_rot).astype(F32) * (-2.0 / ROT) * ROPE_LOG_BASE)
    angles = frequency[:, None] * (places - start).astype(F32)
    cos_t, sin_t = jnp.cos(angles), jnp.sin(angles)

    full_input = gather_all(block_input, nt)
    full_grad = gather_all(grad_output, nt)
    wide = full_input.astype(F32)
    mean = jnp.mean(wide, axis=-1, keepdims=True)
    centered = wide - mean
    variance = jnp.mean(centered * centered, axis=-1, keepdims=True)
    inverse_stddev = lax.rsqrt(variance + EPSILON)
    normed = (centered * inverse_stddev * layer_norm_gain + layer_norm_bias).astype(BF)
    normed = normed.reshape(many, features)
    cotangent = full_grad.reshape(many, features)

    z_at = z.astype(jnp.int32).reshape(1)
    results = []
    d_attended = dot32(cotangent, out_half.T).astype(BF).reshape(all_rows, tokens, att)
    for p in range(groups):
        w = qkv_half[:, :, p * lanes : (p + 1) * lanes].reshape(features, 3 * lanes)
        b = qkv_half_bias[:, p * lanes : (p + 1) * lanes].reshape(3 * lanes)
        qkv = (dot32(normed, w) + b).astype(BF).reshape(all_rows, tokens, 3 * lanes)
        d_att = d_attended[:, :, p * lanes : (p + 1) * lanes]

        def row(array, m):
            return lax.dynamic_index_in_dim(array, jnp.bitwise_xor(z, m), 0, False)

        pieces = [row(qkv, 0)] + [swap(row(qkv, m), "blk", nz, m) for m in range(1, nz)]
        grads = [row(d_att, 0)] + [swap(row(d_att, m), "blk", nz, m) for m in range(1, nz)]
        results.append(attention(z_at, pieces, grads, cos_t, sin_t, start))

    hidden = dot32(normed, up_half) + up_half_bias
    inner = math.sqrt(2.0 / math.pi) * (hidden + 0.044715 * hidden * hidden * hidden)
    tanh = jnp.tanh(inner)
    active = (0.5 * hidden * (1.0 + tanh)).astype(BF)
    slope = 0.5 * (1.0 + tanh) + 0.5 * hidden * (1.0 - tanh * tanh) * math.sqrt(2.0 / math.pi) * (
        1.0 + 3 * 0.044715 * hidden * hidden
    )
    d_hidden = (dot32(cotangent, down_half.T) * slope).astype(BF)
    down_part = dot32(active.T, cotangent).astype(BF)
    up_part = dot32(normed.T, d_hidden).astype(BF)
    up_bias_part = jnp.sum(d_hidden.astype(F32), axis=0)

    down_sum, up_sum = chain([down_part, up_part], 0)

    stacked = []
    for result in results:
        home = jnp.zeros((all_rows, tokens, 4 * lanes), BF)
        for m in range(nz):
            piece = result[m] if m == 0 else swap(result[m], "blk", nz, m)
            home = lax.dynamic_update_slice(home, piece[None], (jnp.bitwise_xor(z, m), 0, 0))
        stacked.append(home.reshape(many, 4 * lanes))
    d_qkv = [s[:, : 3 * lanes] for s in stacked]
    attended = [s[:, 3 * lanes :] for s in stacked]
    qkv_parts = [dot32(normed.T, d).astype(BF) for d in d_qkv]
    out_parts = [dot32(a.T, cotangent).astype(BF) for a in attended]
    qkv_bias_part = jnp.stack(
        [jnp.sum(d.astype(F32), axis=0).reshape(3, lanes) for d in d_qkv], axis=1
    ).reshape(3, att)

    def branch_share(core):
        def cols(weight):
            return weight if core is None else core_columns(weight, nt, core)

        total = dot32(active, cols(down_half))
        for p, a in enumerate(attended):
            total = total + dot32(a, cols(out_half[p * lanes : (p + 1) * lanes]))
        return total.reshape(all_rows, tokens, -1)

    def normed_share(core):
        def cols(weight):
            return weight if core is None else core_columns(weight, nt, core)

        total = dot32(d_hidden, cols(up_half.T))
        for p, d in enumerate(d_qkv):
            w = qkv_half[:, :, p * lanes : (p + 1) * lanes].reshape(features, 3 * lanes)
            total = total + dot32(d, cols(w.T))
        return total.reshape(all_rows, tokens, -1)

    branch = scatter_sum(branch_share, rows, tokens, width, nt)
    d_normed = scatter_sum(normed_share, rows, tokens, width, nt)

    sums = chain(out_parts + qkv_parts, 1)
    out_sums, qkv_sums = sums[:groups], sums[groups:]

    block_output = (block_input.astype(F32) + (branch + out_bias + down_bias)).astype(BF)

    gain = lax.dynamic_slice_in_dim(layer_norm_gain, t * width, width, 0)
    own_mean = lax.dynamic_slice_in_dim(mean, x * rows, rows, 0)
    own_inverse = lax.dynamic_slice_in_dim(inverse_stddev, x * rows, rows, 0)
    xhat = (block_input.astype(F32) - own_mean) * own_inverse
    scaled = d_normed * gain
    moments = jnp.stack([jnp.sum(scaled, axis=-1), jnp.sum(scaled * xhat, axis=-1)])
    moments = butterfly(moments, [("tensor", nt)]) / features
    first, second = moments[0][..., None], moments[1][..., None]
    input_grad = (
        grad_output.astype(F32) + own_inverse * (scaled - first - xhat * second)
    ).astype(BF)

    def spread(part, whole):
        shape = part.shape[:-1] + (whole,)
        at = (0,) * (part.ndim - 1) + (x * part.shape[-1],)
        return lax.dynamic_update_slice(jnp.zeros(shape, F32), part, at)

    small = [
        jnp.sum(d_normed * xhat, axis=(0, 1)),
        jnp.sum(d_normed, axis=(0, 1)),
        jnp.sum(grad_output.astype(F32), axis=(0, 1)),
        spread(up_bias_part, nx * ff),
        spread(qkv_bias_part, nx * att).reshape(-1),
    ]
    packed = butterfly(jnp.concatenate(small), [("dp", nx), ("blk", nz)])
    gain_grad, shift_grad, bias_grad = (packed[i * width : (i + 1) * width] for i in range(3))
    up_bias_grad = packed[3 * width : 3 * width + nx * ff]
    qkv_bias_grad = packed[3 * width + nx * ff :].reshape(3, nx * att)

    down_grad = down_sum.reshape(nx * ff, features).astype(F32)
    up_grad = jnp.swapaxes(up_sum, 0, 1).reshape(features, nx * ff).astype(F32)
    out_grad = jnp.stack(out_sums, axis=1).reshape(nx * att, features).astype(F32)
    qkv_grad = jnp.stack([s.reshape(nx, features, 3, lanes) for s in qkv_sums], axis=1)
    qkv_grad = jnp.transpose(qkv_grad, (2, 3, 0, 1, 4)).reshape(features, 3, nx * att).astype(F32)
    return (
        block_output, input_grad, gain_grad, shift_grad, qkv_grad, qkv_bias_grad, out_grad, bias_grad, up_grad,
        up_bias_grad, down_grad, bias_grad,
    )


def solution(mesh):
    in_specs = (
        P("dp", "blk", "tensor"), P("dp", None), P(), P(), P(None, None, "tensor"), P(None, "tensor"), P("tensor", None),
        P("tensor"), P(None, "tensor"), P("tensor"), P("tensor", None), P("tensor"), P("dp", "blk", "tensor"),
    )
    out_specs = (
        P("dp", "blk", "tensor"), P("dp", "blk", "tensor"), P("tensor"), P("tensor"), P(None, None, "tensor"),
        P(None, "tensor"), P("tensor", None), P("tensor"), P(None, "tensor"), P("tensor"), P("tensor", None), P("tensor"),
    )
    body = functools.partial(local, mesh.shape["dp"], mesh.shape["blk"], mesh.shape["tensor"])
    return jax.shard_map(body, mesh=mesh, in_specs=in_specs, out_specs=out_specs, check_vma=False)
```

```python
import functools
import math

import jax
import jax.numpy as jnp
from jax import lax
from jax.experimental import pallas as pl
from jax.experimental.pallas import tpu as pltpu
from jax.sharding import PartitionSpec as P

HD = 64
ROT = 32
EPSILON = 1e-05
ROPE_LOG_BASE = math.log(10000.0)
NEGATIVE = -1e30
F32 = jnp.float32
BF = jnp.bfloat16
MESH = pl.DeviceIdType.MESH
dot32 = functools.partial(jnp.dot, preferred_element_type=F32)


def swap(value, axis, size, mask):
    return lax.ppermute(value, axis, [(i, i ^ mask) for i in range(size)])


def flip(index, mask):
    if mask == 0:
        return index
    if mask == 1:
        return index + 1 - 2 * (index % 2)
    if mask == 2:
        return (index + 2) % 4
    return 3 - index


def front_kernel(
    gather, split, rows, tokens, x_own, g_own, gain_ref, shift_ref, wq_ref, bq_ref, wo_ref, wu_ref, bu_ref, wd_ref,
    normed_o, g_o, land_o, stats_o, down_o, up_o, branch_o, dnorm_o, ubias_o,
    xin, gin, vq, vo, vu, vd, pay, act, slope, stage, gather_sems, land_sems, load_sems, keep_sems, stage_sems,
):
    x, z, t = lax.axis_index("dp"), lax.axis_index("blk"), lax.axis_index("tensor")
    many, features = xin.shape
    half = rows * tokens
    width = features // 4
    att = vq.shape[2]
    ff = vu.shape[1]
    nz = pay.shape[0]
    wide = min(512, ff)

    def remote(src, dst, sems, device):
        return pltpu.make_async_remote_copy(
            src, dst, sems[0], sems[1], device_id=device, device_id_type=MESH
        )

    peers = {"x": {"dp": 1 - x}, "y": {"tensor": flip(t, 2)}, "c": {"tensor": flip(t, 1)}}
    barrier = pltpu.get_barrier_semaphore()
    greet = [{"blk": flip(z, m)} for m in range(1, nz)] + (list(peers.values()) if gather else [])
    for device in greet:
        pl.semaphore_signal(barrier, inc=1, device_id=device, device_id_type=MESH)

    loads = [
        pltpu.make_async_copy(
            wq_ref.at[:, :, pl.ds(pl.multiple_of(x * att, 128), att)] if split else wq_ref, vq, load_sems.at[0]
        ),
        pltpu.make_async_copy(
            wu_ref.at[:, pl.ds(pl.multiple_of(x * ff, 128), ff)] if split else wu_ref, vu, load_sems.at[1]
        ),
        pltpu.make_async_copy(wd_ref.at[pl.ds(x * ff, ff)] if split else wd_ref, vd, load_sems.at[2]),
        pltpu.make_async_copy(wo_ref.at[pl.ds(x * att, att)] if split else wo_ref, vo, load_sems.at[3]),
    ]
    if not gather:
        both = [
            pltpu.make_async_copy(x_own, xin, load_sems.at[4]),
            pltpu.make_async_copy(g_own, gin, load_sems.at[5]),
        ]
    else:
        both = [
            pltpu.make_async_copy(
                own,
                buf.at[pl.ds(x * half, half), pl.ds(pl.multiple_of(t * width, 128), width)],
                load_sems.at[4 + i],
            )
            for i, (own, buf) in enumerate([(x_own, xin), (g_own, gin)])
        ]
    both[0].start()
    both[1].start()
    pl.semaphore_wait(barrier, len(greet))

    class Gather:
        def __init__(self, which, own, buf):
            self.which, self.own, self.buf, self.names = which, own, buf, []

        def at(self, dx, dt, r):
            return self.buf.at[
                pl.ds(pl.multiple_of((1 - x if dx else x) * half + r * tokens, tokens), tokens),
                pl.ds(pl.multiple_of(flip(t, dt) * width, 128), width),
            ]

        plan = {
            "x": (0, 0, "x", 1, 0), "y": (0, 0, "y", 0, 2), "c": (0, 0, "c", 0, 1),
            "ex": (1, 0, "c", 1, 1), "ey": (0, 2, "c", 0, 3), "ed": (1, 2, "c", 1, 3),
        }

        def sems(self, kind, r):
            k = 2 * ("x", "y", "c", "d", "ex", "ey", "ed").index(kind) + r
            return gather_sems.at[self.which, 0, k], gather_sems.at[self.which, 1, k]

        def copy(self, kind, r):
            if kind == "d":
                dx, dt, to = (1, 0, "y") if r == 0 else (0, 2, "x")
            else:
                dx, dt, to = self.plan[kind][:3]
            src = dst = self.at(dx, dt, r)
            if kind in "xyc":
                src = self.own.at[pl.ds(r * tokens, tokens)]
            return remote(src, dst, self.sems(kind, r), peers[to])

        def start(self, kind, r):
            self.names.append((kind, r))
            self.copy(kind, r).start()

        def wait(self, kind, r):
            if kind == "d":
                dx, dt, to = 1, 2, "y"
            else:
                to, dx, dt = self.plan[kind][2:]
            ref = self.at(dx, dt, r)
            remote(ref, ref, self.sems(kind, r), peers[to]).wait_recv()

        def first(self):
            for kind, r in (("x", 0), ("y", 1), ("x", 1), ("y", 0), ("c", 0), ("c", 1)):
                self.start(kind, r)

        def second(self):
            self.wait("x", 0)
            self.start("d", 0)
            self.start("ex", 0)
            self.wait("y", 1)
            self.start("d", 1)
            self.start("ey", 1)

        def third(self):
            self.wait("x", 1)
            self.start("ex", 1)
            self.wait("y", 0)
            self.start("ey", 0)

        def fourth(self):
            self.wait("d", 0)
            self.start("ed", 0)
            self.wait("d", 1)
            self.start("ed", 1)

        def last(self):
            for kind in ("c", "ex", "ey", "ed"):
                for r in range(2):
                    self.wait(kind, r)

        def drain(self):
            for kind, r in self.names:
                self.copy(kind, r).wait_send()

    ins, cots = Gather(0, x_own, xin), Gather(1, g_own, gin)
    if gather:
        ins.first()
    for load in loads:
        load.start()
    if gather:
        ins.second()
        ins.third()
        cots.first()
        ins.fourth()
    both[0].wait()
    if gather:
        ins.last()
        ins.drain()

    @pl.loop(0, many // 128)
    def _(i):
        at = pl.ds(pl.multiple_of(i * 128, 128), 128)
        v = xin[at, :].astype(F32)
        mean = jnp.sum(v, axis=-1, keepdims=True) * (1.0 / features)
        v = v - mean
        inverse = lax.rsqrt(jnp.sum(v * v, axis=-1, keepdims=True) * (1.0 / features) + EPSILON)
        xin[at, :] = (v * inverse * gain_ref[...] + shift_ref[...]).astype(BF)
        lane = lax.broadcasted_iota(jnp.int32, (128, 128), 1)
        stats_o[at, :] = jnp.where(lane < 64, mean, inverse)

    keep_normed = pltpu.make_async_copy(xin, normed_o, keep_sems.at[0])
    keep_normed.start()
    if gather:
        cots.second()

    def place(position):
        return pl.ds(pl.multiple_of(position * tokens, tokens), tokens)

    def send(kind, m):
        parts = pl.ds(0, 3) if kind == 0 else pl.ds(3, 1)
        src, dst = pay.at[flip(z, m), parts], land_o.at[parts, place(z)]
        if m == 0:
            return pltpu.make_async_copy(src, dst, keep_sems.at[2 + kind])
        sems = land_sems.at[0, kind, m], land_sems.at[1, kind, m]
        return remote(src, dst, sems, {"blk": flip(z, m)})

    def landed(kind, m):
        parts = pl.ds(0, 3) if kind == 0 else pl.ds(3, 1)
        ref = land_o.at[parts, place(flip(z, m))]
        sems = land_sems.at[0, kind, m], land_sems.at[1, kind, m]
        return remote(ref, ref, sems, {"blk": flip(z, m)})

    order = [m for m in (2, 3, 1, 0) if m < nz]
    loads[0].wait()
    for m in order:
        row = flip(z, m)

        @pl.loop(0, 3)
        def _(part):
            value = dot32(xin[place(row), :], vq[part]) + bq_ref[part]
            pay[row, part] = value.astype(BF)

        send(0, m).start()
    if gather:
        cots.third()

    loads[1].wait()

    @pl.loop(0, many // tokens)
    def _(i):
        at = place(i)

        @pl.loop(0, ff // wide)
        def _(j):
            columns = pl.ds(pl.multiple_of(j * wide, wide), wide)
            h = dot32(xin[at, :], vu[:, columns]) + bu_ref[:, columns]
            c = math.sqrt(2.0 / math.pi)
            square = h * h
            tanh = jnp.tanh(c * h * (1.0 + 0.044715 * square))
            one = 0.5 * (1.0 + tanh)
            act[at, columns] = (h * one).astype(BF)
            d = one + 0.5 * h * (1.0 - tanh * tanh) * (c * (1.0 + 3 * 0.044715 * square))
            slope[at, columns] = d.astype(BF)

    if gather:
        cots.fourth()
    both[1].wait()
    if gather:
        cots.last()
    keep_g = pltpu.make_async_copy(gin, g_o, keep_sems.at[1])
    keep_g.start()

    loads[3].wait()
    nt_dims = (((1,), (1,)), ((), ()))
    tn_dims = (((0,), (0,)), ((), ()))
    general = functools.partial(lax.dot_general, preferred_element_type=F32)
    for m in order:
        row = flip(z, m)
        pay[row, 3] = general(gin[place(row), :], vo[...], nt_dims).astype(BF)
        send(1, m).start()

    loads[2].wait()
    ubias_o[...] = jnp.zeros_like(ubias_o)

    @pl.loop(0, many // tokens)
    def _(i):
        at = place(i)

        @pl.loop(0, ff // wide)
        def _(j):
            columns = pl.ds(pl.multiple_of(j * wide, wide), wide)
            d = general(gin[at, :], vd[columns, :], nt_dims) * slope[at, columns].astype(F32)
            d = d.astype(BF)
            slope[at, columns] = d
            ubias_o[0:1, columns] += jnp.sum(d.astype(F32), axis=0, keepdims=True)

    def through(steps, rows_of, columns_of, make, out):
        def copy(i):
            return pltpu.make_async_copy(
                stage.at[i % 2, pl.ds(0, rows_of), pl.ds(0, columns_of)],
                out.at[pl.ds(pl.multiple_of(i * rows_of, rows_of), rows_of)],
                stage_sems.at[i % 2],
            )

        @pl.loop(0, steps)
        def _(i):
            @pl.when(i >= 2)
            def _():
                copy(i - 2).wait()

            make(i, stage.at[i % 2, pl.ds(0, rows_of), pl.ds(0, columns_of)])
            copy(i).start()

        for i in range(max(0, steps - 2), steps):
            copy(i).wait()

    def down_tile(i, target):
        f = pl.ds(pl.multiple_of(i * 256, 256), 256)
        for j in range(0, features, 1024):
            target[:, j : j + 1024] = general(act[:, f], gin[:, j : j + 1024], tn_dims).astype(BF)

    through(ff // 256, 256, features, down_tile, down_o)

    def up_tile(i, target):
        f = pl.ds(pl.multiple_of(i * 256, 256), 256)
        target[...] = general(xin[:, f], slope[...], tn_dims).astype(BF)

    through(features // 256, 256, ff, up_tile, up_o)

    def branch_tile(i, target):
        @pl.loop(0, features // 512)
        def _(j):
            columns = pl.ds(pl.multiple_of(j * 512, 512), 512)
            target[:, columns] = dot32(act[place(i), :], vd[:, columns]).astype(BF)

    through(many // tokens, tokens, features, branch_tile, branch_o)

    def dnorm_tile(i, target):
        @pl.loop(0, features // 512)
        def _(j):
            columns = pl.ds(pl.multiple_of(j * 512, 512), 512)
            target[:, columns] = general(slope[place(i), :], vu[columns, :], nt_dims).astype(BF)

    through(many // tokens, tokens, features, dnorm_tile, dnorm_o)

    keep_normed.wait()
    keep_g.wait()
    for kind in range(2):
        for m in range(nz):
            if m == 0:
                send(kind, 0).wait()
            else:
                send(kind, m).wait_send()
                landed(kind, m).wait_recv()
    if gather:
        cots.drain()


def front(gather, split, rows, tokens, nz, many, features, att, ff, operands):
    hbm = pl.BlockSpec(memory_space=pl.ANY)
    vmem = pl.BlockSpec(memory_space=pltpu.VMEM)
    return pl.pallas_call(
        functools.partial(front_kernel, gather, split, rows, tokens),
        out_shape=[
            jax.ShapeDtypeStruct((many, features), BF),
            jax.ShapeDtypeStruct((many, features), BF),
            jax.ShapeDtypeStruct((4, nz * tokens, att), BF),
            jax.ShapeDtypeStruct((many, 128), F32),
            jax.ShapeDtypeStruct((ff, features), BF),
            jax.ShapeDtypeStruct((features, ff), BF),
            jax.ShapeDtypeStruct((many, features), BF),
            jax.ShapeDtypeStruct((many, features), BF),
            jax.ShapeDtypeStruct((8, ff), F32),
        ],
        in_specs=[hbm, hbm, vmem, vmem, hbm, vmem, hbm, hbm, vmem, hbm],
        out_specs=[hbm, hbm, hbm, vmem, hbm, hbm, hbm, hbm, vmem],
        scratch_shapes=[
            pltpu.VMEM((many, features), BF),
            pltpu.VMEM((many, features), BF),
            pltpu.VMEM((3, features, att), BF),
            pltpu.VMEM((att, features), BF),
            pltpu.VMEM((features, ff), BF),
            pltpu.VMEM((ff, features), BF),
            pltpu.VMEM((nz, 4, tokens, att), BF),
            pltpu.VMEM((many, ff), BF),
            pltpu.VMEM((many, ff), BF),
            pltpu.VMEM((2, tokens, features), BF),
            pltpu.SemaphoreType.DMA((2, 2, 14)),
            pltpu.SemaphoreType.DMA((2, 2, 4)),
            pltpu.SemaphoreType.DMA((6,)),
            pltpu.SemaphoreType.DMA((4,)),
            pltpu.SemaphoreType.DMA((2,)),
        ],
        compiler_params=pltpu.CompilerParams(
            collective_id=2, has_side_effects=True, vmem_limit_bytes=60 << 20
        ),
        cost_estimate=pl.CostEstimate(
            flops=2 * many * features * (6 * ff + 4 * att), bytes_accessed=100 << 20, transcendentals=0
        ),
        name="front",
    )(*operands)


MIDDLE_CHUNK = 1 << 19
TAIL_CHUNK = 1 << 18


def add_rows(target, one, two):
    @pl.loop(0, target.shape[0], step=16)
    def _(r):
        at = pl.ds(pl.multiple_of(r, 16), 16)
        target[at] = (one[at].astype(F32) + two[at].astype(F32)).astype(BF)


def chain_chunks(shapes, chunk_bytes):
    chunks, sizes = [], []
    for a, (rows, columns) in enumerate(shapes):
        size = math.gcd(rows, 1 << (chunk_bytes // (2 * columns)).bit_length() - 1)
        sizes.append(size)
        chunks += [(a, first, size) for first in range(0, rows, size)]
    return chunks, sizes


class Chain:
    def __init__(self, shapes, own, outs, landed, crossed, stage, sems, stage_sem, keep_sem):
        self.chunks = chain_chunks(shapes, MIDDLE_CHUNK if stage else TAIL_CHUNK)[0]
        self.own, self.outs, self.landed, self.crossed = own, outs, landed, crossed
        self.stage, self.sems, self.stage_sem, self.keep_sem = stage, sems, stage_sem, keep_sem
        self.n = len(self.chunks)
        self.x, self.z = lax.axis_index("dp"), lax.axis_index("blk")
        self.at_end = (self.z == 0) | (self.z == 3)
        self.inner = jnp.where(self.z == 0, 1, 2)
        self.outer = jnp.where(self.z == 1, 0, 3)

    @staticmethod
    def scratch(shapes, staged, chunk):
        chunks, sizes = chain_chunks(shapes, chunk)
        full = [pltpu.VMEM(s, BF) for s in shapes]
        stages = [pltpu.VMEM((3, n, s[1]), BF) for n, s in zip(sizes, shapes)] if staged else []
        return full * 2 + stages + [
            pltpu.SemaphoreType.DMA((8, len(chunks))),
            pltpu.SemaphoreType.DMA((3,)),
            pltpu.SemaphoreType.DMA((len(chunks),)),
        ]

    def send(self, kind, c, src, dst, device):
        return pltpu.make_async_remote_copy(
            src, dst, self.sems.at[2 * kind, c], self.sems.at[2 * kind + 1, c],
            device_id=device, device_id_type=MESH,
        )

    def rows(self, refs, c):
        a, first, size = self.chunks[c]
        return refs[a].at[pl.ds(first, size)]

    def final(self, c, half):
        a, first, size = self.chunks[c]
        return self.outs[a].at[half, pl.ds(first, size)]

    def go_in(self, c):
        return self.send(0, c, self.rows(self.own, c), self.rows(self.landed, c), {"blk": self.inner})

    def go_mid(self, c):
        return self.send(1, c, self.rows(self.landed, c), self.rows(self.crossed, c), {"blk": 3 - self.z})

    def go_out(self, c):
        return self.send(2, c, self.rows(self.crossed, c), self.final(c, self.x), {"blk": self.outer})

    def arrive_out(self, c):
        return self.send(2, c, self.final(c, self.x), self.final(c, self.x), {"blk": self.inner})

    def go_x(self, c, end):
        src = self.final(c, self.x) if end else self.rows(self.crossed, c)
        return self.send(3, c, src, self.final(c, self.x), {"dp": 1 - self.x})

    def arrive_x(self, c):
        ref = self.final(c, 1 - self.x)
        return self.send(3, c, ref, ref, {"dp": 1 - self.x})

    def load(self, c):
        a = self.chunks[c][0]
        return pltpu.make_async_copy(
            self.rows(self.own, c), self.stage[a].at[c % 3], self.stage_sem.at[c % 3]
        )

    def keep(self, c):
        return pltpu.make_async_copy(
            self.rows(self.crossed, c), self.final(c, self.x), self.keep_sem.at[c]
        )

    END_LAG = 3
    MID_LAG = 1

    @property
    def steps(self):
        return self.n + self.END_LAG

    def begin(self):
        @pl.when(self.at_end)
        def _():
            for c in range(min(2, self.n)):
                self.go_in(c).start()

        if self.stage:

            @pl.when(jnp.logical_not(self.at_end))
            def _():
                for c in range(min(2, self.n)):
                    self.load(c).start()

    def step(self, c):
        @pl.when(self.at_end)
        def _():
            if c < self.n:
                self.go_in(c).wait_send()
                if c + 2 < self.n:
                    self.go_in(c + 2).start()
            d = c - self.END_LAG
            if 0 <= d < self.n:
                self.arrive_out(d).wait_recv()
                if d >= 2:
                    self.go_x(d - 2, True).wait_send()
                self.go_x(d, True).start()

        if c < self.n + self.MID_LAG:

            @pl.when(jnp.logical_not(self.at_end))
            def _():
                if c < self.n:
                    if self.stage:
                        if c + 2 < self.n:
                            self.load(c + 2).start()
                        self.load(c).wait()
                        mine = self.stage[self.chunks[c][0]].at[c % 3]
                    else:
                        mine = self.rows(self.own, c)
                    self.go_in(c).wait_recv()
                    add_rows(self.rows(self.landed, c), self.rows(self.landed, c), mine)
                    self.go_mid(c).start()
                d = c - self.MID_LAG
                if 0 <= d < self.n:
                    self.go_mid(d).wait_recv()
                    add_rows(self.rows(self.crossed, d), self.rows(self.crossed, d), self.rows(self.landed, d))
                    self.go_out(d).start()
                    self.go_x(d, False).start()
                    self.keep(d).start()

    def finish(self):
        @pl.when(self.at_end)
        def _():
            for c in range(max(0, self.n - 2), self.n):
                self.go_x(c, True).wait_send()

        @pl.when(jnp.logical_not(self.at_end))
        def _():
            for c in range(self.n):
                self.go_mid(c).wait_send()
                self.go_out(c).wait_send()
                self.go_x(c, False).wait_send()
                self.keep(c).wait()

        for c in range(self.n):
            self.arrive_x(c).wait_recv()


def greet(devices):
    barrier = pltpu.get_barrier_semaphore()
    for device in devices:
        pl.semaphore_signal(barrier, inc=1, device_id=device, device_id_type=MESH)
    pl.semaphore_wait(barrier, len(devices))


def chain_kernel(shapes, *refs):
    count = len(shapes)
    own, outs, landed, crossed, stage = (refs[i * count : (i + 1) * count] for i in range(5))
    x, z = lax.axis_index("dp"), lax.axis_index("blk")
    greet([{"dp": 1 - x}] + [{"blk": flip(z, m)} for m in (1, 2, 3)])
    work = Chain(shapes, own, outs, landed, crossed, stage, *refs[5 * count :])
    work.begin()
    for c in range(work.steps):
        work.step(c)
    work.finish()


def chain(arrays, collective_id):
    shapes = [a.shape for a in arrays]
    hbm = pl.BlockSpec(memory_space=pl.ANY)
    return pl.pallas_call(
        functools.partial(chain_kernel, shapes),
        out_shape=[jax.ShapeDtypeStruct((2,) + s, BF) for s in shapes],
        in_specs=[hbm] * len(arrays),
        out_specs=[hbm] * len(arrays),
        scratch_shapes=Chain.scratch(shapes, True, MIDDLE_CHUNK),
        compiler_params=pltpu.CompilerParams(
            collective_id=collective_id, has_side_effects=True, vmem_limit_bytes=60 << 20
        ),
        cost_estimate=pl.CostEstimate(
            flops=0, bytes_accessed=sum(a.size for a in arrays) * 60, transcendentals=0
        ),
        name="weight_sums",
    )(*arrays)


def turn(source, cos_t, sin_t):
    half = ROT // 2
    front_half, back_half = source[:half], source[half:ROT]
    return jnp.concatenate(
        [front_half * cos_t - back_half * sin_t, back_half * cos_t + front_half * sin_t, source[ROT:]], axis=0
    )


def attention_heads(
    first_head, heads, tile, land, cos_ref, sin_ref, start_ref, out, q_t, k_t, v_t, g_t, q_n, k_n, probs, dk_acc, dv_acc,
    between,
):
    total = land.shape[1]
    steps = total // tile
    scale = HD**-0.5
    hs = range(heads)

    def lanes(h):
        return slice((first_head + h) * HD, (first_head + h + 1) * HD)

    @pl.loop(0, steps)
    def _(i):
        place = pl.ds(pl.multiple_of(i * tile, tile), tile)
        cos_t, sin_t = cos_ref[:, place], sin_ref[:, place]
        for h in hs:
            x = turn(land[0, place, lanes(h)].astype(F32).T, cos_t, sin_t) * scale
            q_t[h, :, place] = x.astype(BF)
            q_n[h, place, :] = x.T.astype(BF)
            x = turn(land[1, place, lanes(h)].astype(F32).T, cos_t, sin_t)
            k_t[h, :, place] = x.astype(BF)
            k_n[h, place, :] = x.T.astype(BF)
            v_t[h, :, place] = land[2, place, lanes(h)].astype(F32).T.astype(BF)
            g_t[h, :, place] = land[3, place, lanes(h)].astype(F32).T.astype(BF)
            dk_acc[h, place, :] = jnp.zeros((tile, HD), F32)
            dv_acc[h, place, :] = jnp.zeros((tile, HD), F32)

    def one_tile(i):
        qs = pl.ds(pl.multiple_of(i * tile, tile), tile)
        start = start_ref[:, qs]
        queries = [q_t[h, :, qs] for h in hs]
        queries_n = [q_n[h, qs, :] for h in hs]
        cots = [g_t[h, :, qs] for h in hs]
        cots_n = [land[3, qs, lanes(h)] for h in hs]
        key_at = lax.broadcasted_iota(jnp.int32, (tile, tile), 0)
        query_at = lax.broadcasted_iota(jnp.int32, (tile, tile), 1)

        def score(j, tops, diagonal):
            first = pl.multiple_of(j * tile, tile)
            allowed = key_at >= (start - first)
            if diagonal:
                allowed = allowed & (key_at <= query_at)
            result = []
            for h in hs:
                s = dot32(k_n[h, pl.ds(first, tile), :], queries[h])
                s = jnp.where(allowed, s, NEGATIVE)
                probs[h, pl.ds(first, tile), :] = s
                result.append(jnp.maximum(tops[h], jnp.max(s, axis=0, keepdims=True)))
            return tuple(result)

        tops = tuple(jnp.full((1, tile), NEGATIVE, F32) for _ in hs)
        tops = lax.fori_loop(0, i, lambda j, c: score(j, c, False), tops)
        tops = score(i, tops, True)

        def mix(j, carry):
            sums, mixed = carry
            ks = pl.ds(pl.multiple_of(j * tile, tile), tile)
            new_sums, new_mixed = [], []
            for h in hs:
                p = jnp.exp(probs[h, ks, :] - tops[h])
                probs[h, ks, :] = p
                new_sums.append(sums[h] + jnp.sum(p, axis=0, keepdims=True))
                new_mixed.append(mixed[h] + dot32(v_t[h, :, ks], p.astype(BF)))
            return tuple(new_sums), tuple(new_mixed)

        zeros = tuple(jnp.zeros((1, tile), F32) for _ in hs)
        wide_zeros = tuple(jnp.zeros((HD, tile), F32) for _ in hs)
        sums, mixed = lax.fori_loop(0, i + 1, mix, (zeros, wide_zeros))
        inverse = [1.0 / sums[h] for h in hs]
        mixed = [mixed[h] * inverse[h] for h in hs]
        delta = [jnp.sum(mixed[h] * cots[h].astype(F32), axis=0, keepdims=True) for h in hs]

        def back(j, carry):
            ks = pl.ds(pl.multiple_of(j * tile, tile), tile)
            result = []
            for h in hs:
                p = probs[h, ks, :] * inverse[h]
                dp = dot32(land[2, ks, lanes(h)], cots[h])
                ds = (p * (dp - delta[h])).astype(BF)
                dv_acc[h, ks, :] += dot32(p.astype(BF), cots_n[h])
                dk_acc[h, ks, :] += dot32(ds, queries_n[h])
                result.append(carry[h] + dot32(k_t[h, :, ks], ds))
            return tuple(result)

        dq = lax.fori_loop(0, i + 1, back, wide_zeros)
        cos_t, sin_t = cos_ref[:, qs], sin_ref[:, qs]
        for h in hs:
            out[i, 0, :, lanes(h)] = turn(dq[h] * scale, cos_t, -sin_t).T.astype(BF)
            out[i, 3, :, lanes(h)] = mixed[h].T.astype(BF)

    @pl.loop(0, steps)
    def _(i):
        one_tile(i)
        between(i)

    @pl.loop(0, steps)
    def _(i):
        place = pl.ds(pl.multiple_of(i * tile, tile), tile)
        cos_t, sin_t = cos_ref[:, place], sin_ref[:, place]
        for h in hs:
            out[i, 1, :, lanes(h)] = turn(dk_acc[h, place, :].T, cos_t, -sin_t).T.astype(BF)
            out[i, 2, :, lanes(h)] = dv_acc[h, place, :].astype(BF)


def middle_kernel(shapes, heads, tokens, schedule, *refs):
    count = len(shapes)
    land, cos_ref, sin_ref, start_ref = refs[:4]
    own, refs = refs[4 : 4 + count], refs[4 + count :]
    home, refs = refs[0], refs[1:]
    outs, refs = refs[:count], refs[count:]
    scratch, refs = refs[:10], refs[10:]
    home_sems, home_keep, refs = refs[0], refs[1], refs[2:]
    landed, crossed, stage = (refs[i * count : (i + 1) * count] for i in range(3))
    out = scratch[0]
    nz, att = out.shape[0], out.shape[3]
    groups = att // (heads * HD)
    x, z = lax.axis_index("dp"), lax.axis_index("blk")
    greet([{"dp": 1 - x}] + [{"blk": flip(z, m)} for m in range(1, nz)])
    work = Chain(shapes, own, outs, landed, crossed, stage, *refs[3 * count :])
    work.begin()

    def lanes(p):
        return pl.ds(p * heads * HD, heads * HD)

    def back(p, m):
        src = out.at[flip(z, m), :, :, lanes(p)]
        dst = home.at[:, z, :, lanes(p)]
        if m == 0:
            return pltpu.make_async_copy(src, dst, home_keep.at[p])
        return pltpu.make_async_remote_copy(
            src, dst, home_sems.at[0, p, m], home_sems.at[1, p, m], device_id={"blk": flip(z, m)}, device_id_type=MESH
        )

    def arrived(p, m):
        ref = home.at[:, flip(z, m), :, lanes(p)]
        return pltpu.make_async_remote_copy(
            ref, ref, home_sems.at[0, p, m], home_sems.at[1, p, m], device_id={"blk": flip(z, m)}, device_id_type=MESH
        )

    done = 0
    for p in range(groups):
        plan = schedule[p] if p < len(schedule) else ()
        first = done
        done += sum(plan)

        def between(i, plan=plan, first=first):
            at = first
            for tile, steps in enumerate(plan):
                if steps:

                    @pl.when(i == tile)
                    def _(at=at, steps=steps):
                        for c in range(at, at + steps):
                            work.step(c)

                at += steps

        attention_heads(p * heads, heads, tokens, land, cos_ref, sin_ref, start_ref, *scratch, between)
        for m in (2, 3, 1, 0):
            back(p, m).start()
    for c in range(done, work.steps):
        work.step(c)
    work.finish()
    for p in range(groups):
        for m in range(nz):
            if m == 0:
                back(p, m).wait()
            else:
                back(p, m).wait_send()
                arrived(p, m).wait_recv()


def middle(land, cos_t, sin_t, start, arrays, tokens, schedule):
    _, total, att = land.shape
    nz = total // tokens
    heads = min(2, att // HD)
    groups = att // (heads * HD)
    shapes = [a.shape for a in arrays]
    hbm = pl.BlockSpec(memory_space=pl.ANY)
    vmem = pl.BlockSpec(memory_space=pltpu.VMEM)
    results = pl.pallas_call(
        functools.partial(middle_kernel, shapes, heads, tokens, schedule),
        out_shape=[jax.ShapeDtypeStruct((4, nz, tokens, att), BF)]
        + [jax.ShapeDtypeStruct((2,) + s, BF) for s in shapes],
        in_specs=[vmem] * 4 + [hbm] * len(arrays),
        out_specs=[hbm] * (1 + len(arrays)),
        scratch_shapes=[pltpu.VMEM((nz, 4, tokens, att), BF)]
        + [pltpu.VMEM((heads, HD, total), BF)] * 4
        + [pltpu.VMEM((heads, total, HD), BF)] * 2
        + [pltpu.VMEM((heads, total, tokens), F32)]
        + [pltpu.VMEM((heads, total, HD), F32)] * 2
        + [pltpu.SemaphoreType.DMA((2, groups, nz)), pltpu.SemaphoreType.DMA((groups,))]
        + Chain.scratch(shapes, True, MIDDLE_CHUNK),
        compiler_params=pltpu.CompilerParams(
            collective_id=3, has_side_effects=True, vmem_limit_bytes=60 << 20
        ),
        cost_estimate=pl.CostEstimate(
            flops=12 * (att // HD) * total * total * HD * 4, bytes_accessed=1 << 28, transcendentals=0
        ),
        name="middle",
    )(land, cos_t, sin_t, start, *arrays)
    return results[0], results[1:]


def tail_kernel(
    shapes, split, rows, tokens, home, g_ref, normed_ref, wq_ref, wo_ref, branch_ff, dnorm_ff,
    out_sum, qkv_sum, branch_o, dnorm_o,
    stream, hcat, wcat, wo, dwo, dwq, give, take, take_y, take_x, tile_buf,
    load_sems, stream_sems, tile_sems, scatter_sems, *chain_refs,
):
    x, z, t = lax.axis_index("dp"), lax.axis_index("blk"), lax.axis_index("tensor")
    many, four = hcat.shape
    att = four // 4
    features = wo.shape[1]
    half = many // 2
    width = features // 4
    core, y = t % 2, t // 2
    peers = {"x": {"dp": 1 - x}, "y": {"tensor": flip(t, 2)}, "c": {"tensor": flip(t, 1)}}
    loads = [
        pltpu.make_async_copy(home.at[i], hcat.at[:, pl.ds(i * att, att)], load_sems.at[i]) for i in range(4)
    ] + [
        pltpu.make_async_copy(
            wq_ref.at[i, :, pl.ds(pl.multiple_of(x * att, 128), att)] if split else wq_ref.at[i],
            wcat.at[:, pl.ds(i * att, att)],
            load_sems.at[4 + i],
        )
        for i in range(3)
    ] + [pltpu.make_async_copy(wo_ref.at[pl.ds(x * att, att)] if split else wo_ref, wo, load_sems.at[7])]

    def streamed(k):
        source = g_ref if k < 2 else normed_ref
        return pltpu.make_async_copy(
            source.at[:, pl.ds((k % 2) * (features // 2), features // 2)], stream.at[k % 2], stream_sems.at[k % 2]
        )

    loads[3].start()
    streamed(0).start()
    streamed(1).start()
    for load in loads[:3] + loads[4:]:
        load.start()
    greet([{"blk": flip(z, m)} for m in (1, 2, 3)] + list(peers.values()))

    tn_dims = (((0,), (0,)), ((), ()))
    nt_dims = (((1,), (1,)), ((), ()))
    general = functools.partial(lax.dot_general, preferred_element_type=F32)
    loads[3].wait()
    for k in range(2):
        streamed(k).wait()

        @pl.loop(0, features // 1024)
        def _(j, k=k):
            columns = pl.ds(pl.multiple_of(j * 512, 512), 512)
            value = general(hcat[:, 3 * att :], stream[k, :, columns], tn_dims)
            dwo[:, pl.ds(pl.multiple_of(k * (features // 2) + j * 512, 512), 512)] = value.astype(BF)

        streamed(k + 2).start()
    for load in loads[:3]:
        load.wait()
    for k in range(2):
        streamed(k + 2).wait()

        @pl.loop(0, features // 512)
        def _(j, k=k):
            f = pl.ds(pl.multiple_of(j * 256, 256), 256)
            value = general(stream[k, :, f], hcat[:, : 3 * att], tn_dims).astype(BF)
            for i in range(3):
                at = pl.multiple_of(i * features + k * (features // 2) + j * 256, 256)
                dwq[pl.ds(at, 256), :] = value[:, i * att : (i + 1) * att]

    work = Chain(shapes, [dwo, dwq], [out_sum, qkv_sum], chain_refs[:2], chain_refs[2:4], None, *chain_refs[4:])
    work.begin()

    for load in loads[4:]:
        load.wait()

    def share(which, of_core, target, plus):
        source = branch_ff if which == 0 else dnorm_ff
        blocks = many // tokens

        def columns(v):
            return pl.ds(pl.multiple_of((2 * v + of_core) * width, width), width)

        def fetch(k):
            at = pl.ds(pl.multiple_of((k % blocks) * tokens, tokens), tokens)
            return pltpu.make_async_copy(source.at[at, columns(k // blocks)], tile_buf.at[k % 2], tile_sems.at[k % 2])

        fetch(0).start()

        @pl.loop(0, 2 * blocks)
        def _(k):
            @pl.when(k + 1 < 2 * blocks)
            def _():
                fetch(k + 1).start()

            fetch(k).wait()
            v = k // blocks
            at = pl.ds(pl.multiple_of((k % blocks) * tokens, tokens), tokens)
            value = tile_buf[k % 2].astype(F32)
            if which == 0:
                value = value + dot32(hcat[at, 3 * att :], wo[:, columns(v)])
            else:
                value = value + general(hcat[at, : 3 * att], wcat[columns(v), :], nt_dims)
            if plus:
                value = value + target[v, at, :].astype(F32)
            target[v, at, :] = value.astype(BF)

    def remote(which, stage, src, dst, to):
        return pltpu.make_async_remote_copy(
            src, dst, scatter_sems.at[0, which, stage], scatter_sems.at[1, which, stage],
            device_id=peers[to], device_id_type=MESH,
        )

    def over_core(which):
        return remote(which, 0, give, take.at[which], "c")

    def over_y(which):
        return remote(which, 1, take.at[which, 1 - y], take_y.at[which], "y")

    def over_x(which):
        return remote(which, 2, take_y.at[which, pl.ds((1 - x) * half, half)], take_x.at[which], "x")

    def stage_one(which):
        if which == 1:
            over_core(0).wait_send()
        share(which, 1 - core, give, False)
        over_core(which).start()

    def stage_two(which):
        over_core(which).wait_recv()
        share(which, core, take.at[which], True)
        over_y(which).start()

    def stage_three(which):
        over_y(which).wait_recv()

        @pl.loop(0, many // 256)
        def _(i):
            at = pl.ds(pl.multiple_of(i * 256, 256), 256)
            take_y[which, at, :] = (take_y[which, at, :].astype(F32) + take[which, y, at, :].astype(F32)).astype(BF)

        over_x(which).start()

    def stage_four(which):
        over_x(which).wait_recv()
        target = (branch_o, dnorm_o)[which]

        @pl.loop(0, half // 256)
        def _(i):
            at = pl.ds(pl.multiple_of(i * 256, 256), 256)
            mine = pl.ds(pl.multiple_of(x * half + i * 256, 256), 256)
            target[at, :] = take_x[which, at, :].astype(F32) + take_y[which, mine, :].astype(F32)

    stages = {
        0: [(stage_one, 0)], 1: [(stage_one, 1)], 2: [(stage_two, 0)], 3: [(stage_two, 1)],
        11: [(stage_three, 0)], 15: [(stage_three, 1)], 16: [(stage_four, 0)],
    }
    last = [(stage_three, 0), (stage_three, 1), (stage_four, 0), (stage_four, 1)]
    for c in range(work.steps):
        for stage, which in stages.get(c, ()):
            stage(which)
            if (stage, which) in last:
                last.remove((stage, which))
        work.step(c)
    for stage, which in last:
        stage(which)
    work.finish()
    over_core(1).wait_send()
    for which in range(2):
        over_y(which).wait_send()
        over_x(which).wait_send()


def tail(split, rows, tokens, home, cotangent, normed, wq, wo, branch_ff, dnorm_ff, att):
    many, features = normed.shape
    width = features // 4
    half = many // 2
    shapes = [(att, features), (3 * features, att)]
    hbm = pl.BlockSpec(memory_space=pl.ANY)
    vmem = pl.BlockSpec(memory_space=pltpu.VMEM)
    return pl.pallas_call(
        functools.partial(tail_kernel, shapes, split, rows, tokens),
        out_shape=[jax.ShapeDtypeStruct((2,) + s, BF) for s in shapes]
        + [jax.ShapeDtypeStruct((half, width), F32)] * 2,
        in_specs=[hbm] * 7,
        out_specs=[hbm] * 2 + [vmem] * 2,
        scratch_shapes=[
            pltpu.VMEM((2, many, features // 2), BF),
            pltpu.VMEM((many, 4 * att), BF),
            pltpu.VMEM((features, 3 * att), BF),
            pltpu.VMEM((att, features), BF),
            pltpu.VMEM((att, features), BF),
            pltpu.VMEM((3 * features, att), BF),
            pltpu.VMEM((2, many, width), BF),
            pltpu.VMEM((2, 2, many, width), BF),
            pltpu.VMEM((2, many, width), BF),
            pltpu.VMEM((2, half, width), BF),
            pltpu.VMEM((2, tokens, width), BF),
            pltpu.SemaphoreType.DMA((8,)),
            pltpu.SemaphoreType.DMA((2,)),
            pltpu.SemaphoreType.DMA((2,)),
            pltpu.SemaphoreType.DMA((2, 2, 3)),
        ]
        + Chain.scratch(shapes, False, TAIL_CHUNK),
        compiler_params=pltpu.CompilerParams(
            collective_id=4, has_side_effects=True, vmem_limit_bytes=62 << 20
        ),
        cost_estimate=pl.CostEstimate(flops=30 << 30, bytes_accessed=1 << 28, transcendentals=0),
        name="tail",
    )(home, cotangent, normed, wq, wo, branch_ff, dnorm_ff)


def widen(source, by_columns):
    _, rows, columns = source.shape
    size = min(rows, (1 << 18) // columns)

    def body(source_ref, out_ref):
        out_ref[...] = source_ref[0].astype(F32)

    if by_columns and columns % 128:
        both = jnp.concatenate([source[0], source[1]], axis=1)
        return both.astype(F32)
    shape = (rows, 2 * columns) if by_columns else (2 * rows, columns)
    steps = rows // size
    out_map = (lambda i, h: (i, h)) if by_columns else (lambda i, h: (h * steps + i, 0))
    return pl.pallas_call(
        body,
        out_shape=jax.ShapeDtypeStruct(shape, F32),
        grid=(steps, 2),
        in_specs=[pl.BlockSpec((1, size, columns), lambda i, h: (h, i, 0))],
        out_specs=pl.BlockSpec((size, columns), out_map),
        compiler_params=pltpu.CompilerParams(vmem_limit_bytes=32 << 20),
        cost_estimate=pl.CostEstimate(flops=0, bytes_accessed=source.size * 6, transcendentals=0),
        name="widen",
    )(source)


def scatter_sum(share):
    whole = lax.psum_scatter(share.astype(BF), "dp", scatter_dimension=0, tiled=True)
    return lax.psum_scatter(whole, "tensor", scatter_dimension=2, tiled=True).astype(F32)


def butterfly(value, axes):
    for axis, size in axes:
        mask = 1
        while mask < size:
            value = value + swap(value, axis, size, mask)
            mask *= 2
    return value


SCHEDULE = ((0, 0, 1, 1), (0, 0, 1, 1))


def local(
    nx, nz, nt, block_input, segment_ids, layer_norm_gain, layer_norm_bias, qkv_weight, qkv_bias, out_weight, out_bias,
    up_weight, up_bias, down_weight, down_bias, grad_output,
):
    rows, tokens, width = block_input.shape
    all_rows = nx * rows
    features = nt * width
    many = all_rows * tokens
    x, z, t = lax.axis_index("dp"), lax.axis_index("blk"), lax.axis_index("tensor")
    att = qkv_weight.shape[2] // nx
    ff = up_weight.shape[1] // nx

    gather = nt == 4 and nx == 2
    split = att % 128 == 0
    qkv_whole = jnp.transpose(qkv_weight, (1, 0, 2))
    qkv_half = lax.dynamic_slice_in_dim(qkv_whole, x * att, att, 2)
    qkv_half_bias = lax.dynamic_slice_in_dim(qkv_bias, x * att, att, 1)
    out_half = lax.dynamic_slice_in_dim(out_weight, x * att, att, 0)
    up_half_bias = lax.dynamic_slice_in_dim(up_bias, x * ff, ff, 0)
    if split:
        weights = [qkv_whole, out_weight, up_weight, down_weight]
    else:
        up_half = lax.dynamic_slice_in_dim(up_weight, x * ff, ff, 1)
        down_half = lax.dynamic_slice_in_dim(down_weight, x * ff, ff, 0)
        weights = [qkv_half, out_half, up_half, down_half]

    segments = lax.ppermute(segment_ids, "dp", [(0, 1), (1, 0)])
    segments = jnp.where(z // rows == x, segment_ids, segments)
    segments = lax.dynamic_slice_in_dim(segments, z % rows, 1, 0)
    length = segments.shape[1]
    places = jnp.arange(length, dtype=jnp.int32)[None]
    changed = jnp.concatenate(
        [jnp.ones((1, 1), dtype=bool), segments[:, 1:] != segments[:, :-1]], axis=1
    )
    start = lax.cummax(jnp.where(changed, places, 0), axis=1)
    half_rot = ROT // 2
    frequency = jnp.exp(jnp.arange(half_rot).astype(F32) * (-2.0 / ROT) * ROPE_LOG_BASE)
    angles = frequency[:, None] * (places - start).astype(F32)
    cos_t, sin_t = jnp.cos(angles), jnp.sin(angles)

    if gather:
        sources = [block_input.reshape(rows * tokens, width), grad_output.reshape(rows * tokens, width)]
    else:
        sources = [lax.all_gather(a, "tensor", axis=2, tiled=True) for a in (block_input, grad_output)]
        sources = [lax.all_gather(a, "dp", axis=0, tiled=True).reshape(many, features) for a in sources]
    normed, cotangent, land, stats, down_part, up_part, branch_ff, d_normed_ff, up_bias_part = front(
        gather, split, rows, tokens, nz, many, features, att, ff,
        [
            *sources, layer_norm_gain.reshape(1, features), layer_norm_bias.reshape(1, features), weights[0],
            qkv_half_bias.reshape(3, 1, att), weights[1], weights[2], up_half_bias.reshape(1, ff), weights[3],
        ],
    )
    home, (down_sum, up_sum) = middle(
        land, cos_t, sin_t, start, [down_part, up_part], tokens, SCHEDULE
    )
    home = home.reshape(4, many, att)
    qkv_bias_part = jnp.sum(home[:3].astype(F32), axis=1)
    up_bias_part = up_bias_part[0]
    if gather:
        out_sum, qkv_sum, branch, d_normed = tail(
            split, rows, tokens, home, cotangent, normed, weights[0], weights[1], branch_ff, d_normed_ff, att
        )
        branch = branch.reshape(rows, tokens, width)
        d_normed = d_normed.reshape(rows, tokens, width)
    else:
        branch = branch_ff.astype(F32) + dot32(home[3], out_half)
        d_normed = d_normed_ff.astype(F32)
        for i in range(3):
            d_normed = d_normed + dot32(home[i], qkv_half[i].T)
        branch = scatter_sum(branch.reshape(all_rows, tokens, features))
        d_normed = scatter_sum(d_normed.reshape(all_rows, tokens, features))
        qkv_part = jnp.concatenate([dot32(normed.T, home[i]).astype(BF) for i in range(3)])
        out_sum, qkv_sum = chain([dot32(home[3].T, cotangent).astype(BF), qkv_part], 1)

    block_output = (block_input.astype(F32) + (branch + out_bias + down_bias)).astype(BF)

    gain = lax.dynamic_slice_in_dim(layer_norm_gain, t * width, width, 0)
    stats = lax.dynamic_slice_in_dim(stats, x * rows * tokens, rows * tokens, 0).reshape(rows, tokens, 128)
    own_mean, own_inverse = stats[..., :1], stats[..., 64:65]
    xhat = (block_input.astype(F32) - own_mean) * own_inverse
    scaled = d_normed * gain
    moments = jnp.stack([jnp.sum(scaled, axis=-1), jnp.sum(scaled * xhat, axis=-1)])
    moments = butterfly(moments, [("tensor", nt)]) / features
    first, second = moments[0][..., None], moments[1][..., None]
    input_grad = (
        grad_output.astype(F32) + own_inverse * (scaled - first - xhat * second)
    ).astype(BF)

    def spread(part, whole):
        shape = part.shape[:-1] + (whole,)
        at = (0,) * (part.ndim - 1) + (x * part.shape[-1],)
        return lax.dynamic_update_slice(jnp.zeros(shape, F32), part, at)

    small = [
        jnp.sum(d_normed * xhat, axis=(0, 1)),
        jnp.sum(d_normed, axis=(0, 1)),
        jnp.sum(grad_output.astype(F32), axis=(0, 1)),
        spread(up_bias_part, nx * ff),
        spread(qkv_bias_part, nx * att).reshape(-1),
    ]
    packed = butterfly(jnp.concatenate(small), [("dp", nx), ("blk", nz)])
    gain_grad, shift_grad, bias_grad = (packed[i * width : (i + 1) * width] for i in range(3))
    up_bias_grad = packed[3 * width : 3 * width + nx * ff]
    qkv_bias_grad = packed[3 * width + nx * ff :].reshape(3, nx * att)

    down_grad = widen(down_sum, False)
    up_grad = widen(up_sum, True)
    out_grad = widen(out_sum, False)
    qkv_grad = widen(qkv_sum, True).reshape(3, features, nx * att)
    qkv_grad = jnp.transpose(qkv_grad, (1, 0, 2))
    return (
        block_output, input_grad, gain_grad, shift_grad, qkv_grad, qkv_bias_grad, out_grad, bias_grad, up_grad,
        up_bias_grad, down_grad, bias_grad,
    )


def solution(mesh):
    in_specs = (
        P("dp", "blk", "tensor"), P("dp", None), P(), P(), P(None, None, "tensor"), P(None, "tensor"), P("tensor", None),
        P("tensor"), P(None, "tensor"), P("tensor"), P("tensor", None), P("tensor"), P("dp", "blk", "tensor"),
    )
    out_specs = (
        P("dp", "blk", "tensor"), P("dp", "blk", "tensor"), P("tensor"), P("tensor"), P(None, None, "tensor"),
        P(None, "tensor"), P("tensor", None), P("tensor"), P(None, "tensor"), P("tensor"), P("tensor", None), P("tensor"),
    )
    body = functools.partial(local, mesh.shape["dp"], mesh.shape["blk"], mesh.shape["tensor"])
    return jax.shard_map(body, mesh=mesh, in_specs=in_specs, out_specs=out_specs, check_vma=False)
```

```python
import functools
import math

import jax
import jax.numpy as jnp
from jax import lax
from jax.experimental import pallas as pl
from jax.experimental.pallas import tpu as pltpu
from jax.sharding import PartitionSpec as P

HD = 64
ROT = 32
EPSILON = 1e-05
ROPE_LOG_BASE = math.log(10000.0)
NEGATIVE = -1e30
F32 = jnp.float32
BF = jnp.bfloat16
MESH = pl.DeviceIdType.MESH
dot32 = functools.partial(jnp.dot, preferred_element_type=F32)


def swap(value, axis, size, mask):
    return lax.ppermute(value, axis, [(i, i ^ mask) for i in range(size)])


def flip(index, mask):
    if mask == 0:
        return index
    if mask == 1:
        return index + 1 - 2 * (index % 2)
    if mask == 2:
        return (index + 2) % 4
    return 3 - index


def core_share(cross_ref, stage, cross_sems, stage_sems, tokens, t, value, out):
    _, many, width = out.shape
    blocks = many // tokens
    core = t % 2

    def place(k):
        return pl.ds(pl.multiple_of((k % blocks) * tokens, tokens), tokens)

    def tile(slot, k):
        return stage.at[k % 2, :, pl.ds(slot * width, width)]

    def at(ref, k):
        return ref.at[k // blocks, place(k)]

    def columns(k, of_core):
        return pl.ds(pl.multiple_of((2 * (k // blocks) + of_core) * width, width), width)

    def cross(k, src, dst):
        return pltpu.make_async_remote_copy(
            src, dst, cross_sems.at[0, k], cross_sems.at[1, k], device_id={"tensor": flip(t, 1)}, device_id_type=MESH
        )

    def give(k):
        return cross(k, tile(0, k), at(cross_ref, k))

    def got(k):
        return cross(k, at(cross_ref, k), at(cross_ref, k))

    def fetch(k):
        return pltpu.make_async_copy(at(cross_ref, k), tile(1, k), stage_sems.at[k % 2])

    def keep(k):
        return pltpu.make_async_copy(tile(2, k), at(out, k), stage_sems.at[2 + k % 2])

    @pl.loop(0, 2 * blocks)
    def _(k):
        @pl.when(k >= 2)
        def _():
            give(k - 2).wait_send()

        stage[k % 2, :, :width] = value(place(k), columns(k, 1 - core)).astype(BF)
        give(k).start()

    for k in (2 * blocks - 2, 2 * blocks - 1):
        give(k).wait_send()
    got(0).wait_recv()
    fetch(0).start()

    @pl.loop(0, 2 * blocks)
    def _(k):
        @pl.when(k >= 2)
        def _():
            keep(k - 2).wait()

        @pl.when(k + 1 < 2 * blocks)
        def _():
            got(k + 1).wait_recv()
            fetch(k + 1).start()

        mine = value(place(k), columns(k, core))
        fetch(k).wait()
        stage[k % 2, :, 2 * width : 3 * width] = (mine + stage[k % 2, :, width : 2 * width].astype(F32)).astype(BF)
        keep(k).start()

    for k in (2 * blocks - 2, 2 * blocks - 1):
        keep(k).wait()


def front_kernel(
    gather, split, rows, tokens, x_own, g_own, gain_ref, shift_ref, wq_ref, bq_ref, wo_ref, wu_ref, bu_ref, wd_ref,
    normed_o, g_o, land_o, stats_o, down_o, d_hidden_o, branch_o, ubias_o, branch_y_o, cross_o,
    xin, gin, vq, vo, vu, vd, pay, act, slope, stage, gather_sems, land_sems, load_sems, keep_sems, stage_sems, cross_sems, over_y_sems,
):
    x, z, t = lax.axis_index("dp"), lax.axis_index("blk"), lax.axis_index("tensor")
    many, features = xin.shape
    half = rows * tokens
    width = features // 4
    att = vq.shape[2]
    ff = vu.shape[1]
    nz = pay.shape[0]
    wide = min(512, ff)

    def remote(src, dst, sems, device):
        return pltpu.make_async_remote_copy(
            src, dst, sems[0], sems[1], device_id=device, device_id_type=MESH
        )

    peers = {"x": {"dp": 1 - x}, "y": {"tensor": flip(t, 2)}, "c": {"tensor": flip(t, 1)}}
    barrier = pltpu.get_barrier_semaphore()
    greet = [{"blk": flip(z, m)} for m in range(1, nz)] + (list(peers.values()) if gather else [])
    for device in greet:
        pl.semaphore_signal(barrier, inc=1, device_id=device, device_id_type=MESH)

    loads = [
        pltpu.make_async_copy(
            wq_ref.at[:, :, pl.ds(pl.multiple_of(x * att, 128), att)] if split else wq_ref, vq, load_sems.at[0]
        ),
        pltpu.make_async_copy(
            wu_ref.at[:, pl.ds(pl.multiple_of(x * ff, 128), ff)] if split else wu_ref, vu, load_sems.at[1]
        ),
        pltpu.make_async_copy(wd_ref.at[pl.ds(x * ff, ff)] if split else wd_ref, vd, load_sems.at[2]),
        pltpu.make_async_copy(wo_ref.at[pl.ds(x * att, att)] if split else wo_ref, vo, load_sems.at[3]),
    ]
    if not gather:
        both = [
            pltpu.make_async_copy(x_own, xin, load_sems.at[4]),
            pltpu.make_async_copy(g_own, gin, load_sems.at[5]),
        ]
    else:
        both = [
            pltpu.make_async_copy(
                own,
                buf.at[pl.ds(x * half, half), pl.ds(pl.multiple_of(t * width, 128), width)],
                load_sems.at[4 + i],
            )
            for i, (own, buf) in enumerate([(x_own, xin), (g_own, gin)])
        ]
    both[0].start()
    both[1].start()
    pl.semaphore_wait(barrier, len(greet))

    class Gather:
        def __init__(self, which, own, buf, first, size):
            self.which, self.own, self.buf, self.names = which, own, buf, []
            self.base, self.size = first, size

        def at(self, dx, dt, r):
            return self.buf.at[
                pl.ds(pl.multiple_of((1 - x if dx else x) * half + self.base + r * self.size, self.size), self.size),
                pl.ds(pl.multiple_of(flip(t, dt) * width, 128), width),
            ]

        plan = {
            "x": (0, 0, "x", 1, 0), "y": (0, 0, "y", 0, 2), "c": (0, 0, "c", 0, 1),
            "ex": (1, 0, "c", 1, 1), "ey": (0, 2, "c", 0, 3), "ed": (1, 2, "c", 1, 3),
        }

        def sems(self, kind, r):
            k = 2 * ("x", "y", "c", "d", "ex", "ey", "ed").index(kind) + r
            return gather_sems.at[self.which, 0, k], gather_sems.at[self.which, 1, k]

        def copy(self, kind, r):
            if kind == "d":
                dx, dt, to = (1, 0, "y") if r == 0 else (0, 2, "x")
            else:
                dx, dt, to = self.plan[kind][:3]
            src = dst = self.at(dx, dt, r)
            if kind in "xyc":
                src = self.own.at[pl.ds(self.base + r * self.size, self.size)]
            return remote(src, dst, self.sems(kind, r), peers[to])

        def start(self, kind, r):
            self.names.append((kind, r))
            self.copy(kind, r).start()

        def wait(self, kind, r):
            if kind == "d":
                dx, dt, to = 1, 2, "y"
            else:
                to, dx, dt = self.plan[kind][2:]
            ref = self.at(dx, dt, r)
            remote(ref, ref, self.sems(kind, r), peers[to]).wait_recv()

        def begin(self):
            for kind, r in (("x", 0), ("y", 1), ("x", 1), ("y", 0), ("c", 0), ("c", 1)):
                self.start(kind, r)

        def second(self):
            self.wait("x", 0)
            self.start("d", 0)
            self.start("ex", 0)
            self.wait("y", 1)
            self.start("d", 1)
            self.start("ey", 1)

        def third(self):
            self.wait("x", 1)
            self.start("ex", 1)
            self.wait("y", 0)
            self.start("ey", 0)

        def fourth(self):
            self.wait("d", 0)
            self.start("ed", 0)
            self.wait("d", 1)
            self.start("ed", 1)

        def last(self):
            for kind in ("c", "ex", "ey", "ed"):
                for r in range(2):
                    self.wait(kind, r)

        def drain(self):
            for kind, r in self.names:
                self.copy(kind, r).wait_send()

    ins = [Gather(r, x_own, xin, r * tokens, tokens // 2) for r in range(rows)]
    cots = Gather(rows, g_own, gin, 0, half // 2)
    if gather:
        ins[0].begin()
    for load in loads:
        load.start()

    def place(position):
        return pl.ds(pl.multiple_of(position * tokens, tokens), tokens)

    def normalize(row):
        @pl.loop(0, tokens // 128)
        def _(i):
            at = pl.ds(pl.multiple_of(row * tokens + i * 128, 128), 128)
            v = xin[at, :].astype(F32)
            mean = jnp.sum(v, axis=-1, keepdims=True) * (1.0 / features)
            v = v - mean
            inverse = lax.rsqrt(jnp.sum(v * v, axis=-1, keepdims=True) * (1.0 / features) + EPSILON)
            xin[at, :] = (v * inverse * gain_ref[...] + shift_ref[...]).astype(BF)
            lane = lax.broadcasted_iota(jnp.int32, (128, 128), 1)
            stats_o[at, :] = jnp.where(lane < 64, mean, inverse)

    def parts(kind):
        return pl.ds(0, 3) if kind == 0 else pl.ds(3, 1)

    def sems(kind, m):
        return land_sems.at[0, kind, m], land_sems.at[1, kind, m]

    def own_row(kind):
        return pltpu.make_async_copy(
            pay.at[z, parts(kind)], land_o.at[parts(kind), place(z)], keep_sems.at[2 + kind]
        )

    def other_row(kind, row, m):
        return remote(pay.at[row, parts(kind)], land_o.at[parts(kind), place(z)], sems(kind, m), {"blk": row})

    def send(kind, row):
        @pl.when(z == row)
        def _():
            own_row(kind).start()

        @pl.when(z != row)
        def _():
            other_row(kind, row, flip(z, row)).start()

    def landed(kind, m):
        ref = land_o.at[parts(kind), place(flip(z, m))]
        return remote(ref, ref, sems(kind, m), {"blk": flip(z, m)})

    def project(row):
        @pl.loop(0, 3)
        def _(part):
            value = dot32(xin[place(row), :], vq[part]) + bq_ref[part]
            pay[row, part] = value.astype(BF)

        send(0, row)

    if gather:
        ins[0].second()
        ins[0].third()
        ins[1].begin()
        ins[0].fourth()
    both[0].wait()
    for r in range(rows):
        if gather:
            ins[r].last()
            ins[r].drain()
        for row in range(r, nz, rows):
            normalize(row)
        if gather and r == 0:
            ins[1].second()
        if r == 0:
            loads[0].wait()
        for row in range(r, nz, rows):
            project(row)
        if gather and r == 0:
            ins[1].third()
            cots.begin()
            ins[1].fourth()
    keep_normed = pltpu.make_async_copy(xin, normed_o, keep_sems.at[0])
    keep_normed.start()
    if gather:
        cots.second()

    loads[1].wait()

    @pl.loop(0, many // tokens)
    def _(i):
        at = place(i)

        @pl.loop(0, ff // wide)
        def _(j):
            columns = pl.ds(pl.multiple_of(j * wide, wide), wide)
            h = dot32(xin[at, :], vu[:, columns]) + bu_ref[:, columns]
            c = math.sqrt(2.0 / math.pi)
            square = h * h
            tanh = jnp.tanh(c * h * (1.0 + 0.044715 * square))
            one = 0.5 * (1.0 + tanh)
            act[at, columns] = (h * one).astype(BF)
            d = one + 0.5 * h * (1.0 - tanh * tanh) * (c * (1.0 + 3 * 0.044715 * square))
            slope[at, columns] = d.astype(BF)

    if gather:
        cots.third()
    nt_dims = (((1,), (1,)), ((), ()))
    tn_dims = (((0,), (0,)), ((), ()))
    general = functools.partial(lax.dot_general, preferred_element_type=F32)

    def through(steps, rows_of, columns_of, make, out):
        def copy(i):
            return pltpu.make_async_copy(
                stage.at[i % 2, pl.ds(0, rows_of), pl.ds(0, columns_of)],
                out.at[pl.ds(pl.multiple_of(i * rows_of, rows_of), rows_of)],
                stage_sems.at[i % 2],
            )

        @pl.loop(0, steps)
        def _(i):
            @pl.when(i >= 2)
            def _():
                copy(i - 2).wait()

            make(i, stage.at[i % 2, pl.ds(0, rows_of), pl.ds(0, columns_of)])
            copy(i).start()

        for i in range(max(0, steps - 2), steps):
            copy(i).wait()

    loads[2].wait()
    if gather:
        core_share(
            cross_o, stage, cross_sems, stage_sems, tokens, t,
            lambda at, columns: dot32(act[at, :], vd[:, columns]), branch_o,
        )
        branch_over_y = remote(
            branch_o.at[1 - t // 2, pl.ds(0, half)], branch_y_o, (over_y_sems.at[0], over_y_sems.at[1]), peers["y"]
        )
        branch_over_y.start()
    else:

        def whole(i, target):
            @pl.loop(0, features // 512)
            def _(j):
                columns = pl.ds(pl.multiple_of(j * 512, 512), 512)
                target[:, columns] = dot32(act[place(i), :], vd[:, columns]).astype(BF)

        through(many // tokens, tokens, features, whole, branch_o)

    if gather:
        cots.fourth()
    both[1].wait()
    if gather:
        cots.last()
    keep_g = pltpu.make_async_copy(gin, g_o, keep_sems.at[1])
    keep_g.start()

    loads[3].wait()
    for row in range(nz):
        pay[row, 3] = general(gin[place(row), :], vo[...], nt_dims).astype(BF)
        send(1, row)

    ubias_o[...] = jnp.zeros_like(ubias_o)

    @pl.loop(0, many // tokens)
    def _(i):
        at = place(i)

        @pl.loop(0, ff // wide)
        def _(j):
            columns = pl.ds(pl.multiple_of(j * wide, wide), wide)
            d = general(gin[at, :], vd[columns, :], nt_dims) * slope[at, columns].astype(F32)
            d = d.astype(BF)
            slope[at, columns] = d
            ubias_o[0:1, columns] += jnp.sum(d.astype(F32), axis=0, keepdims=True)

    keep_d = pltpu.make_async_copy(slope, d_hidden_o, keep_sems.at[4])
    keep_d.start()

    def down_tile(i, target):
        f = pl.ds(pl.multiple_of(i * 256, 256), 256)
        for j in range(0, features, 1024):
            target[:, j : j + 1024] = general(act[:, f], gin[:, j : j + 1024], tn_dims).astype(BF)

    through(ff // 256, 256, features, down_tile, down_o)

    keep_normed.wait()
    keep_g.wait()
    keep_d.wait()
    for kind in range(2):
        own_row(kind).wait()
        for m in range(1, nz):
            other_row(kind, flip(z, m), m).wait_send()
            landed(kind, m).wait_recv()
    if gather:
        cots.drain()
        branch_over_y.wait()


def front(gather, split, rows, tokens, nz, many, features, att, ff, operands):
    hbm = pl.BlockSpec(memory_space=pl.ANY)
    vmem = pl.BlockSpec(memory_space=pltpu.VMEM)
    shares = (2, many, features // 4) if gather else (many, features)
    return pl.pallas_call(
        functools.partial(front_kernel, gather, split, rows, tokens),
        out_shape=[
            jax.ShapeDtypeStruct((many, features), BF),
            jax.ShapeDtypeStruct((many, features), BF),
            jax.ShapeDtypeStruct((4, nz * tokens, att), BF),
            jax.ShapeDtypeStruct((many, 128), F32),
            jax.ShapeDtypeStruct((ff, features), BF),
            jax.ShapeDtypeStruct((many, ff), BF),
            jax.ShapeDtypeStruct(shares, BF),
            jax.ShapeDtypeStruct((8, ff), F32),
            jax.ShapeDtypeStruct((many // 2, features // 4), BF),
            jax.ShapeDtypeStruct((2, many, features // 4), BF),
        ],
        in_specs=[hbm, hbm, vmem, vmem, hbm, vmem, hbm, hbm, vmem, hbm],
        out_specs=[hbm, hbm, hbm, vmem, hbm, hbm, hbm, vmem, hbm, hbm],
        scratch_shapes=[
            pltpu.VMEM((many, features), BF),
            pltpu.VMEM((many, features), BF),
            pltpu.VMEM((3, features, att), BF),
            pltpu.VMEM((att, features), BF),
            pltpu.VMEM((features, ff), BF),
            pltpu.VMEM((ff, features), BF),
            pltpu.VMEM((nz, 4, tokens, att), BF),
            pltpu.VMEM((many, ff), BF),
            pltpu.VMEM((many, ff), BF),
            pltpu.VMEM((2, tokens, features), BF),
            pltpu.SemaphoreType.DMA((rows + 1, 2, 14)),
            pltpu.SemaphoreType.DMA((2, 2, 4)),
            pltpu.SemaphoreType.DMA((6,)),
            pltpu.SemaphoreType.DMA((5,)),
            pltpu.SemaphoreType.DMA((4,)),
            pltpu.SemaphoreType.DMA((2, 2 * many // tokens)),
            pltpu.SemaphoreType.DMA((2,)),
        ],
        compiler_params=pltpu.CompilerParams(
            collective_id=2, has_side_effects=True, vmem_limit_bytes=60 << 20
        ),
        cost_estimate=pl.CostEstimate(
            flops=2 * many * features * (6 * ff + 4 * att), bytes_accessed=100 << 20, transcendentals=0
        ),
        name="front",
    )(*operands)[:9]


def add_rows(target, one, two):
    @pl.loop(0, target.shape[0], step=32)
    def _(r):
        at = pl.ds(pl.multiple_of(r, 32), 32)
        target[at] = (one[at].astype(F32) + two[at].astype(F32)).astype(BF)


class Chain:
    COLUMNS = 256
    SLOTS = {"own": 3, "in": 2, "cross": 2, "sum": 4, "total": 6}
    END_LAG = 5
    MID_LAG = 2
    INWARD = 4
    ASIDE = 8

    @classmethod
    def layout(cls, arrays):
        chunks, rings = [], {}
        for a, (rows, columns, size, _) in enumerate(arrays):
            size, wide = math.gcd(rows, size), math.gcd(columns, cls.COLUMNS)
            rings[wide] = max(rings.get(wide, 0), size)
            chunks += [(a, r, size, c, wide) for r in range(0, rows, size) for c in range(0, columns, wide)]
        return chunks, rings

    @classmethod
    def scratch(cls, arrays):
        chunks, rings = cls.layout(arrays)
        return [pltpu.VMEM((k, rows, wide), BF) for wide, rows in rings.items() for k in cls.SLOTS.values()] + [
            pltpu.SemaphoreType.DMA((8, len(chunks))),
            pltpu.SemaphoreType.DMA((3, 3)),
            pltpu.SemaphoreType.DMA((len(chunks),)),
        ]

    def __init__(self, arrays, own, outs, landed, crossed, scratch):
        self.arrays, self.own, self.outs, self.landed, self.crossed = arrays, own, outs, landed, crossed
        self.chunks, rings = self.layout(arrays)
        scratch = list(scratch)
        self.rings = {wide: {name: scratch.pop(0) for name in self.SLOTS} for wide in rings}
        self.sems, self.load_sems, self.keep_sem = scratch
        self.n = len(self.chunks)
        self.x, self.z = lax.axis_index("dp"), lax.axis_index("blk")
        self.at_end = (self.z == 0) | (self.z == 3)
        self.inner = jnp.where(self.z == 0, 1, 2)
        self.outer = jnp.where(self.z == 1, 0, 3)

    def send(self, kind, c, src, dst, device):
        return pltpu.make_async_remote_copy(
            src, dst, self.sems.at[2 * kind, c], self.sems.at[2 * kind + 1, c],
            device_id=device, device_id_type=MESH,
        )

    def part(self, refs, c):
        a, r, rows, column, columns = self.chunks[c]
        return refs[a].at[pl.ds(r, rows), pl.ds(column, columns)]

    def final(self, c, half):
        a, r, rows, column, columns = self.chunks[c]
        return self.outs[a].at[half, pl.ds(r, rows), pl.ds(column, columns)]

    def slot(self, name, c):
        _, _, rows, _, columns = self.chunks[c]
        return self.rings[columns][name].at[c % self.SLOTS[name], pl.ds(0, rows)]

    def go_in(self, c):
        return self.send(0, c, self.part(self.own, c), self.part(self.landed, c), {"blk": self.inner})

    def arrive_in(self, c):
        ref = self.part(self.landed, c)
        return self.send(0, c, ref, ref, {"blk": self.outer})

    def go_mid(self, c):
        return self.send(1, c, self.slot("sum", c), self.part(self.crossed, c), {"blk": 3 - self.z})

    def go_out(self, c):
        return self.send(2, c, self.slot("total", c), self.final(c, self.x), {"blk": self.outer})

    def arrive_out(self, c):
        return self.send(2, c, self.final(c, self.x), self.final(c, self.x), {"blk": self.inner})

    def go_x(self, c, end):
        src = self.final(c, self.x) if end else self.slot("total", c)
        return self.send(3, c, src, self.final(c, self.x), {"dp": 1 - self.x})

    def arrive_x(self, c):
        ref = self.final(c, 1 - self.x)
        return self.send(3, c, ref, ref, {"dp": 1 - self.x})

    def load(self, name, refs, c):
        at = self.load_sems.at[list(self.SLOTS).index(name), c % self.SLOTS[name]]
        return pltpu.make_async_copy(self.part(refs, c), self.slot(name, c), at)

    def load_own(self, c):
        return self.load("own", self.own, c)

    def in_hbm(self, c):
        return c < self.n and self.arrays[self.chunks[c][0]][3]

    def keep(self, c):
        return pltpu.make_async_copy(self.slot("total", c), self.final(c, self.x), self.keep_sem.at[c])

    @property
    def steps(self):
        return self.n + self.END_LAG

    def begin(self):
        @pl.when(self.at_end)
        def _():
            for c in range(min(self.INWARD, self.n)):
                self.go_in(c).start()

        @pl.when(jnp.logical_not(self.at_end))
        def _():
            for c in range(2):
                if self.in_hbm(c):
                    self.load_own(c).start()

    def sent(self, c):
        self.go_out(c).wait_send()
        self.go_x(c, False).wait_send()
        self.keep(c).wait()

    def step(self, c):
        n, slots = self.n, self.SLOTS

        @pl.when(self.at_end)
        def _():
            if c < n:
                self.go_in(c).wait_send()
                if c + self.INWARD < n:
                    self.go_in(c + self.INWARD).start()
            d = c - self.END_LAG
            if 0 <= d < n:
                self.arrive_out(d).wait_recv()
                if d >= self.ASIDE:
                    self.go_x(d - self.ASIDE, True).wait_send()
                self.go_x(d, True).start()

        if c >= n + self.MID_LAG:
            return

        @pl.when(jnp.logical_not(self.at_end))
        def _():
            d = c - self.MID_LAG
            if c < n:
                if self.in_hbm(c + 2):
                    self.load_own(c + 2).start()
                self.arrive_in(c).wait_recv()
                self.load("in", self.landed, c).start()
                if self.in_hbm(c):
                    self.load_own(c).wait()
                    mine = self.slot("own", c)
                else:
                    mine = self.part(self.own, c)
                if c >= slots["sum"]:
                    self.go_mid(c - slots["sum"]).wait_send()
                self.load("in", self.landed, c).wait()
                add_rows(self.slot("sum", c), self.slot("in", c), mine)
                self.go_mid(c).start()
            if 0 <= d < n:
                self.go_mid(d).wait_recv()
                self.load("cross", self.crossed, d).start()
                if d >= slots["total"]:
                    self.sent(d - slots["total"])
                self.load("cross", self.crossed, d).wait()
                add_rows(self.slot("total", d), self.slot("cross", d), self.slot("sum", d))
                self.go_out(d).start()
                self.go_x(d, False).start()
                self.keep(d).start()

    def finish(self):
        n, slots = self.n, self.SLOTS

        @pl.when(self.at_end)
        def _():
            for c in range(max(0, n - self.ASIDE), n):
                self.go_x(c, True).wait_send()

        @pl.when(jnp.logical_not(self.at_end))
        def _():
            for c in range(max(0, n - slots["sum"]), n):
                self.go_mid(c).wait_send()
            for c in range(max(0, n - slots["total"]), n):
                self.sent(c)

        for c in range(n):
            self.arrive_x(c).wait_recv()


def greet(devices):
    barrier = pltpu.get_barrier_semaphore()
    for device in devices:
        pl.semaphore_signal(barrier, inc=1, device_id=device, device_id_type=MESH)
    pl.semaphore_wait(barrier, len(devices))


def turn(source, cos_t, sin_t):
    half = ROT // 2
    front_half, back_half = source[:half], source[half:ROT]
    return jnp.concatenate(
        [front_half * cos_t - back_half * sin_t, back_half * cos_t + front_half * sin_t, source[ROT:]], axis=0
    )


def attention_heads(
    first_head, heads, tile, land, cos_ref, sin_ref, start_ref, out, q_t, k_t, v_t, g_t, q_n, k_n, probs, dk_acc, dv_acc,
    between,
):
    total = land.shape[1]
    steps = total // tile
    scale = HD**-0.5
    hs = range(heads)

    def lanes(h):
        return slice((first_head + h) * HD, (first_head + h + 1) * HD)

    @pl.loop(0, steps)
    def _(i):
        place = pl.ds(pl.multiple_of(i * tile, tile), tile)
        cos_t, sin_t = cos_ref[:, place], sin_ref[:, place]
        for h in hs:
            x = turn(land[0, place, lanes(h)].astype(F32).T, cos_t, sin_t) * scale
            q_t[h, :, place] = x.astype(BF)
            q_n[h, place, :] = x.T.astype(BF)
            x = turn(land[1, place, lanes(h)].astype(F32).T, cos_t, sin_t)
            k_t[h, :, place] = x.astype(BF)
            k_n[h, place, :] = x.T.astype(BF)
            v_t[h, :, place] = land[2, place, lanes(h)].astype(F32).T.astype(BF)
            g_t[h, :, place] = land[3, place, lanes(h)].astype(F32).T.astype(BF)
            dk_acc[h, place, :] = jnp.zeros((tile, HD), F32)
            dv_acc[h, place, :] = jnp.zeros((tile, HD), F32)

    def one_tile(i):
        qs = pl.ds(pl.multiple_of(i * tile, tile), tile)
        start = start_ref[:, qs]
        queries = [q_t[h, :, qs] for h in hs]
        queries_n = [q_n[h, qs, :] for h in hs]
        cots = [g_t[h, :, qs] for h in hs]
        cots_n = [land[3, qs, lanes(h)] for h in hs]
        key_at = lax.broadcasted_iota(jnp.int32, (tile, tile), 0)
        query_at = lax.broadcasted_iota(jnp.int32, (tile, tile), 1)

        def score(j, tops, diagonal):
            first = pl.multiple_of(j * tile, tile)
            allowed = key_at >= (start - first)
            if diagonal:
                allowed = allowed & (key_at <= query_at)
            result = []
            for h in hs:
                s = dot32(k_n[h, pl.ds(first, tile), :], queries[h])
                s = jnp.where(allowed, s, NEGATIVE)
                probs[h, pl.ds(first, tile), :] = s
                result.append(jnp.maximum(tops[h], jnp.max(s, axis=0, keepdims=True)))
            return tuple(result)

        tops = tuple(jnp.full((1, tile), NEGATIVE, F32) for _ in hs)
        tops = lax.fori_loop(0, i, lambda j, c: score(j, c, False), tops)
        tops = score(i, tops, True)

        def mix(j, carry):
            sums, mixed = carry
            ks = pl.ds(pl.multiple_of(j * tile, tile), tile)
            new_sums, new_mixed = [], []
            for h in hs:
                p = jnp.exp(probs[h, ks, :] - tops[h])
                probs[h, ks, :] = p
                new_sums.append(sums[h] + jnp.sum(p, axis=0, keepdims=True))
                new_mixed.append(mixed[h] + dot32(v_t[h, :, ks], p.astype(BF)))
            return tuple(new_sums), tuple(new_mixed)

        zeros = tuple(jnp.zeros((1, tile), F32) for _ in hs)
        wide_zeros = tuple(jnp.zeros((HD, tile), F32) for _ in hs)
        sums, mixed = lax.fori_loop(0, i + 1, mix, (zeros, wide_zeros))
        inverse = [1.0 / sums[h] for h in hs]
        mixed = [mixed[h] * inverse[h] for h in hs]
        delta = [jnp.sum(mixed[h] * cots[h].astype(F32), axis=0, keepdims=True) for h in hs]

        def back(j, carry):
            ks = pl.ds(pl.multiple_of(j * tile, tile), tile)
            result = []
            for h in hs:
                p = probs[h, ks, :] * inverse[h]
                dp = dot32(land[2, ks, lanes(h)], cots[h])
                ds = (p * (dp - delta[h])).astype(BF)
                dv_acc[h, ks, :] += dot32(p.astype(BF), cots_n[h])
                dk_acc[h, ks, :] += dot32(ds, queries_n[h])
                result.append(carry[h] + dot32(k_t[h, :, ks], ds))
            return tuple(result)

        dq = lax.fori_loop(0, i + 1, back, wide_zeros)
        cos_t, sin_t = cos_ref[:, qs], sin_ref[:, qs]
        for h in hs:
            out[i, 0, :, lanes(h)] = turn(dq[h] * scale, cos_t, -sin_t).T.astype(BF)
            out[i, 3, :, lanes(h)] = mixed[h].T.astype(BF)

    @pl.loop(0, steps)
    def _(i):
        one_tile(i)
        between(i)

    @pl.loop(0, steps)
    def _(i):
        place = pl.ds(pl.multiple_of(i * tile, tile), tile)
        cos_t, sin_t = cos_ref[:, place], sin_ref[:, place]
        for h in hs:
            out[i, 1, :, lanes(h)] = turn(dk_acc[h, place, :].T, cos_t, -sin_t).T.astype(BF)
            out[i, 2, :, lanes(h)] = dv_acc[h, place, :].astype(BF)


def back_kernel(
    arrays, scatter, split, heads, tokens, land_ref, cos_ref, sin_ref, start_ref, g_ref, normed_ref, wq_ref, wo_ref,
    branch_ff, branch_y, d_hidden_ref, wu_ref, *refs,
):
    x, z, t = lax.axis_index("dp"), lax.axis_index("blk"), lax.axis_index("tensor")
    refs = list(refs)

    def take_refs(n):
        taken = refs[:n]
        del refs[:n]
        return taken

    own = take_refs(1)
    (home,) = take_refs(1)
    outs, landed, crossed = take_refs(4), take_refs(4), take_refs(4)
    up_part, dnorm_ff = take_refs(2)
    home_x, branch_y2, dnorm_y, sum_ff, over_x_ff, cross_ff = take_refs(6) if scatter else [None] * 6
    shares_o = take_refs(2) if scatter else []
    out, dwo, dwq, load_sems, home_sems, home_keep, stage_sems = take_refs(7)
    give, take, take_y, tile_sems, scatter_sems, cross_sems = take_refs(6) if scatter else [None] * 6
    nz, _, _, att = out.shape
    total = nz * tokens
    many, features = normed_ref.shape
    half, width = many // 2, features // 4
    rows = nz // 2
    groups = att // (heads * HD)
    peers = {"x": {"dp": 1 - x}, "y": {"tensor": flip(t, 2)}, "c": {"tensor": flip(t, 1)}}
    greet([{"blk": flip(z, m)} for m in range(1, nz)] + (list(peers.values()) if scatter else [peers["x"]]))
    work = Chain(arrays, own + [up_part, dwo, dwq], outs, landed, crossed, refs)
    work.begin()

    def remote(which, stage, src, dst, to):
        return pltpu.make_async_remote_copy(
            src, dst, scatter_sems.at[0, which, stage], scatter_sems.at[1, which, stage],
            device_id=peers[to], device_id_type=MESH,
        )

    def branch_over_y():
        return remote(0, 0, branch_ff.at[1 - t // 2, pl.ds(half, half)], branch_y2, "y")

    def dnorm_over_y():
        return remote(1, 0, dnorm_ff.at[1 - t // 2], dnorm_y, "y")

    def ff_x(which):
        return remote(which, 1, sum_ff.at[which, pl.ds((1 - x) * half, half)], over_x_ff.at[which], "x")

    def add_ff(which):
        (dnorm_over_y if which else branch_over_y)().wait_recv()
        ours = (branch_ff, dnorm_ff)[which]
        size = half // 4

        def at(k):
            return pl.ds(k * size, size)

        def tile(i, k):
            n = 2 * i + k % 2
            return give.at[n // 4, at(n % 4)]

        def theirs(k):
            if which == 1:
                return dnorm_y.at[at(k)]
            return branch_y.at[at(k)] if k < 4 else branch_y2.at[at(k - 4)]

        def fetch(k):
            return [
                pltpu.make_async_copy(ours.at[t // 2, at(k)], tile(0, k), tile_sems.at[0, k % 2]),
                pltpu.make_async_copy(theirs(k), tile(1, k), tile_sems.at[1, k % 2]),
            ]

        def keep(k):
            return pltpu.make_async_copy(tile(2, k), sum_ff.at[which, at(k)], tile_sems.at[2, k % 2])

        blocks = many // size
        for copy in fetch(0):
            copy.start()
        for k in range(blocks):
            if k + 1 < blocks:
                for copy in fetch(k + 1):
                    copy.start()
            for copy in fetch(k):
                copy.wait()
            if k >= 2:
                keep(k - 2).wait()
            add_rows(tile(2, k), tile(0, k), tile(1, k))
            keep(k).start()
        for k in range(blocks - 2, blocks):
            keep(k).wait()
        ff_x(which).start()

    tn_dims = (((0,), (0,)), ((), ()))
    nt_dims = (((1,), (1,)), ((), ()))
    general = functools.partial(lax.dot_general, preferred_element_type=F32)
    at_step = [0]

    def step():
        work.step(at_step[0])
        at_step[0] += 1

    def spread(d_hidden, weight, normed, stage):
        ff = d_hidden.shape[1]
        part = features // 2
        wide = pl.ds(pl.multiple_of(x * ff, 128), ff)
        loads = [
            pltpu.make_async_copy(d_hidden_ref, d_hidden, load_sems.at[0, 0]),
            pltpu.make_async_copy(wu_ref.at[:, wide] if split else wu_ref, weight, load_sems.at[0, 1]),
        ] + [
            pltpu.make_async_copy(normed_ref.at[:, pl.ds(k * part, part)], normed.at[k], load_sems.at[1, k]) for k in range(2)
        ]
        for copy in loads:
            copy.start()
        loads[0].wait()
        loads[1].wait()

        def value(at, columns):
            return general(d_hidden[at, :], weight[columns, :], nt_dims)

        if scatter:
            core_share(cross_ff, stage, cross_sems, stage_sems, tokens, t, value, dnorm_ff)
            dnorm_over_y().start()
            add_ff(0)
        else:
            for r in range(nz):
                at = pl.ds(r * tokens, tokens)
                for columns in range(0, features, 512):
                    stage[0, :, columns : columns + 512] = value(at, pl.ds(columns, 512)).astype(BF)
                copy = pltpu.make_async_copy(stage.at[0], dnorm_ff.at[at], stage_sems.at[0])
                copy.start()
                copy.wait()
        step()

        def keep(k, i):
            rows = pl.ds(pl.multiple_of(k * part + i * 256, 256), 256)
            return pltpu.make_async_copy(
                stage.at[i % 2, pl.ds(0, 256), pl.ds(0, ff)], up_part.at[rows], stage_sems.at[i % 2]
            )

        for k in range(2):
            loads[2 + k].wait()

            @pl.loop(0, part // 256)
            def _(i, k=k):
                @pl.when(i >= 2)
                def _():
                    keep(k, i - 2).wait()

                f = pl.ds(pl.multiple_of(i * 256, 256), 256)
                stage[i % 2, :256, :ff] = general(normed[k, :, f], d_hidden[...], tn_dims).astype(BF)
                keep(k, i).start()

            for i in range(part // 256 - 2, part // 256):
                keep(k, i).wait()
            if k == 0:
                step()

    if scatter:
        branch_over_y().start()
    pl.run_scoped(
        spread,
        pltpu.VMEM(d_hidden_ref.shape, BF),
        pltpu.VMEM((features, d_hidden_ref.shape[1]), BF),
        pltpu.VMEM((2, many, features // 2), BF),
        pltpu.VMEM((2, tokens, features), BF),
    )

    def lanes(p):
        return pl.ds(p * heads * HD, heads * HD)

    def home_copy(p, m, src, dst):
        return pltpu.make_async_remote_copy(
            src, dst, home_sems.at[0, p, m], home_sems.at[1, p, m], device_id={"blk": flip(z, m)}, device_id_type=MESH
        )

    def go_home(p, m):
        src = out.at[flip(z, m), :, :, lanes(p)]
        dst = home.at[:, z, :, lanes(p)]
        if m == 0:
            return pltpu.make_async_copy(src, dst, home_keep.at[p])
        return home_copy(p, m, src, dst)

    def arrive_home(p, m):
        ref = home.at[:, flip(z, m), :, lanes(p)]
        return home_copy(p, m, ref, ref)

    def attend(land, *scratch):
        load = pltpu.make_async_copy(land_ref, land, load_sems.at[0, 0])
        load.start()
        load.wait()
        for p in range(groups):
            plan = SCHEDULE[p] if p < len(SCHEDULE) else ()
            first = at_step[0]
            at_step[0] += sum(plan)

            def between(i, plan=plan, first=first):
                at = first
                for tile, steps in enumerate(plan):
                    if steps:

                        @pl.when(i == tile)
                        def _(at=at, steps=steps):
                            for c in range(at, at + steps):
                                work.step(c)

                    at += steps

            attention_heads(p * heads, heads, tokens, land, cos_ref, sin_ref, start_ref, out, *scratch, between)
            for m in (2, 3, 1, 0):
                go_home(p, m).start()
            if p == 0 and scatter:
                add_ff(1)

    pl.run_scoped(
        attend,
        pltpu.VMEM((4, total, att), BF),
        *[pltpu.VMEM((heads, HD, total), BF)] * 4,
        *[pltpu.VMEM((heads, total, HD), BF)] * 2,
        pltpu.VMEM((heads, total, tokens), F32),
        *[pltpu.VMEM((heads, total, HD), F32)] * 2,
    )
    def share_home(p):
        src, dst = home.at[:, pl.ds((1 - x) * rows, rows), :, lanes(p)], home_x.at[:, :, :, lanes(p)]
        return remote(p, 2, src, dst, "x")

    def come_home(p):
        for m in range(nz):
            if m == 0:
                go_home(p, m).wait()
            else:
                go_home(p, m).wait_send()
                arrive_home(p, m).wait_recv()
        if scatter:
            share_home(p).start()

    while at_step[0] < max(BEFORE) + 1:
        for which in BEFORE.get(at_step[0], ()):
            if which < groups:
                come_home(which)
        step()

    def over_core(which):
        return remote(which, 3, give, take.at[which], "c")

    def over_y(which):
        return remote(which, 4, take.at[which, 1 - t // 2], take_y.at[which], "y")

    def project(stream, hcat, hx, wcat, wo):
        def piece(i, r):
            at = pl.ds(r * tokens, tokens)
            return hcat.at[at, pl.ds(i * att, att)] if split else hcat.at[i, at]

        loads = [
            pltpu.make_async_copy(home.at[i, r], piece(i, r), load_sems.at[i, r])
            for i in (3, 0, 1, 2)
            for r in range(nz)
        ]
        weights = [] if not scatter else [
            pltpu.make_async_copy(
                wq_ref.at[i, :, pl.ds(pl.multiple_of(side * att, 128), att)],
                wcat.at[s, :, pl.ds(i * att, att)],
                load_sems.at[4 + s, i],
            )
            for s, side in enumerate((x, 1 - x))
            for i in range(3)
        ] + [
            pltpu.make_async_copy(wo_ref.at[pl.ds(side * att, att)], wo.at[s], load_sems.at[4 + s, 3])
            for s, side in enumerate((x, 1 - x))
        ]
        part = features // 2

        def streamed(k):
            source = g_ref if k < 2 else normed_ref
            return pltpu.make_async_copy(source.at[:, pl.ds((k % 2) * part, part)], stream.at[k % 2], load_sems.at[6, k % 2])

        for copy in loads[:4] + [streamed(0), streamed(1)] + loads[4:] + (weights if scatter else []):
            copy.start()
        step()
        for copy in loads:
            copy.wait()
        if split:
            attended = hcat[:, 3 * att :]
        else:
            d_qkv, attended = jnp.concatenate([hcat[i] for i in range(3)], axis=1), hcat[3]
        for k in range(2):
            streamed(k).wait()
            for j in range(part // width):
                value = general(attended, stream[k, :, j * width : (j + 1) * width], tn_dims)
                dwo[pl.ds((k * (part // width) + j) * att, att), :] = value.astype(BF)
            streamed(k + 2).start()
        for k in range(2):
            step()
            streamed(k + 2).wait()

            @pl.loop(0, part // 256)
            def _(j, k=k):
                f = pl.ds(pl.multiple_of(j * 256, 256), 256)
                value = general(stream[k, :, f], hcat[:, : 3 * att] if split else d_qkv, tn_dims).astype(BF)
                for i in range(3):
                    at = pl.multiple_of(i * features + k * part + j * 256, 256)
                    dwq[pl.ds(at, 256), :] = value[:, i * att : (i + 1) * att]

        if not scatter:
            return
        others = [
            pltpu.make_async_copy(
                home_x.at[i, r], hx.at[pl.ds(r * tokens, tokens), pl.ds(i * att, att)], load_sems.at[i, r]
            )
            for i in range(4)
            for r in range(rows)
        ]
        for p in range(groups):
            share_home(p).wait_recv()
        for copy in others:
            copy.start()
        for copy in weights + others:
            copy.wait()

        def share(which, of_core, target, plus):
            @pl.loop(0, 2 * rows)
            def _(k):
                v = k // rows
                columns = pl.ds(pl.multiple_of((2 * v + of_core) * width, width), width)
                at = pl.ds(pl.multiple_of((k % rows) * tokens, tokens), tokens)
                mine = pl.ds(pl.multiple_of(x * half + (k % rows) * tokens, tokens), tokens)
                if which == 0:
                    value = dot32(hcat[mine, 3 * att :], wo[0, :, columns]) + dot32(hx[at, 3 * att :], wo[1, :, columns])
                else:
                    value = general(hcat[mine, : 3 * att], wcat[0, columns, :], nt_dims)
                    value = value + general(hx[at, : 3 * att], wcat[1, columns, :], nt_dims)
                if plus:
                    value = value + target[v, at, :].astype(F32)
                target[v, at, :] = value.astype(BF)

        core = t % 2
        share(0, 1 - core, give, False)
        over_core(0).start()
        step()
        over_core(0).wait_send()
        share(1, 1 - core, give, False)
        over_core(1).start()
        step()
        for which in range(2):
            over_core(which).wait_recv()
            share(which, core, take.at[which], True)
            over_y(which).start()
            step()

    pl.run_scoped(
        project,
        pltpu.VMEM((2, many, features // 2), BF),
        pltpu.VMEM((many, 4 * att) if split else (4, many, att), BF),
        pltpu.VMEM((half, 4 * att), BF),
        pltpu.VMEM((2, features, 3 * att), BF),
        pltpu.VMEM((2, att, features), BF),
    )

    def total_share(which):
        if which == 0:
            over_core(1).wait_send()
        ff_x(which).wait_recv()
        loads = [
            pltpu.make_async_copy(sum_ff.at[which, pl.ds(x * half, half)], give.at[0], tile_sems.at[0, 0]),
            pltpu.make_async_copy(over_x_ff.at[which], give.at[1], tile_sems.at[0, 1]),
        ]
        for copy in loads:
            copy.start()
        for copy in loads:
            copy.wait()
        over_y(which).wait_recv()

        @pl.loop(0, half // 256)
        def _(i):
            at = pl.ds(pl.multiple_of(i * 256, 256), 256)
            ff = give[0, at, :].astype(F32) + give[1, at, :].astype(F32)
            heads_sum = take[which, t // 2, at, :].astype(F32) + take_y[which, at, :].astype(F32)
            shares_o[which][at, :] = ff + heads_sum

    later = dict(LATER) if scatter else {}
    while at_step[0] < work.steps:
        for which in later.pop(at_step[0], ()):
            total_share(which)
        step()
    assert not later
    work.finish()
    if scatter:
        for which in range(2):
            ff_x(which).wait_send()
            over_y(which).wait_send()
        branch_over_y().wait_send()
        dnorm_over_y().wait_send()
        for p in range(groups):
            share_home(p).wait_send()


def back(
    scatter, split, tokens, land, cos_t, sin_t, start, cotangent, normed, wq, wo, branch_ff, branch_y, d_hidden, wu, down
):
    _, total, att = land.shape
    nz = total // tokens
    many, features = normed.shape
    width, half = features // 4, many // 2
    heads = min(2, att // HD)
    groups = att // (heads * HD)
    ff = d_hidden.shape[1]
    arrays = [
        (*down.shape, 1024, True), (features, ff, 1024, True), (4 * att, width, 1024, False), (3 * features, att, 512, False),
    ]
    shapes = [a[:2] for a in arrays]
    hbm = pl.BlockSpec(memory_space=pl.ANY)
    vmem = pl.BlockSpec(memory_space=pltpu.VMEM)
    dma = pltpu.SemaphoreType.DMA
    scatter_scratch = [
        pltpu.VMEM((2, half, width), BF),
        pltpu.VMEM((2, 2, half, width), BF),
        pltpu.VMEM((2, half, width), BF),
        dma((3, 2)),
        dma((2, 2, 5)),
        dma((2, 2 * many // tokens)),
    ]
    scatter_outs = [
        jax.ShapeDtypeStruct((4, nz // 2, tokens, att), BF),
        jax.ShapeDtypeStruct((half, width), BF),
        jax.ShapeDtypeStruct((many, width), BF),
        jax.ShapeDtypeStruct((2, many, width), BF),
        jax.ShapeDtypeStruct((2, half, width), BF),
        jax.ShapeDtypeStruct((2, many, width), BF),
        jax.ShapeDtypeStruct((half, width), F32),
        jax.ShapeDtypeStruct((half, width), F32),
    ]
    results = pl.pallas_call(
        functools.partial(back_kernel, arrays, scatter, split, heads, tokens),
        out_shape=[jax.ShapeDtypeStruct((4, nz, tokens, att), BF)]
        + [jax.ShapeDtypeStruct((2,) + s, BF) for s in shapes]
        + [jax.ShapeDtypeStruct(s, BF) for s in shapes] * 2
        + [jax.ShapeDtypeStruct((features, ff), BF)]
        + [jax.ShapeDtypeStruct((2, many, width) if scatter else (many, features), BF)]
        + (scatter_outs if scatter else []),
        in_specs=[hbm] + [vmem] * 3 + [hbm] * 9,
        out_specs=[hbm] * 15 + ([hbm] * 6 + [vmem] * 2 if scatter else []),
        scratch_shapes=[
            pltpu.VMEM((nz, 4, tokens, att), BF),
            pltpu.VMEM(shapes[2], BF),
            pltpu.VMEM(shapes[3], BF),
            dma((7, 4)),
            dma((2, groups, nz)),
            dma((groups,)),
            dma((4,)),
        ]
        + (scatter_scratch if scatter else [])
        + Chain.scratch(arrays),
        compiler_params=pltpu.CompilerParams(collective_id=3, has_side_effects=True, vmem_limit_bytes=60 << 20),
        cost_estimate=pl.CostEstimate(
            flops=12 * (att // HD) * total * total * HD * 4, bytes_accessed=1 << 29, transcendentals=0
        ),
        name="back",
    )(land, cos_t, sin_t, start, cotangent, normed, wq, wo, branch_ff, branch_y, d_hidden, wu, down)
    return results[0], results[1:5], results[14], results[21:]


def widen(source, out_shape, block, in_map, out_map, grid):
    def body(source_ref, out_ref):
        out_ref[...] = source_ref[0].astype(F32)

    return pl.pallas_call(
        body,
        out_shape=jax.ShapeDtypeStruct(out_shape, F32),
        grid=grid,
        in_specs=[pl.BlockSpec((1,) + block, in_map)],
        out_specs=pl.BlockSpec(block, out_map),
        compiler_params=pltpu.CompilerParams(vmem_limit_bytes=32 << 20),
        cost_estimate=pl.CostEstimate(flops=0, bytes_accessed=source.size * 6, transcendentals=0),
        name="widen",
    )(source)


def widen_rows(source):
    _, rows, columns = source.shape
    size = min(rows, (1 << 18) // columns)
    steps = rows // size
    return widen(
        source, (2 * rows, columns), (size, columns), lambda i, h: (h, i, 0), lambda i, h: (h * steps + i, 0), (steps, 2)
    )


def widen_columns(source):
    _, rows, columns = source.shape
    if columns % 128:
        return jnp.concatenate([source[0], source[1]], axis=1).astype(F32)
    size = min(rows, (1 << 18) // columns)
    return widen(
        source, (rows, 2 * columns), (size, columns), lambda i, h: (h, i, 0), lambda i, h: (i, h), (rows // size, 2)
    )


def widen_blocks(source):
    _, rows, columns = source.shape
    rows = rows // 4
    return widen(
        source, (2 * rows, 4 * columns), (rows, columns), lambda h, j: (h, j, 0), lambda h, j: (h, j), (2, 4)
    )


def scatter_sum(share):
    whole = lax.psum_scatter(share.astype(BF), "dp", scatter_dimension=0, tiled=True)
    return lax.psum_scatter(whole, "tensor", scatter_dimension=2, tiled=True).astype(F32)


def butterfly(value, axes):
    for axis, size in axes:
        mask = 1
        while mask < size:
            value = value + swap(value, axis, size, mask)
            mask *= 2
    return value


SCHEDULE = ((0, 1, 1, 1), (0, 0, 1, 1))
BEFORE = {8: [0], 10: [1]}
LATER = {24: [0], 26: [1]}


def local(
    nx, nz, nt, block_input, segment_ids, layer_norm_gain, layer_norm_bias, qkv_weight, qkv_bias, out_weight, out_bias,
    up_weight, up_bias, down_weight, down_bias, grad_output,
):
    rows, tokens, width = block_input.shape
    all_rows = nx * rows
    features = nt * width
    many = all_rows * tokens
    x, z, t = lax.axis_index("dp"), lax.axis_index("blk"), lax.axis_index("tensor")
    att = qkv_weight.shape[2] // nx
    ff = up_weight.shape[1] // nx

    split = att % 128 == 0
    gather = nt == 4 and nx == 2 and split
    qkv_whole = jnp.transpose(qkv_weight, (1, 0, 2))
    qkv_half = lax.dynamic_slice_in_dim(qkv_whole, x * att, att, 2)
    qkv_half_bias = lax.dynamic_slice_in_dim(qkv_bias, x * att, att, 1)
    out_half = lax.dynamic_slice_in_dim(out_weight, x * att, att, 0)
    up_half_bias = lax.dynamic_slice_in_dim(up_bias, x * ff, ff, 0)
    if split:
        weights = [qkv_whole, out_weight, up_weight, down_weight]
    else:
        up_half = lax.dynamic_slice_in_dim(up_weight, x * ff, ff, 1)
        down_half = lax.dynamic_slice_in_dim(down_weight, x * ff, ff, 0)
        weights = [qkv_half, out_half, up_half, down_half]

    segments = lax.ppermute(segment_ids, "dp", [(0, 1), (1, 0)])
    segments = jnp.where(z // rows == x, segment_ids, segments)
    segments = lax.dynamic_slice_in_dim(segments, z % rows, 1, 0)
    length = segments.shape[1]
    places = jnp.arange(length, dtype=jnp.int32)[None]
    changed = jnp.concatenate(
        [jnp.ones((1, 1), dtype=bool), segments[:, 1:] != segments[:, :-1]], axis=1
    )
    start = lax.cummax(jnp.where(changed, places, 0), axis=1)
    half_rot = ROT // 2
    frequency = jnp.exp(jnp.arange(half_rot).astype(F32) * (-2.0 / ROT) * ROPE_LOG_BASE)
    angles = frequency[:, None] * (places - start).astype(F32)
    cos_t, sin_t = jnp.cos(angles), jnp.sin(angles)

    if gather:
        sources = [block_input.reshape(rows * tokens, width), grad_output.reshape(rows * tokens, width)]
    else:
        sources = [lax.all_gather(a, "tensor", axis=2, tiled=True) for a in (block_input, grad_output)]
        sources = [lax.all_gather(a, "dp", axis=0, tiled=True).reshape(many, features) for a in sources]
    normed, cotangent, land, stats, down_part, d_hidden, branch_ff, up_bias_part, branch_y = front(
        gather, split, rows, tokens, nz, many, features, att, ff,
        [
            *sources, layer_norm_gain.reshape(1, features), layer_norm_bias.reshape(1, features), weights[0],
            qkv_half_bias.reshape(3, 1, att), weights[1], weights[2], up_half_bias.reshape(1, ff), weights[3],
        ],
    )
    home, sums, d_normed_ff, shares = back(
        gather, split, tokens, land, cos_t, sin_t, start, cotangent, normed, weights[0], weights[1], branch_ff, branch_y,
        d_hidden, weights[2], down_part,
    )
    down_sum, up_sum, out_sum, qkv_sum = sums
    home = home.reshape(4, many, att)
    qkv_bias_part = jnp.sum(home[:3].astype(F32), axis=1)
    up_bias_part = up_bias_part[0]
    if gather:
        branch, d_normed = (share.reshape(rows, tokens, width) for share in shares)
    else:
        branch = branch_ff.astype(F32) + dot32(home[3], out_half)
        d_normed = d_normed_ff.astype(F32)
        for i in range(3):
            d_normed = d_normed + dot32(home[i], qkv_half[i].T)
        branch = scatter_sum(branch.reshape(all_rows, tokens, features))
        d_normed = scatter_sum(d_normed.reshape(all_rows, tokens, features))

    block_output = (block_input.astype(F32) + (branch + out_bias + down_bias)).astype(BF)

    gain = lax.dynamic_slice_in_dim(layer_norm_gain, t * width, width, 0)
    stats = lax.dynamic_slice_in_dim(stats, x * rows * tokens, rows * tokens, 0).reshape(rows, tokens, 128)
    own_mean, own_inverse = stats[..., :1], stats[..., 64:65]
    xhat = (block_input.astype(F32) - own_mean) * own_inverse
    scaled = d_normed * gain
    moments = jnp.stack([jnp.sum(scaled, axis=-1), jnp.sum(scaled * xhat, axis=-1)])
    moments = butterfly(moments, [("tensor", nt)]) / features
    first, second = moments[0][..., None], moments[1][..., None]
    input_grad = (
        grad_output.astype(F32) + own_inverse * (scaled - first - xhat * second)
    ).astype(BF)

    def spread(part, whole):
        shape = part.shape[:-1] + (whole,)
        at = (0,) * (part.ndim - 1) + (x * part.shape[-1],)
        return lax.dynamic_update_slice(jnp.zeros(shape, F32), part, at)

    small = [
        jnp.sum(d_normed * xhat, axis=(0, 1)),
        jnp.sum(d_normed, axis=(0, 1)),
        jnp.sum(grad_output.astype(F32), axis=(0, 1)),
        spread(up_bias_part, nx * ff),
        spread(qkv_bias_part, nx * att).reshape(-1),
    ]
    packed = butterfly(jnp.concatenate(small), [("dp", nx), ("blk", nz)])
    gain_grad, shift_grad, bias_grad = (packed[i * width : (i + 1) * width] for i in range(3))
    up_bias_grad = packed[3 * width : 3 * width + nx * ff]
    qkv_bias_grad = packed[3 * width + nx * ff :].reshape(3, nx * att)

    down_grad = widen_rows(down_sum)
    up_grad = widen_columns(up_sum)
    out_grad = widen_blocks(out_sum)
    qkv_grad = widen_columns(qkv_sum).reshape(3, features, nx * att)
    qkv_grad = jnp.transpose(qkv_grad, (1, 0, 2))
    return (
        block_output, input_grad, gain_grad, shift_grad, qkv_grad, qkv_bias_grad, out_grad, bias_grad, up_grad,
        up_bias_grad, down_grad, bias_grad,
    )


def solution(mesh):
    in_specs = (
        P("dp", "blk", "tensor"), P("dp", None), P(), P(), P(None, None, "tensor"), P(None, "tensor"), P("tensor", None),
        P("tensor"), P(None, "tensor"), P("tensor"), P("tensor", None), P("tensor"), P("dp", "blk", "tensor"),
    )
    out_specs = (
        P("dp", "blk", "tensor"), P("dp", "blk", "tensor"), P("tensor"), P("tensor"), P(None, None, "tensor"),
        P(None, "tensor"), P("tensor", None), P("tensor"), P(None, "tensor"), P("tensor"), P("tensor", None), P("tensor"),
    )
    body = functools.partial(local, mesh.shape["dp"], mesh.shape["blk"], mesh.shape["tensor"])
    return jax.shard_map(body, mesh=mesh, in_specs=in_specs, out_specs=out_specs, check_vma=False)
```

```python
import functools
import math

import jax
import jax.numpy as jnp
import numpy as np
from jax import lax
from jax.experimental import pallas as pl
from jax.experimental.pallas import tpu as pltpu
from jax.sharding import PartitionSpec as P

HD = 64
ROT = 32
EPSILON = 1e-05
ROPE_LOG_BASE = math.log(10000.0)
NEGATIVE = -1e30
F32 = jnp.float32
BF = jnp.bfloat16
MESH = pl.DeviceIdType.MESH
dot32 = functools.partial(jnp.dot, preferred_element_type=F32)


def swap(value, axis, size, mask):
    return lax.ppermute(value, axis, [(i, i ^ mask) for i in range(size)])


def flip(index, mask):
    if mask == 0:
        return index
    if mask == 1:
        return index + 1 - 2 * (index % 2)
    if mask == 2:
        return (index + 2) % 4
    return 3 - index


def core_share(cross_ref, stage, cross_sems, stage_sems, tokens, t, value, out, between=None):
    _, many, width = out.shape
    blocks = many // tokens
    core = t % 2

    def place(k):
        return pl.ds(pl.multiple_of((k % blocks) * tokens, tokens), tokens)

    def tile(slot, k):
        return stage.at[k % 2, :, pl.ds(slot * width, width)]

    def at(ref, k):
        return ref.at[k // blocks, place(k)]

    def columns(k, of_core):
        return pl.ds(pl.multiple_of((2 * (k // blocks) + of_core) * width, width), width)

    def cross(k, src, dst):
        return pltpu.make_async_remote_copy(
            src, dst, cross_sems.at[0, k], cross_sems.at[1, k], device_id={"tensor": flip(t, 1)}, device_id_type=MESH
        )

    def give(k):
        return cross(k, tile(0, k), at(cross_ref, k))

    def got(k):
        return cross(k, at(cross_ref, k), at(cross_ref, k))

    def fetch(k):
        return pltpu.make_async_copy(at(cross_ref, k), tile(1, k), stage_sems.at[k % 2])

    def keep(k):
        return pltpu.make_async_copy(tile(2, k), at(out, k), stage_sems.at[2 + k % 2])

    @pl.loop(0, 2 * blocks)
    def _(k):
        @pl.when(k >= 2)
        def _():
            give(k - 2).wait_send()

        stage[k % 2, :, :width] = value(place(k), columns(k, 1 - core)).astype(BF)
        give(k).start()

    for k in (2 * blocks - 2, 2 * blocks - 1):
        give(k).wait_send()
    if between:
        between()
    got(0).wait_recv()
    fetch(0).start()

    @pl.loop(0, 2 * blocks)
    def _(k):
        @pl.when(k >= 2)
        def _():
            keep(k - 2).wait()

        @pl.when(k + 1 < 2 * blocks)
        def _():
            got(k + 1).wait_recv()
            fetch(k + 1).start()

        mine = value(place(k), columns(k, core))
        fetch(k).wait()
        stage[k % 2, :, 2 * width : 3 * width] = (mine + stage[k % 2, :, width : 2 * width].astype(F32)).astype(BF)
        keep(k).start()

    for k in (2 * blocks - 2, 2 * blocks - 1):
        keep(k).wait()


def front_kernel(
    gather, split, rows, tokens, segments_ref, frequency_ref, x_own, g_own, gain_ref, shift_ref, wq_ref, bq_ref, wo_ref, wu_ref, bu_ref, wd_ref,
    normed_o, g_o, land_o, stats_o, down_o, d_hidden_o, branch_o, ubias_o, cos_o, sin_o, start_o, branch_y_o, cross_o,
    xin, gin, vq, vo, vu, vd, pay, act, slope, stage, gather_sems, land_sems, load_sems, keep_sems, stage_sems, cross_sems, over_y_sems, segments, segment_sems,
):
    x, z, t = lax.axis_index("dp"), lax.axis_index("blk"), lax.axis_index("tensor")
    many, features = xin.shape
    half = rows * tokens
    width = features // 4
    att = vq.shape[2]
    ff = vu.shape[1]
    nz = pay.shape[0]
    wide = min(512, ff)

    def remote(src, dst, sems, device):
        return pltpu.make_async_remote_copy(
            src, dst, sems[0], sems[1], device_id=device, device_id_type=MESH
        )

    peers = {"x": {"dp": 1 - x}, "y": {"tensor": flip(t, 2)}, "c": {"tensor": flip(t, 1)}}
    barrier = pltpu.get_barrier_semaphore()
    greet = [{"blk": flip(z, m)} for m in range(1, nz)] + (list(peers.values()) if gather else [peers["x"]])
    for device in greet:
        pl.semaphore_signal(barrier, inc=1, device_id=device, device_id_type=MESH)

    loads = [
        pltpu.make_async_copy(
            wq_ref.at[:, :, pl.ds(pl.multiple_of(x * att, 128), att)] if split else wq_ref, vq, load_sems.at[0]
        ),
        pltpu.make_async_copy(
            wu_ref.at[:, pl.ds(pl.multiple_of(x * ff, 128), ff)] if split else wu_ref, vu, load_sems.at[1]
        ),
        pltpu.make_async_copy(wd_ref.at[pl.ds(x * ff, ff)] if split else wd_ref, vd, load_sems.at[2]),
        pltpu.make_async_copy(wo_ref.at[pl.ds(x * att, att)] if split else wo_ref, vo, load_sems.at[3]),
    ]
    if not gather:
        both = [
            pltpu.make_async_copy(x_own, xin, load_sems.at[4]),
            pltpu.make_async_copy(g_own, gin, load_sems.at[5]),
        ]
    else:
        both = [
            pltpu.make_async_copy(
                own,
                buf.at[pl.ds(x * half, half), pl.ds(pl.multiple_of(t * width, 128), width)],
                load_sems.at[4 + i],
            )
            for i, (own, buf) in enumerate([(x_own, xin), (g_own, gin)])
        ]
    both[0].start()
    both[1].start()
    pl.semaphore_wait(barrier, len(greet))

    class Gather:
        def __init__(self, which, own, buf, first, size):
            self.which, self.own, self.buf, self.names = which, own, buf, []
            self.base, self.size = first, size

        def at(self, dx, dt, r):
            return self.buf.at[
                pl.ds(pl.multiple_of((1 - x if dx else x) * half + self.base + r * self.size, self.size), self.size),
                pl.ds(pl.multiple_of(flip(t, dt) * width, 128), width),
            ]

        plan = {
            "x": (0, 0, "x", 1, 0), "y": (0, 0, "y", 0, 2), "c": (0, 0, "c", 0, 1),
            "ex": (1, 0, "c", 1, 1), "ey": (0, 2, "c", 0, 3), "ed": (1, 2, "c", 1, 3),
        }

        def sems(self, kind, r):
            k = 2 * ("x", "y", "c", "d", "ex", "ey", "ed").index(kind) + r
            return gather_sems.at[self.which, 0, k], gather_sems.at[self.which, 1, k]

        def copy(self, kind, r):
            if kind == "d":
                dx, dt, to = (1, 0, "y") if r == 0 else (0, 2, "x")
            else:
                dx, dt, to = self.plan[kind][:3]
            src = dst = self.at(dx, dt, r)
            if kind in "xyc":
                src = self.own.at[pl.ds(self.base + r * self.size, self.size)]
            return remote(src, dst, self.sems(kind, r), peers[to])

        def start(self, kind, r):
            self.names.append((kind, r))
            self.copy(kind, r).start()

        def wait(self, kind, r):
            if kind == "d":
                dx, dt, to = 1, 2, "y"
            else:
                to, dx, dt = self.plan[kind][2:]
            ref = self.at(dx, dt, r)
            remote(ref, ref, self.sems(kind, r), peers[to]).wait_recv()

        def begin(self):
            for kind, r in (("x", 0), ("y", 1), ("x", 1), ("y", 0), ("c", 0), ("c", 1)):
                self.start(kind, r)

        def second(self):
            self.wait("x", 0)
            self.start("d", 0)
            self.start("ex", 0)
            self.wait("y", 1)
            self.start("d", 1)
            self.start("ey", 1)

        def third(self):
            self.wait("x", 1)
            self.start("ex", 1)
            self.wait("y", 0)
            self.start("ey", 0)

        def fourth(self):
            self.wait("d", 0)
            self.start("ed", 0)
            self.wait("d", 1)
            self.start("ed", 1)

        def last(self):
            for kind in ("c", "ex", "ey", "ed"):
                for r in range(2):
                    self.wait(kind, r)

        def drain(self):
            for kind, r in self.names:
                self.copy(kind, r).wait_send()

    ins = [Gather(r, x_own, xin, r * tokens, tokens // 2) for r in range(rows)]
    cots = Gather(rows, g_own, gin, 0, half // 2)
    own_segments = pltpu.make_async_copy(segments_ref, segments.at[x], segment_sems.at[0])
    own_segments.start()
    segments_x = remote(segments_ref, segments.at[x], (segment_sems.at[1], segment_sems.at[2]), peers["x"])
    segments_x.start()
    if gather:
        ins[0].begin()
    for load in loads:
        load.start()

    own_segments.wait()
    segments_x.wait()
    ids = segments[z // rows]
    length = ids.shape[1]
    ids = jnp.sum(jnp.where(lax.broadcasted_iota(jnp.int32, ids.shape, 0) == z % rows, ids, 0), axis=0, keepdims=True)
    ids = jnp.broadcast_to(ids, (8, length))
    at = lax.broadcasted_iota(jnp.int32, (8, length), 1)
    first_of = jnp.where(ids != pltpu.roll(ids, 1, 1), at, 0)
    reach = 1
    while reach < length:
        first_of = jnp.maximum(first_of, jnp.where(at >= reach, pltpu.roll(first_of, reach, 1), 0))
        reach *= 2
    start_o[...] = first_of
    angles = frequency_ref[...] * (at - first_of)[0:1].astype(F32)
    cos_o[...] = jnp.cos(angles)
    sin_o[...] = jnp.sin(angles)

    def place(position):
        return pl.ds(pl.multiple_of(position * tokens, tokens), tokens)

    def normalize(row):
        @pl.loop(0, tokens // 128)
        def _(i):
            at = pl.ds(pl.multiple_of(row * tokens + i * 128, 128), 128)
            v = xin[at, :].astype(F32)
            mean = jnp.sum(v, axis=-1, keepdims=True) * (1.0 / features)
            v = v - mean
            inverse = lax.rsqrt(jnp.sum(v * v, axis=-1, keepdims=True) * (1.0 / features) + EPSILON)
            xin[at, :] = (v * inverse * gain_ref[...] + shift_ref[...]).astype(BF)
            lane = lax.broadcasted_iota(jnp.int32, (128, 128), 1)
            stats_o[at, :] = jnp.where(lane < 64, mean, inverse)

    def parts(kind):
        return pl.ds(0, 3) if kind == 0 else pl.ds(3, 1)

    def sems(kind, m):
        return land_sems.at[0, kind, m], land_sems.at[1, kind, m]

    def own_row(kind):
        return pltpu.make_async_copy(
            pay.at[z, parts(kind)], land_o.at[parts(kind), place(z)], keep_sems.at[2 + kind]
        )

    def other_row(kind, row, m):
        return remote(pay.at[row, parts(kind)], land_o.at[parts(kind), place(z)], sems(kind, m), {"blk": row})

    def send(kind, row):
        @pl.when(z == row)
        def _():
            own_row(kind).start()

        @pl.when(z != row)
        def _():
            other_row(kind, row, flip(z, row)).start()

    def landed(kind, m):
        ref = land_o.at[parts(kind), place(flip(z, m))]
        return remote(ref, ref, sems(kind, m), {"blk": flip(z, m)})

    def project(row):
        @pl.loop(0, 3)
        def _(part):
            bias = bq_ref[part, :, pl.ds(pl.multiple_of(x * att, 128), att)] if split else bq_ref[part]
            value = dot32(xin[place(row), :], vq[part]) + bias
            pay[row, part] = value.astype(BF)

        send(0, row)

    if gather:
        ins[0].second()
        ins[0].third()
        ins[1].begin()
        ins[0].fourth()
    both[0].wait()
    for r in range(rows):
        if gather:
            ins[r].last()
            ins[r].drain()
        for row in range(r, nz, rows):
            normalize(row)
        if gather and r == 0:
            ins[1].second()
        if r == 0:
            loads[0].wait()
        for row in range(r, nz, rows):
            project(row)
        if gather and r == 0:
            ins[1].third()
            cots.begin()
            ins[1].fourth()
    keep_normed = pltpu.make_async_copy(xin, normed_o, keep_sems.at[0])
    keep_normed.start()
    if gather:
        cots.second()

    loads[1].wait()

    @pl.loop(0, many // tokens)
    def _(i):
        at = place(i)

        @pl.loop(0, ff // wide)
        def _(j):
            columns = pl.ds(pl.multiple_of(j * wide, wide), wide)
            first = x * ff if split else 0
            h = dot32(xin[at, :], vu[:, columns]) + bu_ref[:, pl.ds(pl.multiple_of(first + j * wide, wide), wide)]
            c = math.sqrt(2.0 / math.pi)
            square = h * h
            tanh = jnp.tanh(c * h * (1.0 + 0.044715 * square))
            one = 0.5 * (1.0 + tanh)
            act[at, columns] = (h * one).astype(BF)
            d = one + 0.5 * h * (1.0 - tanh * tanh) * (c * (1.0 + 3 * 0.044715 * square))
            slope[at, columns] = d.astype(BF)

    if gather:
        cots.third()
    nt_dims = (((1,), (1,)), ((), ()))
    tn_dims = (((0,), (0,)), ((), ()))
    general = functools.partial(lax.dot_general, preferred_element_type=F32)

    def through(steps, rows_of, columns_of, make, out):
        def copy(i):
            return pltpu.make_async_copy(
                stage.at[i % 2, pl.ds(0, rows_of), pl.ds(0, columns_of)],
                out.at[pl.ds(pl.multiple_of(i * rows_of, rows_of), rows_of)],
                stage_sems.at[i % 2],
            )

        @pl.loop(0, steps)
        def _(i):
            @pl.when(i >= 2)
            def _():
                copy(i - 2).wait()

            make(i, stage.at[i % 2, pl.ds(0, rows_of), pl.ds(0, columns_of)])
            copy(i).start()

        for i in range(max(0, steps - 2), steps):
            copy(i).wait()

    loads[2].wait()
    if gather:
        core_share(
            cross_o, stage, cross_sems, stage_sems, tokens, t,
            lambda at, columns: dot32(act[at, :], vd[:, columns]), branch_o,
        )
        branch_over_y = remote(
            branch_o.at[1 - t // 2, pl.ds(0, half)], branch_y_o, (over_y_sems.at[0], over_y_sems.at[1]), peers["y"]
        )
        branch_over_y.start()
    else:

        def whole(i, target):
            @pl.loop(0, features // 512)
            def _(j):
                columns = pl.ds(pl.multiple_of(j * 512, 512), 512)
                target[:, columns] = dot32(act[place(i), :], vd[:, columns]).astype(BF)

        through(many // tokens, tokens, features, whole, branch_o)

    if gather:
        cots.fourth()
    both[1].wait()
    if gather:
        cots.last()
    keep_g = pltpu.make_async_copy(gin, g_o, keep_sems.at[1])
    keep_g.start()

    loads[3].wait()
    for row in range(nz):
        pay[row, 3] = general(gin[place(row), :], vo[...], nt_dims).astype(BF)
        send(1, row)

    ubias_o[...] = jnp.zeros_like(ubias_o)

    @pl.loop(0, many // tokens)
    def _(i):
        at = place(i)

        @pl.loop(0, ff // wide)
        def _(j):
            columns = pl.ds(pl.multiple_of(j * wide, wide), wide)
            d = general(gin[at, :], vd[columns, :], nt_dims) * slope[at, columns].astype(F32)
            d = d.astype(BF)
            slope[at, columns] = d
            ubias_o[0:1, columns] += jnp.sum(d.astype(F32), axis=0, keepdims=True)

    keep_d = pltpu.make_async_copy(slope, d_hidden_o, keep_sems.at[4])
    keep_d.start()

    def down_tile(i, target):
        f = pl.ds(pl.multiple_of(i * 256, 256), 256)
        for j in range(0, features, 1024):
            target[:, j : j + 1024] = general(act[:, f], gin[:, j : j + 1024], tn_dims).astype(BF)

    through(ff // 256, 256, features, down_tile, down_o)

    keep_normed.wait()
    keep_g.wait()
    keep_d.wait()
    for kind in range(2):
        own_row(kind).wait()
        for m in range(1, nz):
            other_row(kind, flip(z, m), m).wait_send()
            landed(kind, m).wait_recv()
    if gather:
        cots.drain()
        branch_over_y.wait()


def front(gather, split, rows, tokens, nz, many, features, att, ff, operands):
    hbm = pl.BlockSpec(memory_space=pl.ANY)
    vmem = pl.BlockSpec(memory_space=pltpu.VMEM)
    shares = (2, many, features // 4) if gather else (many, features)
    return pl.pallas_call(
        functools.partial(front_kernel, gather, split, rows, tokens),
        out_shape=[
            jax.ShapeDtypeStruct((many, features), BF),
            jax.ShapeDtypeStruct((many, features), BF),
            jax.ShapeDtypeStruct((4, nz * tokens, att), BF),
            jax.ShapeDtypeStruct((many, 128), F32),
            jax.ShapeDtypeStruct((ff, features), BF),
            jax.ShapeDtypeStruct((many, ff), BF),
            jax.ShapeDtypeStruct(shares, BF),
            jax.ShapeDtypeStruct((8, ff), F32),
            jax.ShapeDtypeStruct((ROT // 2, nz * tokens), F32),
            jax.ShapeDtypeStruct((ROT // 2, nz * tokens), F32),
            jax.ShapeDtypeStruct((8, nz * tokens), jnp.int32),
            jax.ShapeDtypeStruct((many // 2, features // 4), BF),
            jax.ShapeDtypeStruct((2, many, features // 4), BF),
        ],
        in_specs=[hbm, vmem, hbm, hbm, vmem, vmem, hbm, vmem, hbm, hbm, vmem, hbm],
        out_specs=[hbm, hbm, hbm, vmem, hbm, hbm, hbm, vmem, vmem, vmem, vmem, hbm, hbm],
        scratch_shapes=[
            pltpu.VMEM((many, features), BF),
            pltpu.VMEM((many, features), BF),
            pltpu.VMEM((3, features, att), BF),
            pltpu.VMEM((att, features), BF),
            pltpu.VMEM((features, ff), BF),
            pltpu.VMEM((ff, features), BF),
            pltpu.VMEM((nz, 4, tokens, att), BF),
            pltpu.VMEM((many, ff), BF),
            pltpu.VMEM((many, ff), BF),
            pltpu.VMEM((2, tokens, features), BF),
            pltpu.SemaphoreType.DMA((rows + 1, 2, 14)),
            pltpu.SemaphoreType.DMA((2, 2, 4)),
            pltpu.SemaphoreType.DMA((6,)),
            pltpu.SemaphoreType.DMA((5,)),
            pltpu.SemaphoreType.DMA((4,)),
            pltpu.SemaphoreType.DMA((2, 2 * many // tokens)),
            pltpu.SemaphoreType.DMA((2,)),
            pltpu.VMEM((2, rows, nz * tokens), jnp.int32),
            pltpu.SemaphoreType.DMA((3,)),
        ],
        compiler_params=pltpu.CompilerParams(
            collective_id=2, has_side_effects=True, vmem_limit_bytes=60 << 20
        ),
        cost_estimate=pl.CostEstimate(
            flops=2 * many * features * (6 * ff + 4 * att), bytes_accessed=100 << 20, transcendentals=0
        ),
        name="front",
    )(*operands)[:12]


def add_rows(target, one, two):
    @pl.loop(0, target.shape[0], step=32)
    def _(r):
        at = pl.ds(pl.multiple_of(r, 32), 32)
        target[at] = (one[at].astype(F32) + two[at].astype(F32)).astype(BF)


class Chain:
    COLUMNS = 256
    SLOTS = {"own": 3, "in": 2, "cross": 2, "sum": 4, "total": 6}
    END_LAG = 5
    MID_LAG = 2
    INWARD = 2
    APART = 3
    ASIDE = 8

    @classmethod
    def layout(cls, arrays):
        chunks, rings = [], {}
        for a, (rows, columns, size, _) in enumerate(arrays):
            size, wide = math.gcd(rows, size), math.gcd(columns, cls.COLUMNS)
            rings[wide] = max(rings.get(wide, 0), size)
            chunks += [(a, r, size, c, wide) for r in range(0, rows, size) for c in range(0, columns, wide)]
        return chunks, rings

    @classmethod
    def scratch(cls, arrays):
        chunks, rings = cls.layout(arrays)
        return [pltpu.VMEM((k, rows, wide), BF) for wide, rows in rings.items() for k in cls.SLOTS.values()] + [
            pltpu.SemaphoreType.DMA((8, len(chunks))),
            pltpu.SemaphoreType.DMA((3, 3)),
            pltpu.SemaphoreType.DMA((len(chunks),)),
        ]

    def __init__(self, arrays, own, outs, landed, crossed, scratch):
        self.arrays, self.own, self.outs, self.landed, self.crossed = arrays, own, outs, landed, crossed
        self.chunks, rings = self.layout(arrays)
        scratch = list(scratch)
        self.rings = {wide: {name: scratch.pop(0) for name in self.SLOTS} for wide in rings}
        self.sems, self.load_sems, self.keep_sem = scratch
        self.n = len(self.chunks)
        self.x, self.z = lax.axis_index("dp"), lax.axis_index("blk")
        self.at_end = (self.z == 0) | (self.z == 3)
        self.inner = jnp.where(self.z == 0, 1, 2)
        self.outer = jnp.where(self.z == 1, 0, 3)

    def send(self, kind, c, src, dst, device):
        return pltpu.make_async_remote_copy(
            src, dst, self.sems.at[2 * kind, c], self.sems.at[2 * kind + 1, c],
            device_id=device, device_id_type=MESH,
        )

    def part(self, refs, c):
        a, r, rows, column, columns = self.chunks[c]
        return refs[a].at[pl.ds(r, rows), pl.ds(column, columns)]

    def final(self, c, half):
        a, r, rows, column, columns = self.chunks[c]
        return self.outs[a].at[half, pl.ds(r, rows), pl.ds(column, columns)]

    def slot(self, name, c):
        _, _, rows, _, columns = self.chunks[c]
        return self.rings[columns][name].at[c % self.SLOTS[name], pl.ds(0, rows)]

    def go_in(self, c):
        return self.send(0, c, self.part(self.own, c), self.part(self.landed, c), {"blk": self.inner})

    def arrive_in(self, c):
        ref = self.part(self.landed, c)
        return self.send(0, c, ref, ref, {"blk": self.outer})

    def go_mid(self, c):
        return self.send(1, c, self.slot("sum", c), self.part(self.crossed, c), {"blk": 3 - self.z})

    def go_out(self, c):
        return self.send(2, c, self.slot("total", c), self.final(c, self.x), {"blk": self.outer})

    def arrive_out(self, c):
        return self.send(2, c, self.final(c, self.x), self.final(c, self.x), {"blk": self.inner})

    def go_x(self, c, end):
        src = self.final(c, self.x) if end else self.slot("total", c)
        return self.send(3, c, src, self.final(c, self.x), {"dp": 1 - self.x})

    def arrive_x(self, c):
        ref = self.final(c, 1 - self.x)
        return self.send(3, c, ref, ref, {"dp": 1 - self.x})

    def load(self, name, refs, c):
        at = self.load_sems.at[list(self.SLOTS).index(name), c % self.SLOTS[name]]
        return pltpu.make_async_copy(self.part(refs, c), self.slot(name, c), at)

    def load_own(self, c):
        return self.load("own", self.own, c)

    def first_of(self, array):
        return [a for a, *_ in self.chunks].index(array)

    def in_hbm(self, c):
        return c < self.n and self.arrays[self.chunks[c][0]][3]

    def keep(self, c):
        return pltpu.make_async_copy(self.slot("total", c), self.final(c, self.x), self.keep_sem.at[c])

    @property
    def steps(self):
        return self.n + self.END_LAG

    def begin(self):
        @pl.when(self.at_end)
        def _():
            for c in range(min(self.INWARD, self.n)):
                self.go_in(c).start()

        @pl.when(jnp.logical_not(self.at_end))
        def _():
            for c in range(2):
                if self.in_hbm(c):
                    self.load_own(c).start()

    def sent(self, c):
        self.go_out(c).wait_send()
        if c < self.n - self.APART:
            self.go_x(c, False).wait_send()
        self.keep(c).wait()

    def step(self, c):
        n, slots = self.n, self.SLOTS

        @pl.when(self.at_end)
        def _():
            if c < n:
                self.go_in(c).wait_send()
                if c + self.INWARD < n:
                    self.go_in(c + self.INWARD).start()
            d = c - self.END_LAG
            if 0 <= d < n:
                self.arrive_out(d).wait_recv()
                if d >= self.ASIDE:
                    self.go_x(d - self.ASIDE, True).wait_send()
                if d < n - self.APART:
                    self.go_x(d, True).start()

        if c >= n + self.MID_LAG:
            return

        @pl.when(jnp.logical_not(self.at_end))
        def _():
            d = c - self.MID_LAG
            crossing = 0 <= d < n
            if c < n:
                if self.in_hbm(c + 2):
                    self.load_own(c + 2).start()
                self.arrive_in(c).wait_recv()
                self.load("in", self.landed, c).start()
            if crossing:
                self.go_mid(d).wait_recv()
                self.load("cross", self.crossed, d).start()
            if c < n:
                if self.in_hbm(c):
                    self.load_own(c).wait()
                    mine = self.slot("own", c)
                else:
                    mine = self.part(self.own, c)
                if c >= slots["sum"]:
                    self.go_mid(c - slots["sum"]).wait_send()
                self.load("in", self.landed, c).wait()
                add_rows(self.slot("sum", c), self.slot("in", c), mine)
                self.go_mid(c).start()
            if crossing:
                if d >= slots["total"]:
                    self.sent(d - slots["total"])
                self.load("cross", self.crossed, d).wait()
                add_rows(self.slot("total", d), self.slot("cross", d), self.slot("sum", d))
                self.go_out(d).start()
                if d < n - self.APART:
                    self.go_x(d, False).start()
                self.keep(d).start()

    def finish(self):
        n, slots = self.n, self.SLOTS

        @pl.when(self.at_end)
        def _():
            for c in range(max(0, n - self.ASIDE), n - self.APART):
                self.go_x(c, True).wait_send()

        @pl.when(jnp.logical_not(self.at_end))
        def _():
            for c in range(max(0, n - slots["sum"]), n):
                self.go_mid(c).wait_send()
            for c in range(max(0, n - slots["total"]), n):
                self.sent(c)

        for c in range(n - self.APART):
            self.arrive_x(c).wait_recv()


def greet(devices):
    barrier = pltpu.get_barrier_semaphore()
    for device in devices:
        pl.semaphore_signal(barrier, inc=1, device_id=device, device_id_type=MESH)
    pl.semaphore_wait(barrier, len(devices))


def turn(source, cos_t, sin_t):
    half = ROT // 2
    front_half, back_half = source[:half], source[half:ROT]
    return jnp.concatenate(
        [front_half * cos_t - back_half * sin_t, back_half * cos_t + front_half * sin_t, source[ROT:]], axis=0
    )


def attention_heads(
    first_head, heads, tile, land, cos_ref, sin_ref, start_ref, out, q_t, k_t, v_t, g_t, q_n, k_n, probs, dk_acc, dv_acc,
    between,
):
    total = land.shape[1]
    steps = total // tile
    scale = HD**-0.5
    hs = range(heads)

    def lanes(h):
        return slice((first_head + h) * HD, (first_head + h + 1) * HD)

    @pl.loop(0, steps)
    def _(i):
        place = pl.ds(pl.multiple_of(i * tile, tile), tile)
        cos_t, sin_t = cos_ref[:, place], sin_ref[:, place]
        for h in hs:
            x = turn(land[0, place, lanes(h)].astype(F32).T, cos_t, sin_t) * scale
            q_t[h, :, place] = x.astype(BF)
            q_n[h, place, :] = x.T.astype(BF)
            x = turn(land[1, place, lanes(h)].astype(F32).T, cos_t, sin_t)
            k_t[h, :, place] = x.astype(BF)
            k_n[h, place, :] = x.T.astype(BF)
            v_t[h, :, place] = land[2, place, lanes(h)].astype(F32).T.astype(BF)
            g_t[h, :, place] = land[3, place, lanes(h)].astype(F32).T.astype(BF)
            dk_acc[h, place, :] = jnp.zeros((tile, HD), F32)
            dv_acc[h, place, :] = jnp.zeros((tile, HD), F32)

    def one_tile(i):
        qs = pl.ds(pl.multiple_of(i * tile, tile), tile)
        start = start_ref[0:1, qs]
        queries = [q_t[h, :, qs] for h in hs]
        queries_n = [q_n[h, qs, :] for h in hs]
        cots = [g_t[h, :, qs] for h in hs]
        cots_n = [land[3, qs, lanes(h)] for h in hs]
        key_at = lax.broadcasted_iota(jnp.int32, (tile, tile), 0)
        query_at = lax.broadcasted_iota(jnp.int32, (tile, tile), 1)

        def score(j, tops, diagonal):
            first = pl.multiple_of(j * tile, tile)
            allowed = key_at >= (start - first)
            if diagonal:
                allowed = allowed & (key_at <= query_at)
            result = []
            for h in hs:
                s = dot32(k_n[h, pl.ds(first, tile), :], queries[h])
                s = jnp.where(allowed, s, NEGATIVE)
                probs[h, pl.ds(first, tile), :] = s
                result.append(jnp.maximum(tops[h], jnp.max(s, axis=0, keepdims=True)))
            return tuple(result)

        tops = tuple(jnp.full((1, tile), NEGATIVE, F32) for _ in hs)
        tops = lax.fori_loop(0, i, lambda j, c: score(j, c, False), tops)
        tops = score(i, tops, True)

        def mix(j, carry):
            sums, mixed = carry
            ks = pl.ds(pl.multiple_of(j * tile, tile), tile)
            new_sums, new_mixed = [], []
            for h in hs:
                p = jnp.exp(probs[h, ks, :] - tops[h])
                probs[h, ks, :] = p
                new_sums.append(sums[h] + jnp.sum(p, axis=0, keepdims=True))
                new_mixed.append(mixed[h] + dot32(v_t[h, :, ks], p.astype(BF)))
            return tuple(new_sums), tuple(new_mixed)

        zeros = tuple(jnp.zeros((1, tile), F32) for _ in hs)
        wide_zeros = tuple(jnp.zeros((HD, tile), F32) for _ in hs)
        sums, mixed = lax.fori_loop(0, i + 1, mix, (zeros, wide_zeros))
        inverse = [1.0 / sums[h] for h in hs]
        mixed = [mixed[h] * inverse[h] for h in hs]
        delta = [jnp.sum(mixed[h] * cots[h].astype(F32), axis=0, keepdims=True) for h in hs]

        def back(j, carry):
            ks = pl.ds(pl.multiple_of(j * tile, tile), tile)
            result = []
            for h in hs:
                p = probs[h, ks, :] * inverse[h]
                dp = dot32(land[2, ks, lanes(h)], cots[h])
                ds = (p * (dp - delta[h])).astype(BF)
                dv_acc[h, ks, :] += dot32(p.astype(BF), cots_n[h])
                dk_acc[h, ks, :] += dot32(ds, queries_n[h])
                result.append(carry[h] + dot32(k_t[h, :, ks], ds))
            return tuple(result)

        dq = lax.fori_loop(0, i + 1, back, wide_zeros)
        cos_t, sin_t = cos_ref[:, qs], sin_ref[:, qs]
        for h in hs:
            out[i, 0, :, lanes(h)] = turn(dq[h] * scale, cos_t, -sin_t).T.astype(BF)
            out[i, 3, :, lanes(h)] = mixed[h].T.astype(BF)

    @pl.loop(0, steps)
    def _(i):
        one_tile(i)
        between(i)

    @pl.loop(0, steps)
    def _(i):
        place = pl.ds(pl.multiple_of(i * tile, tile), tile)
        cos_t, sin_t = cos_ref[:, place], sin_ref[:, place]
        for h in hs:
            out[i, 1, :, lanes(h)] = turn(dk_acc[h, place, :].T, cos_t, -sin_t).T.astype(BF)
            out[i, 2, :, lanes(h)] = dv_acc[h, place, :].astype(BF)


def back_kernel(
    arrays, scatter, split, heads, tokens, land_ref, cos_ref, sin_ref, start_ref, g_ref, normed_ref, wq_ref, wo_ref,
    branch_ff, branch_y, d_hidden_ref, wu_ref, input_ref, grad_ref, stats_ref, gain_ref, out_bias_ref, down_bias_ref,
    ubias_ref, *refs,
):
    x, z, t = lax.axis_index("dp"), lax.axis_index("blk"), lax.axis_index("tensor")
    refs = list(refs)

    def take_refs(n):
        taken = refs[:n]
        del refs[:n]
        return taken

    own = take_refs(1)
    (home,) = take_refs(1)
    outs, landed, crossed = take_refs(4), take_refs(4), take_refs(4)
    up_part, dnorm_ff = take_refs(2)
    home_x, branch_y2, dnorm_y, sum_ff, over_x_ff, cross_ff = take_refs(6) if scatter else [None] * 6
    output_o, input_grad_o, small = take_refs(3) if scatter else [None] * 3
    out, dwo, dwq, load_sems, home_sems, home_keep, stage_sems = take_refs(7)
    give, take, take_y, tile_sems, scatter_sems, cross_sems = take_refs(6) if scatter else [None] * 6
    d_normed, moments, stats, small_in, norm_sems = take_refs(5) if scatter else [None] * 5
    nz, _, _, att = out.shape
    total = nz * tokens
    many, features = normed_ref.shape
    half, width = many // 2, features // 4
    rows = nz // 2
    groups = att // (heads * HD)
    peers = {"x": {"dp": 1 - x}, "y": {"tensor": flip(t, 2)}, "c": {"tensor": flip(t, 1)}}
    greet([{"blk": flip(z, m)} for m in range(1, nz)] + (list(peers.values()) if scatter else [peers["x"]]))
    work = Chain(arrays, own + [up_part, dwo, dwq], outs, landed, crossed, refs)
    work.begin()

    def remote(which, stage, src, dst, to):
        return pltpu.make_async_remote_copy(
            src, dst, scatter_sems.at[0, which, stage], scatter_sems.at[1, which, stage],
            device_id=peers[to], device_id_type=MESH,
        )

    if scatter:
        small[...] = jnp.zeros_like(small)
        ff = ubias_ref.shape[1]
        for r in range(ff // width):
            small[pl.ds(3 + x * (ff // width) + r, 1), :] = ubias_ref[0:1, r * width : (r + 1) * width]
        qkv_row = 3 + 2 * ff // width

    def branch_over_y():
        return remote(0, 0, branch_ff.at[1 - t // 2, pl.ds(half, half)], branch_y2, "y")

    def dnorm_over_y():
        return remote(1, 0, dnorm_ff.at[1 - t // 2], dnorm_y, "y")

    def ff_x(which):
        return remote(which, 1, sum_ff.at[which, pl.ds((1 - x) * half, half)], over_x_ff.at[which], "x")

    def add_ff(which):
        (dnorm_over_y if which else branch_over_y)().wait_recv()
        ours = (branch_ff, dnorm_ff)[which]
        size = half // 4

        def at(k):
            return pl.ds(k * size, size)

        def tile(i, k):
            n = 2 * i + k % 2
            return give.at[n // 4, at(n % 4)]

        def theirs(k):
            if which == 1:
                return dnorm_y.at[at(k)]
            return branch_y.at[at(k)] if k < 4 else branch_y2.at[at(k - 4)]

        def fetch(k):
            return [
                pltpu.make_async_copy(ours.at[t // 2, at(k)], tile(0, k), tile_sems.at[0, k % 2]),
                pltpu.make_async_copy(theirs(k), tile(1, k), tile_sems.at[1, k % 2]),
            ]

        def keep(k):
            return pltpu.make_async_copy(tile(2, k), sum_ff.at[which, at(k)], tile_sems.at[2, k % 2])

        blocks = many // size
        for copy in fetch(0):
            copy.start()
        for k in range(blocks):
            if k + 1 < blocks:
                for copy in fetch(k + 1):
                    copy.start()
            for copy in fetch(k):
                copy.wait()
            if k >= 2:
                keep(k - 2).wait()
            add_rows(tile(2, k), tile(0, k), tile(1, k))
            keep(k).start()
        for k in range(blocks - 2, blocks):
            keep(k).wait()
        ff_x(which).start()

    tn_dims = (((0,), (0,)), ((), ()))
    nt_dims = (((1,), (1,)), ((), ()))
    general = functools.partial(lax.dot_general, preferred_element_type=F32)
    at_step, ready = [0], [work.first_of(2)]

    def step():
        work.step(at_step[0])
        assert at_step[0] + work.INWARD < ready[0]
        at_step[0] += 1

    def spread(d_hidden, weight, normed, stage):
        ff = d_hidden.shape[1]
        part = features // 2
        wide = pl.ds(pl.multiple_of(x * ff, 128), ff)
        loads = [
            pltpu.make_async_copy(d_hidden_ref, d_hidden, load_sems.at[0, 0]),
            pltpu.make_async_copy(wu_ref.at[:, wide] if split else wu_ref, weight, load_sems.at[0, 1]),
        ] + [
            pltpu.make_async_copy(normed_ref.at[:, pl.ds(k * part, part)], normed.at[k], load_sems.at[1, k]) for k in range(2)
        ]
        for copy in loads:
            copy.start()
        loads[0].wait()
        loads[1].wait()

        def value(at, columns):
            return general(d_hidden[at, :], weight[columns, :], nt_dims)

        if scatter:
            core_share(cross_ff, stage, cross_sems, stage_sems, tokens, t, value, dnorm_ff, step)
            dnorm_over_y().start()
        else:
            for r in range(nz):
                at = pl.ds(r * tokens, tokens)
                for columns in range(0, features, 512):
                    stage[0, :, columns : columns + 512] = value(at, pl.ds(columns, 512)).astype(BF)
                copy = pltpu.make_async_copy(stage.at[0], dnorm_ff.at[at], stage_sems.at[0])
                copy.start()
                copy.wait()
        step()

        def keep(k, i):
            rows = pl.ds(pl.multiple_of(k * part + i * 256, 256), 256)
            return pltpu.make_async_copy(
                stage.at[i % 2, pl.ds(0, 256), pl.ds(0, ff)], up_part.at[rows], stage_sems.at[i % 2]
            )

        for k in range(2):
            loads[2 + k].wait()

            @pl.loop(0, part // 256)
            def _(i, k=k):
                @pl.when(i >= 2)
                def _():
                    keep(k, i - 2).wait()

                f = pl.ds(pl.multiple_of(i * 256, 256), 256)
                stage[i % 2, :256, :ff] = general(normed[k, :, f], d_hidden[...], tn_dims).astype(BF)
                keep(k, i).start()

            for i in range(part // 256 - 2, part // 256):
                keep(k, i).wait()
            step()

    if scatter:
        branch_over_y().start()
    pl.run_scoped(
        spread,
        pltpu.VMEM(d_hidden_ref.shape, BF),
        pltpu.VMEM((features, d_hidden_ref.shape[1]), BF),
        pltpu.VMEM((2, many, features // 2), BF),
        pltpu.VMEM((2, tokens, features), BF),
    )

    def lanes(p):
        return pl.ds(p * heads * HD, heads * HD)

    def home_copy(p, m, src, dst):
        return pltpu.make_async_remote_copy(
            src, dst, home_sems.at[0, p, m], home_sems.at[1, p, m], device_id={"blk": flip(z, m)}, device_id_type=MESH
        )

    def go_home(p, m):
        src = out.at[flip(z, m), :, :, lanes(p)]
        dst = home.at[:, z, :, lanes(p)]
        if m == 0:
            return pltpu.make_async_copy(src, dst, home_keep.at[p])
        return home_copy(p, m, src, dst)

    def arrive_home(p, m):
        ref = home.at[:, flip(z, m), :, lanes(p)]
        return home_copy(p, m, ref, ref)

    def attend(land, *scratch):
        load = pltpu.make_async_copy(land_ref, land, load_sems.at[0, 0])
        load.start()
        load.wait()
        for p in range(groups):
            plan = SCHEDULE[p] if p < len(SCHEDULE) else ()
            first = at_step[0]
            at_step[0] += sum(plan)

            def between(i, plan=plan, first=first):
                at = first
                for tile, steps in enumerate(plan):
                    if steps:

                        @pl.when(i == tile)
                        def _(at=at, steps=steps):
                            for c in range(at, at + steps):
                                work.step(c)

                    at += steps

            attention_heads(p * heads, heads, tokens, land, cos_ref, sin_ref, start_ref, out, *scratch, between)
            for m in (2, 3, 1, 0):
                go_home(p, m).start()
            if scatter:
                for which in (0, 1) if groups == 1 else (p,):
                    add_ff(which)

    pl.run_scoped(
        attend,
        pltpu.VMEM((4, total, att), BF),
        *[pltpu.VMEM((heads, HD, total), BF)] * 4,
        *[pltpu.VMEM((heads, total, HD), BF)] * 2,
        pltpu.VMEM((heads, total, tokens), F32),
        *[pltpu.VMEM((heads, total, HD), F32)] * 2,
    )
    def share_home(p):
        src, dst = home.at[:, pl.ds((1 - x) * rows, rows), :, lanes(p)], home_x.at[:, :, :, lanes(p)]
        return remote(p, 2, src, dst, "x")

    def come_home(p):
        for m in range(nz):
            if m == 0:
                go_home(p, m).wait()
            else:
                go_home(p, m).wait_send()
                arrive_home(p, m).wait_recv()
        if scatter:
            share_home(p).start()

    last = work.first_of(2) - work.INWARD - 2
    assert at_step[0] <= last - HOME_APART * (groups - 1)
    while at_step[0] <= last:
        for p in range(groups):
            if at_step[0] == last - HOME_APART * (groups - 1 - p):
                come_home(p)
        step()

    def over_core(which):
        return remote(which, 3, give, take.at[which], "c")

    def over_y(which):
        return remote(which, 4, take.at[which, 1 - t // 2], take_y.at[which], "y")

    def project(stream, hcat, hx, wcat, wo):
        def piece(i, r):
            at = pl.ds(r * tokens, tokens)
            return hcat.at[at, pl.ds(i * att, att)] if split else hcat.at[i, at]

        loads = [
            pltpu.make_async_copy(home.at[i, r], piece(i, r), load_sems.at[i, r])
            for i in (3, 0, 1, 2)
            for r in range(nz)
        ]
        weights = [] if not scatter else [
            pltpu.make_async_copy(
                wq_ref.at[i, :, pl.ds(pl.multiple_of(side * att, 128), att)],
                wcat.at[s, :, pl.ds(i * att, att)],
                load_sems.at[4 + s, i],
            )
            for s, side in enumerate((x, 1 - x))
            for i in range(3)
        ] + [
            pltpu.make_async_copy(wo_ref.at[pl.ds(side * att, att)], wo.at[s], load_sems.at[4 + s, 3])
            for s, side in enumerate((x, 1 - x))
        ]
        part = features // 2

        def streamed(k):
            source = g_ref if k < 2 else normed_ref
            return pltpu.make_async_copy(source.at[:, pl.ds((k % 2) * part, part)], stream.at[k % 2], load_sems.at[6, k % 2])

        for copy in loads[:4] + [streamed(0), streamed(1)] + loads[4:] + (weights if scatter else []):
            copy.start()
        step()
        for copy in loads:
            copy.wait()
        if split:
            attended = hcat[:, 3 * att :]
        else:
            d_qkv, attended = jnp.concatenate([hcat[i] for i in range(3)], axis=1), hcat[3]
        for k in range(2):
            streamed(k).wait()
            for j in range(part // width):
                value = general(attended, stream[k, :, j * width : (j + 1) * width], tn_dims)
                dwo[pl.ds((k * (part // width) + j) * att, att), :] = value.astype(BF)
            streamed(k + 2).start()
        ready[0] = work.first_of(3)
        for k in range(2):
            step()
            streamed(k + 2).wait()

            @pl.loop(0, part // 256)
            def _(j, k=k):
                f = pl.ds(pl.multiple_of(j * 256, 256), 256)
                value = general(stream[k, :, f], hcat[:, : 3 * att] if split else d_qkv, tn_dims).astype(BF)
                for i in range(3):
                    at = pl.multiple_of(i * features + k * part + j * 256, 256)
                    dwq[pl.ds(at, 256), :] = value[:, i * att : (i + 1) * att]

        ready[0] = work.n + work.steps
        if not scatter:
            return
        others = [
            pltpu.make_async_copy(
                home_x.at[i, r], hx.at[pl.ds(r * tokens, tokens), pl.ds(i * att, att)], load_sems.at[i, r]
            )
            for i in range(4)
            for r in range(rows)
        ]
        for p in range(groups):
            share_home(p).wait_recv()
        for copy in others:
            copy.start()
        for copy in weights + others:
            copy.wait()

        def share(which, of_core, target, plus):
            @pl.loop(0, 2 * rows)
            def _(k):
                v = k // rows
                columns = pl.ds(pl.multiple_of((2 * v + of_core) * width, width), width)
                at = pl.ds(pl.multiple_of((k % rows) * tokens, tokens), tokens)
                mine = pl.ds(pl.multiple_of(x * half + (k % rows) * tokens, tokens), tokens)
                if which == 0:
                    value = dot32(hcat[mine, 3 * att :], wo[0, :, columns]) + dot32(hx[at, 3 * att :], wo[1, :, columns])
                else:
                    value = general(hcat[mine, : 3 * att], wcat[0, columns, :], nt_dims)
                    value = value + general(hx[at, : 3 * att], wcat[1, columns, :], nt_dims)
                if plus:
                    value = value + target[v, at, :].astype(F32)
                target[v, at, :] = value.astype(BF)

        sums = jnp.sum(hcat[:, : 3 * att].astype(F32), axis=0, keepdims=True)
        for i in range(3):
            at = pl.ds(pl.multiple_of(x * att, 128), att)
            small[qkv_row + i : qkv_row + i + 1, at] = sums[:, i * att : (i + 1) * att]
        core = t % 2
        share(0, 1 - core, give, False)
        over_core(0).start()
        step()
        over_core(0).wait_send()
        share(1, 1 - core, give, False)
        over_core(1).start()
        step()
        for which in range(2):
            over_core(which).wait_recv()
            share(which, core, take.at[which], True)
            over_y(which).start()
            step()

    pl.run_scoped(
        project,
        pltpu.VMEM((2, many, features // 2), BF),
        pltpu.VMEM((many, 4 * att) if split else (4, many, att), BF),
        pltpu.VMEM((half, 4 * att), BF),
        pltpu.VMEM((2, features, 3 * att), BF),
        pltpu.VMEM((2, att, features), BF),
    )

    def load_to(refs):
        copies = [pltpu.make_async_copy(src, dst, tile_sems.at[i // 2, i % 2]) for i, (src, dst) in enumerate(refs)]
        for copy in copies:
            copy.start()
        for copy in copies:
            copy.wait()

    mine = pl.ds(x * half, half)
    spare = 1 - t // 2

    def total_share(which):
        over_y(which).wait_recv()
        over_y(which).wait_send()
        ff_x(which).wait_recv()
        load_to(
            [
                (sum_ff.at[which, mine], give.at[0]),
                (over_x_ff.at[which], give.at[1]),
                ((input_ref, grad_ref)[which], take.at[which, spare]),
            ]
            + ([(stats_ref.at[mine], stats)] if which else [])
        )

        def value(at):
            ff = give[0, at, :].astype(F32) + give[1, at, :].astype(F32)
            return ff + (take[which, t // 2, at, :].astype(F32) + take_y[which, at, :].astype(F32))

        return value

    def block_at(i):
        return pl.ds(pl.multiple_of(i * 128, 128), 128)

    def save(which):
        return pltpu.make_async_copy(take_y.at[which], (output_o, input_grad_o)[which], home_keep.at[which])

    def norm_copy(k, src, dst, device):
        return pltpu.make_async_remote_copy(
            src, dst, norm_sems.at[0, k], norm_sems.at[1, k], device_id=device, device_id_type=MESH
        )

    def exchange(k):
        return norm_copy(k, moments.at[2 * k], moments.at[2 * k + 1], peers["cy"[k]])

    def output():
        over_core(1).wait_send()
        value = total_share(0)

        @pl.loop(0, half // 128)
        def _(i):
            at = block_at(i)
            total = take[0, spare, at, :].astype(F32) + (value(at) + out_bias_ref[...] + down_bias_ref[...])
            take_y[0, at, :] = total.astype(BF)

        save(0).start()

    def own_gain():
        return gain_ref[:, pl.ds(pl.multiple_of(t * width, width), width)]

    def standardized(at):
        inverse = stats[at, 64:65]
        return (take[0, spare, at, :].astype(F32) - stats[at, 0:1]) * inverse, inverse

    def norm_sums():
        value = total_share(1)

        @pl.loop(0, half // 128)
        def _(i):
            at = block_at(i)
            d = value(at)
            d_normed[at, :] = d
            xhat, _ = standardized(at)
            scaled = d * own_gain()
            one = jnp.sum(scaled, axis=-1, keepdims=True)
            two = jnp.sum(scaled * xhat, axis=-1, keepdims=True)
            lane = lax.broadcasted_iota(jnp.int32, (128, 128), 1)
            moments[0, at, :] = jnp.where(lane < 64, one, two)
            small[0:1, :] += jnp.sum(d * xhat, axis=0, keepdims=True)
            small[1:2, :] += jnp.sum(d, axis=0, keepdims=True)
            small[2:3, :] += jnp.sum(take[1, spare, at, :].astype(F32), axis=0, keepdims=True)

        exchange(0).start()

    def norm_sums_core():
        exchange(0).wait()
        moments[2] = moments[0] + moments[1]
        exchange(1).start()

    def norm_back():
        exchange(1).wait()

        @pl.loop(0, half // 128)
        def _(i):
            at = block_at(i)
            total = (moments[2, at, :] + moments[3, at, :]) * (1.0 / features)
            xhat, inverse = standardized(at)
            scaled = d_normed[at, :] * own_gain()
            back = inverse * (scaled - total[:, 0:1] - xhat * total[:, 64:65])
            take_y[1, at, :] = (take[1, spare, at, :].astype(F32) + back).astype(BF)

        save(1).start()

    def small_sums(k):
        device = ({"dp": 1 - x}, {"blk": flip(z, 1)}, {"blk": flip(z, 2)})[k]
        copy = norm_copy(2 + k, small, small_in.at[k], device)
        copy.start()
        copy.wait()
        small[...] += small_in[k]

    stages = {
        "output": output, "norm_sums": norm_sums, "norm_sums_core": norm_sums_core, "norm_back": norm_back,
        "dp": functools.partial(small_sums, 0), "blk_1": functools.partial(small_sums, 1),
        "blk_2": functools.partial(small_sums, 2),
    }
    later = dict(LATER) if scatter else {}
    while at_step[0] < work.steps:
        for name in later.pop(at_step[0], ()):
            stages[name]()
        step()
    assert not later
    work.finish()
    if scatter:
        for which in range(2):
            ff_x(which).wait_send()
            save(which).wait()
        branch_over_y().wait_send()
        dnorm_over_y().wait_send()
        for p in range(groups):
            share_home(p).wait_send()


def weight_arrays(down, d_hidden, features, att):
    return [
        (*down, 1024, True), (features, d_hidden[1], 1024, True), (4 * att, features // 4, 1024, False),
        (3 * features, att, 512, False),
    ]


def back(
    scatter, split, tokens, land, cos_t, sin_t, start, cotangent, normed, wq, wo, branch_ff, branch_y, d_hidden, wu, down,
    block_input, grad_output, stats, gain, out_bias, down_bias, up_bias_part,
):
    _, total, att = land.shape
    nz = total // tokens
    many, features = normed.shape
    width, half = features // 4, many // 2
    heads = min(2, att // HD)
    groups = att // (heads * HD)
    ff = d_hidden.shape[1]
    arrays = weight_arrays(down.shape, d_hidden.shape, features, att)
    shapes = [a[:2] for a in arrays]
    hbm = pl.BlockSpec(memory_space=pl.ANY)
    vmem = pl.BlockSpec(memory_space=pltpu.VMEM)
    dma = pltpu.SemaphoreType.DMA
    scatter_scratch = [
        pltpu.VMEM((2, half, width), BF),
        pltpu.VMEM((2, 2, half, width), BF),
        pltpu.VMEM((2, half, width), BF),
        dma((3, 2)),
        dma((2, 2, 5)),
        dma((2, 2 * many // tokens)),
        pltpu.VMEM((half, width), F32),
        pltpu.VMEM((4, half, 128), F32),
        pltpu.VMEM((half, 128), F32),
        pltpu.VMEM((3, 16, width), F32),
        dma((2, 5)),
    ]
    scatter_outs = [
        jax.ShapeDtypeStruct((4, nz // 2, tokens, att), BF),
        jax.ShapeDtypeStruct((half, width), BF),
        jax.ShapeDtypeStruct((many, width), BF),
        jax.ShapeDtypeStruct((2, many, width), BF),
        jax.ShapeDtypeStruct((2, half, width), BF),
        jax.ShapeDtypeStruct((2, many, width), BF),
        jax.ShapeDtypeStruct((half, width), BF),
        jax.ShapeDtypeStruct((half, width), BF),
        jax.ShapeDtypeStruct((16, width), F32),
    ]
    results = pl.pallas_call(
        functools.partial(back_kernel, arrays, scatter, split, heads, tokens),
        out_shape=[jax.ShapeDtypeStruct((4, nz, tokens, att), BF)]
        + [jax.ShapeDtypeStruct((2,) + s, BF) for s in shapes]
        + [jax.ShapeDtypeStruct(s, BF) for s in shapes] * 2
        + [jax.ShapeDtypeStruct((features, ff), BF)]
        + [jax.ShapeDtypeStruct((2, many, width) if scatter else (many, features), BF)]
        + (scatter_outs if scatter else []),
        in_specs=[hbm] + [vmem] * 3 + [hbm] * 8 + [hbm] * 3 + [vmem] * 4 + [hbm],
        out_specs=[hbm] * 15 + ([hbm] * 8 + [vmem] if scatter else []),
        scratch_shapes=[
            pltpu.VMEM((nz, 4, tokens, att), BF),
            pltpu.VMEM(shapes[2], BF),
            pltpu.VMEM(shapes[3], BF),
            dma((7, 4)),
            dma((2, groups, nz)),
            dma((max(groups, 2),)),
            dma((4,)),
        ]
        + (scatter_scratch if scatter else [])
        + Chain.scratch(arrays),
        compiler_params=pltpu.CompilerParams(collective_id=3, has_side_effects=True, vmem_limit_bytes=60 << 20),
        cost_estimate=pl.CostEstimate(
            flops=12 * (att // HD) * total * total * HD * 4, bytes_accessed=1 << 29, transcendentals=0
        ),
        name="back",
    )(land, cos_t, sin_t, start, cotangent, normed, wq, wo, branch_ff, branch_y, d_hidden, wu, block_input, grad_output, stats,
      gain, out_bias, down_bias, up_bias_part, down)
    return results[0], results[1:5], results[14], results[21:]


def widen(source, out_shape, block, in_map, out_map, grid):
    def body(source_ref, out_ref):
        out_ref[...] = source_ref[0].astype(F32)

    return pl.pallas_call(
        body,
        out_shape=jax.ShapeDtypeStruct(out_shape, F32),
        grid=grid,
        in_specs=[pl.BlockSpec((1,) + block, in_map)],
        out_specs=pl.BlockSpec(block, out_map),
        compiler_params=pltpu.CompilerParams(vmem_limit_bytes=32 << 20),
        cost_estimate=pl.CostEstimate(flops=0, bytes_accessed=source.size * 6, transcendentals=0),
        name="widen",
    )(source)


def widen_rows(source):
    _, rows, columns = source.shape
    size = min(rows, (1 << 18) // columns)
    steps = rows // size
    return widen(
        source, (2 * rows, columns), (size, columns), lambda i, h: (h, i, 0), lambda i, h: (h * steps + i, 0), (steps, 2)
    )


def widen_columns(source):
    _, rows, columns = source.shape
    if columns % 128:
        return jnp.concatenate([source[0], source[1]], axis=1).astype(F32)
    size = min(rows, (1 << 18) // columns)
    return widen(
        source, (rows, 2 * columns), (size, columns), lambda i, h: (h, i, 0), lambda i, h: (i, h), (rows // size, 2)
    )


def widen_blocks(source):
    _, rows, columns = source.shape
    rows = rows // 4
    return widen(
        source, (2 * rows, 4 * columns), (rows, columns), lambda h, j: (h, j, 0), lambda h, j: (h, j), (2, 4)
    )


def scatter_sum(share):
    whole = lax.psum_scatter(share.astype(BF), "dp", scatter_dimension=0, tiled=True)
    return lax.psum_scatter(whole, "tensor", scatter_dimension=2, tiled=True).astype(F32)


def butterfly(value, axes):
    for axis, size in axes:
        mask = 1
        while mask < size:
            value = value + swap(value, axis, size, mask)
            mask *= 2
    return value


SCHEDULE = ((0, 1, 1, 1), (0, 1, 0, 1))
HOME_APART = 2
LATER = {26: ["output"], 28: ["norm_sums"], 29: ["norm_sums_core"], 31: ["norm_back"], 32: ["dp"], 33: ["blk_1"], 34: ["blk_2"]}


def local(
    nx, nz, nt, block_input, segment_ids, layer_norm_gain, layer_norm_bias, qkv_weight, qkv_bias, out_weight, out_bias,
    up_weight, up_bias, down_weight, down_bias, grad_output,
):
    rows, tokens, width = block_input.shape
    all_rows = nx * rows
    features = nt * width
    many = all_rows * tokens
    x, z, t = lax.axis_index("dp"), lax.axis_index("blk"), lax.axis_index("tensor")
    att = qkv_weight.shape[2] // nx
    ff = up_weight.shape[1] // nx

    split = att % 128 == 0
    gather = nt == 4 and nx == 2 and split
    qkv_whole = jnp.transpose(qkv_weight, (1, 0, 2))
    qkv_half = lax.dynamic_slice_in_dim(qkv_whole, x * att, att, 2)
    out_half = lax.dynamic_slice_in_dim(out_weight, x * att, att, 0)
    if split:
        weights = [qkv_whole, out_weight, up_weight, down_weight]
        first_biases = [qkv_bias.reshape(3, 1, nx * att), up_bias.reshape(1, nx * ff)]
    else:
        up_half = lax.dynamic_slice_in_dim(up_weight, x * ff, ff, 1)
        down_half = lax.dynamic_slice_in_dim(down_weight, x * ff, ff, 0)
        weights = [qkv_half, out_half, up_half, down_half]
        first_biases = [
            lax.dynamic_slice_in_dim(qkv_bias, x * att, att, 1).reshape(3, 1, att),
            lax.dynamic_slice_in_dim(up_bias, x * ff, ff, 0).reshape(1, ff),
        ]

    frequency = np.exp(np.arange(ROT // 2) * (-2.0 / ROT) * ROPE_LOG_BASE).astype(np.float32)[:, None]

    if gather:
        sources = [block_input.reshape(rows * tokens, width), grad_output.reshape(rows * tokens, width)]
    else:
        sources = [lax.all_gather(a, "tensor", axis=2, tiled=True) for a in (block_input, grad_output)]
        sources = [lax.all_gather(a, "dp", axis=0, tiled=True).reshape(many, features) for a in sources]
    normed, cotangent, land, stats, down_part, d_hidden, branch_ff, up_bias_part, cos_t, sin_t, start, branch_y = front(
        gather, split, rows, tokens, nz, many, features, att, ff,
        [
            segment_ids, jnp.asarray(frequency), *sources, layer_norm_gain.reshape(1, features), layer_norm_bias.reshape(1, features), weights[0],
            first_biases[0], weights[1], weights[2], first_biases[1], weights[3],
        ],
    )
    home, sums, d_normed_ff, results = back(
        gather, split, tokens, land, cos_t, sin_t, start, cotangent, normed, weights[0], weights[1], branch_ff, branch_y,
        d_hidden, weights[2], down_part, block_input.reshape(rows * tokens, width),
        grad_output.reshape(rows * tokens, width), stats, layer_norm_gain.reshape(1, features), out_bias.reshape(1, width),
        down_bias.reshape(1, width), up_bias_part,
    )
    down_sum, up_sum, out_sum, qkv_sum = sums
    chunks = Chain.layout(weight_arrays(down_part.shape, d_hidden.shape, features, att))[0][-Chain.APART :]
    first = chunks[0][1]
    last_rows = lax.dynamic_slice(qkv_sum, (x, first, 0), (1, 3 * features - first, att))
    last_rows = lax.ppermute(last_rows, "dp", [(0, 1), (1, 0)])
    qkv_sum = lax.dynamic_update_slice(qkv_sum, last_rows, (1 - x, first, 0))
    if gather:
        block_output, input_grad, small = results
        block_output = block_output.reshape(rows, tokens, width)
        input_grad = input_grad.reshape(rows, tokens, width)
        gain_grad, shift_grad, bias_grad = small[0], small[1], small[2]
        units = nx * ff // width
        up_bias_grad = small[3 : 3 + units].reshape(nx * ff)
        qkv_bias_grad = small[3 + units : 6 + units]
    else:
        home = home.reshape(4, many, att)
        qkv_bias_part = jnp.sum(home[:3].astype(F32), axis=1)
        branch = branch_ff.astype(F32) + dot32(home[3], out_half)
        d_normed = d_normed_ff.astype(F32)
        for i in range(3):
            d_normed = d_normed + dot32(home[i], qkv_half[i].T)
        branch = scatter_sum(branch.reshape(all_rows, tokens, features))
        d_normed = scatter_sum(d_normed.reshape(all_rows, tokens, features))
        block_output = (block_input.astype(F32) + (branch + out_bias + down_bias)).astype(BF)

        stats = lax.dynamic_slice_in_dim(stats, x * rows * tokens, rows * tokens, 0).reshape(rows, tokens, 128)
        own_mean, own_inverse = stats[..., :1], stats[..., 64:65]
        xhat = (block_input.astype(F32) - own_mean) * own_inverse
        gain = lax.dynamic_slice_in_dim(layer_norm_gain, t * width, width, 0)
        scaled = d_normed * gain
        moments = jnp.stack([jnp.sum(scaled, axis=-1), jnp.sum(scaled * xhat, axis=-1)])
        moments = butterfly(moments, [("tensor", nt)]) / features
        first, second = moments[0][..., None], moments[1][..., None]
        input_grad = (
            grad_output.astype(F32) + own_inverse * (scaled - first - xhat * second)
        ).astype(BF)

        def spread(part, whole):
            shape = part.shape[:-1] + (whole,)
            at = (0,) * (part.ndim - 1) + (x * part.shape[-1],)
            return lax.dynamic_update_slice(jnp.zeros(shape, F32), part, at)

        small = [
            jnp.sum(d_normed * xhat, axis=(0, 1)),
            jnp.sum(d_normed, axis=(0, 1)),
            jnp.sum(grad_output.astype(F32), axis=(0, 1)),
            spread(up_bias_part[0], nx * ff),
            spread(qkv_bias_part, nx * att).reshape(-1),
        ]
        packed = butterfly(jnp.concatenate(small), [("dp", nx), ("blk", nz)])
        gain_grad, shift_grad, bias_grad = (packed[i * width : (i + 1) * width] for i in range(3))
        up_bias_grad = packed[3 * width : 3 * width + nx * ff]
        qkv_bias_grad = packed[3 * width + nx * ff :].reshape(3, nx * att)

    down_grad = widen_rows(down_sum)
    up_grad = widen_columns(up_sum)
    out_grad = widen_blocks(out_sum)
    qkv_grad = widen_columns(qkv_sum).reshape(3, features, nx * att)
    qkv_grad = jnp.transpose(qkv_grad, (1, 0, 2))
    return (
        block_output, input_grad, gain_grad, shift_grad, qkv_grad, qkv_bias_grad, out_grad, bias_grad, up_grad,
        up_bias_grad, down_grad, bias_grad,
    )


def solution(mesh):
    in_specs = (
        P("dp", "blk", "tensor"), P("dp", None), P(), P(), P(None, None, "tensor"), P(None, "tensor"), P("tensor", None),
        P("tensor"), P(None, "tensor"), P("tensor"), P("tensor", None), P("tensor"), P("dp", "blk", "tensor"),
    )
    out_specs = (
        P("dp", "blk", "tensor"), P("dp", "blk", "tensor"), P("tensor"), P("tensor"), P(None, None, "tensor"),
        P(None, "tensor"), P("tensor", None), P("tensor"), P(None, "tensor"), P("tensor"), P("tensor", None), P("tensor"),
    )
    body = functools.partial(local, mesh.shape["dp"], mesh.shape["blk"], mesh.shape["tensor"])
    return jax.shard_map(body, mesh=mesh, in_specs=in_specs, out_specs=out_specs, check_vma=False)
```

```python
import functools
import math

import jax
import jax.numpy as jnp
import numpy as np
from jax import lax
from jax.experimental import pallas as pl
from jax.experimental.pallas import tpu as pltpu
from jax.sharding import PartitionSpec as P

HD = 64
ROT = 32
EPSILON = 1e-05
ROPE_LOG_BASE = math.log(10000.0)
NEGATIVE = -1e30
F32 = jnp.float32
BF = jnp.bfloat16
MESH = pl.DeviceIdType.MESH
dot32 = functools.partial(jnp.dot, preferred_element_type=F32)


def swap(value, axis, size, mask):
    return lax.ppermute(value, axis, [(i, i ^ mask) for i in range(size)])


def flip(index, mask):
    if mask == 0:
        return index
    if mask == 1:
        return index + 1 - 2 * (index % 2)
    if mask == 2:
        return (index + 2) % 4
    return 3 - index


def core_share(cross_ref, stage, cross_sems, stage_sems, tokens, t, value, out, between=None):
    _, many, width = out.shape
    blocks = many // tokens
    core = t % 2

    def place(k):
        return pl.ds(pl.multiple_of((k % blocks) * tokens, tokens), tokens)

    def tile(slot, k):
        return stage.at[k % 2, :, pl.ds(slot * width, width)]

    def at(ref, k):
        return ref.at[k // blocks, place(k)]

    def columns(k, of_core):
        return pl.ds(pl.multiple_of((2 * (k // blocks) + of_core) * width, width), width)

    def cross(k, src, dst):
        return pltpu.make_async_remote_copy(
            src, dst, cross_sems.at[0, k], cross_sems.at[1, k], device_id={"tensor": flip(t, 1)}, device_id_type=MESH
        )

    def give(k):
        return cross(k, tile(0, k), at(cross_ref, k))

    def got(k):
        return cross(k, at(cross_ref, k), at(cross_ref, k))

    def fetch(k):
        return pltpu.make_async_copy(at(cross_ref, k), tile(1, k), stage_sems.at[k % 2])

    def keep(k):
        return pltpu.make_async_copy(tile(2, k), at(out, k), stage_sems.at[2 + k % 2])

    @pl.loop(0, 2 * blocks)
    def _(k):
        @pl.when(k >= 2)
        def _():
            give(k - 2).wait_send()

        stage[k % 2, :, :width] = value(place(k), columns(k, 1 - core)).astype(BF)
        give(k).start()

    for k in (2 * blocks - 2, 2 * blocks - 1):
        give(k).wait_send()
    if between:
        between()
    got(0).wait_recv()
    fetch(0).start()

    @pl.loop(0, 2 * blocks)
    def _(k):
        @pl.when(k >= 2)
        def _():
            keep(k - 2).wait()

        @pl.when(k + 1 < 2 * blocks)
        def _():
            got(k + 1).wait_recv()
            fetch(k + 1).start()

        mine = value(place(k), columns(k, core))
        fetch(k).wait()
        stage[k % 2, :, 2 * width : 3 * width] = (mine + stage[k % 2, :, width : 2 * width].astype(F32)).astype(BF)
        keep(k).start()

    for k in (2 * blocks - 2, 2 * blocks - 1):
        keep(k).wait()


def front_kernel(
    gather, split, rows, tokens, segments_ref, frequency_ref, x_own, g_own, gain_ref, shift_ref, wq_ref, bq_ref, wo_ref, wu_ref, bu_ref, wd_ref,
    normed_o, g_o, land_o, stats_o, down_o, d_hidden_o, branch_o, ubias_o, cos_o, sin_o, start_o, branch_y_o, cross_o,
    xin, gin, vq, vo, vu, vd, pay, act, slope, stage, gather_sems, land_sems, load_sems, keep_sems, stage_sems, cross_sems, over_y_sems, segments, segment_sems,
):
    x, z, t = lax.axis_index("dp"), lax.axis_index("blk"), lax.axis_index("tensor")
    many, features = xin.shape
    half = rows * tokens
    width = features // 4
    att = vq.shape[2]
    ff = vu.shape[1]
    nz = pay.shape[0]
    wide = min(512, ff)

    def remote(src, dst, sems, device):
        return pltpu.make_async_remote_copy(
            src, dst, sems[0], sems[1], device_id=device, device_id_type=MESH
        )

    peers = {"x": {"dp": 1 - x}, "y": {"tensor": flip(t, 2)}, "c": {"tensor": flip(t, 1)}}
    barrier = pltpu.get_barrier_semaphore()
    greet = [{"blk": flip(z, m)} for m in range(1, nz)] + (list(peers.values()) if gather else [peers["x"]])
    for device in greet:
        pl.semaphore_signal(barrier, inc=1, device_id=device, device_id_type=MESH)

    loads = [
        pltpu.make_async_copy(
            wq_ref.at[:, :, pl.ds(pl.multiple_of(x * att, 128), att)] if split else wq_ref, vq, load_sems.at[0]
        ),
        pltpu.make_async_copy(
            wu_ref.at[:, pl.ds(pl.multiple_of(x * ff, 128), ff)] if split else wu_ref, vu, load_sems.at[1]
        ),
        pltpu.make_async_copy(wd_ref.at[pl.ds(x * ff, ff)] if split else wd_ref, vd, load_sems.at[2]),
        pltpu.make_async_copy(wo_ref.at[pl.ds(x * att, att)] if split else wo_ref, vo, load_sems.at[3]),
    ]
    if not gather:
        both = [
            pltpu.make_async_copy(x_own, xin, load_sems.at[4]),
            pltpu.make_async_copy(g_own, gin, load_sems.at[5]),
        ]
    else:
        both = [
            pltpu.make_async_copy(
                own,
                buf.at[pl.ds(x * half, half), pl.ds(pl.multiple_of(t * width, 128), width)],
                load_sems.at[4 + i],
            )
            for i, (own, buf) in enumerate([(x_own, xin), (g_own, gin)])
        ]
    both[0].start()
    both[1].start()
    pl.semaphore_wait(barrier, len(greet))

    class Gather:
        def __init__(self, which, own, buf, first, size):
            self.which, self.own, self.buf, self.names = which, own, buf, []
            self.base, self.size = first, size

        def at(self, dx, dt, r):
            return self.buf.at[
                pl.ds(pl.multiple_of((1 - x if dx else x) * half + self.base + r * self.size, self.size), self.size),
                pl.ds(pl.multiple_of(flip(t, dt) * width, 128), width),
            ]

        plan = {
            "x": (0, 0, "x", 1, 0), "y": (0, 0, "y", 0, 2), "c": (0, 0, "c", 0, 1),
            "ex": (1, 0, "c", 1, 1), "ey": (0, 2, "c", 0, 3), "ed": (1, 2, "c", 1, 3),
        }

        def sems(self, kind, r):
            k = 2 * ("x", "y", "c", "d", "ex", "ey", "ed").index(kind) + r
            return gather_sems.at[self.which, 0, k], gather_sems.at[self.which, 1, k]

        def copy(self, kind, r):
            if kind == "d":
                dx, dt, to = (1, 0, "y") if r == 0 else (0, 2, "x")
            else:
                dx, dt, to = self.plan[kind][:3]
            src = dst = self.at(dx, dt, r)
            if kind in "xyc":
                src = self.own.at[pl.ds(self.base + r * self.size, self.size)]
            return remote(src, dst, self.sems(kind, r), peers[to])

        def start(self, kind, r):
            self.names.append((kind, r))
            self.copy(kind, r).start()

        def wait(self, kind, r):
            if kind == "d":
                dx, dt, to = 1, 2, "y"
            else:
                to, dx, dt = self.plan[kind][2:]
            ref = self.at(dx, dt, r)
            remote(ref, ref, self.sems(kind, r), peers[to]).wait_recv()

        def begin(self):
            for kind, r in (("x", 0), ("y", 1), ("x", 1), ("y", 0), ("c", 0), ("c", 1)):
                self.start(kind, r)

        def second(self):
            self.wait("x", 0)
            self.start("d", 0)
            self.start("ex", 0)
            self.wait("y", 1)
            self.start("d", 1)
            self.start("ey", 1)

        def third(self):
            self.wait("x", 1)
            self.start("ex", 1)
            self.wait("y", 0)
            self.start("ey", 0)

        def fourth(self):
            self.wait("d", 0)
            self.start("ed", 0)
            self.wait("d", 1)
            self.start("ed", 1)

        def last(self):
            for kind in ("c", "ex", "ey", "ed"):
                for r in range(2):
                    self.wait(kind, r)

        def drain(self):
            for kind, r in self.names:
                self.copy(kind, r).wait_send()

    ins = [Gather(r, x_own, xin, r * tokens, tokens // 2) for r in range(rows)]
    cots = Gather(rows, g_own, gin, 0, half // 2)
    own_segments = pltpu.make_async_copy(segments_ref, segments.at[x], segment_sems.at[0])
    own_segments.start()
    segments_x = remote(segments_ref, segments.at[x], (segment_sems.at[1], segment_sems.at[2]), peers["x"])
    segments_x.start()
    if gather:
        ins[0].begin()
    for load in loads:
        load.start()

    own_segments.wait()
    segments_x.wait()
    ids = segments[z // rows]
    length = ids.shape[1]
    ids = jnp.sum(jnp.where(lax.broadcasted_iota(jnp.int32, ids.shape, 0) == z % rows, ids, 0), axis=0, keepdims=True)
    ids = jnp.broadcast_to(ids, (8, length))
    at = lax.broadcasted_iota(jnp.int32, (8, length), 1)
    first_of = jnp.where(ids != pltpu.roll(ids, 1, 1), at, 0)
    reach = 1
    while reach < length:
        first_of = jnp.maximum(first_of, jnp.where(at >= reach, pltpu.roll(first_of, reach, 1), 0))
        reach *= 2
    start_o[...] = first_of
    angles = frequency_ref[...] * (at - first_of)[0:1].astype(F32)
    cos_o[...] = jnp.cos(angles)
    sin_o[...] = jnp.sin(angles)

    def place(position):
        return pl.ds(pl.multiple_of(position * tokens, tokens), tokens)

    def normalize(row):
        @pl.loop(0, tokens // 128)
        def _(i):
            at = pl.ds(pl.multiple_of(row * tokens + i * 128, 128), 128)
            v = xin[at, :].astype(F32)
            mean = jnp.sum(v, axis=-1, keepdims=True) * (1.0 / features)
            v = v - mean
            inverse = lax.rsqrt(jnp.sum(v * v, axis=-1, keepdims=True) * (1.0 / features) + EPSILON)
            xin[at, :] = (v * inverse * gain_ref[...] + shift_ref[...]).astype(BF)
            lane = lax.broadcasted_iota(jnp.int32, (128, 128), 1)
            stats_o[at, :] = jnp.where(lane < 64, mean, inverse)

    def parts(kind):
        return pl.ds(0, 3) if kind == 0 else pl.ds(3, 1)

    def sems(kind, m):
        return land_sems.at[0, kind, m], land_sems.at[1, kind, m]

    def own_row(kind):
        return pltpu.make_async_copy(
            pay.at[z, parts(kind)], land_o.at[parts(kind), place(z)], keep_sems.at[2 + kind]
        )

    def other_row(kind, row, m):
        return remote(pay.at[row, parts(kind)], land_o.at[parts(kind), place(z)], sems(kind, m), {"blk": row})

    def send(kind, row):
        @pl.when(z == row)
        def _():
            own_row(kind).start()

        @pl.when(z != row)
        def _():
            other_row(kind, row, flip(z, row)).start()

    def landed(kind, m):
        ref = land_o.at[parts(kind), place(flip(z, m))]
        return remote(ref, ref, sems(kind, m), {"blk": flip(z, m)})

    def project(row):
        @pl.loop(0, 3)
        def _(part):
            bias = bq_ref[part, :, pl.ds(pl.multiple_of(x * att, 128), att)] if split else bq_ref[part]
            value = dot32(xin[place(row), :], vq[part]) + bias
            pay[row, part] = value.astype(BF)

        send(0, row)

    if gather:
        ins[0].second()
        ins[0].third()
        ins[1].begin()
        ins[0].fourth()
    both[0].wait()
    for r in range(rows):
        if gather:
            ins[r].last()
            ins[r].drain()
        for row in range(r, nz, rows):
            normalize(row)
        if gather and r == 0:
            ins[1].second()
        if r == 0:
            loads[0].wait()
        for row in range(r, nz, rows):
            project(row)
        if gather and r == 0:
            ins[1].third()
            cots.begin()
            ins[1].fourth()
    keep_normed = pltpu.make_async_copy(xin, normed_o, keep_sems.at[0])
    keep_normed.start()
    if gather:
        cots.second()

    loads[1].wait()

    @pl.loop(0, many // tokens)
    def _(i):
        at = place(i)

        @pl.loop(0, ff // wide)
        def _(j):
            columns = pl.ds(pl.multiple_of(j * wide, wide), wide)
            first = x * ff if split else 0
            h = dot32(xin[at, :], vu[:, columns]) + bu_ref[:, pl.ds(pl.multiple_of(first + j * wide, wide), wide)]
            c = math.sqrt(2.0 / math.pi)
            square = h * h
            tanh = jnp.tanh(c * h * (1.0 + 0.044715 * square))
            one = 0.5 * (1.0 + tanh)
            act[at, columns] = (h * one).astype(BF)
            d = one + 0.5 * h * (1.0 - tanh * tanh) * (c * (1.0 + 3 * 0.044715 * square))
            slope[at, columns] = d.astype(BF)

    if gather:
        cots.third()
    nt_dims = (((1,), (1,)), ((), ()))
    tn_dims = (((0,), (0,)), ((), ()))
    general = functools.partial(lax.dot_general, preferred_element_type=F32)

    def through(steps, rows_of, columns_of, make, out):
        def copy(i):
            return pltpu.make_async_copy(
                stage.at[i % 2, pl.ds(0, rows_of), pl.ds(0, columns_of)],
                out.at[pl.ds(pl.multiple_of(i * rows_of, rows_of), rows_of)],
                stage_sems.at[i % 2],
            )

        @pl.loop(0, steps)
        def _(i):
            @pl.when(i >= 2)
            def _():
                copy(i - 2).wait()

            make(i, stage.at[i % 2, pl.ds(0, rows_of), pl.ds(0, columns_of)])
            copy(i).start()

        for i in range(max(0, steps - 2), steps):
            copy(i).wait()

    loads[2].wait()
    if gather:
        core_share(
            cross_o, stage, cross_sems, stage_sems, tokens, t,
            lambda at, columns: dot32(act[at, :], vd[:, columns]), branch_o,
        )
        branch_over_y = remote(
            branch_o.at[1 - t // 2, pl.ds(0, half)], branch_y_o, (over_y_sems.at[0], over_y_sems.at[1]), peers["y"]
        )
        branch_over_y.start()
    else:

        def whole(i, target):
            @pl.loop(0, features // 512)
            def _(j):
                columns = pl.ds(pl.multiple_of(j * 512, 512), 512)
                target[:, columns] = dot32(act[place(i), :], vd[:, columns]).astype(BF)

        through(many // tokens, tokens, features, whole, branch_o)

    if gather:
        cots.fourth()
    both[1].wait()
    if gather:
        cots.last()
    keep_g = pltpu.make_async_copy(gin, g_o, keep_sems.at[1])
    keep_g.start()

    loads[3].wait()
    for row in range(nz):
        pay[row, 3] = general(gin[place(row), :], vo[...], nt_dims).astype(BF)
        send(1, row)

    ubias_o[...] = jnp.zeros_like(ubias_o)

    @pl.loop(0, many // tokens)
    def _(i):
        at = place(i)

        @pl.loop(0, ff // wide)
        def _(j):
            columns = pl.ds(pl.multiple_of(j * wide, wide), wide)
            d = general(gin[at, :], vd[columns, :], nt_dims) * slope[at, columns].astype(F32)
            d = d.astype(BF)
            slope[at, columns] = d
            ubias_o[0:1, columns] += jnp.sum(d.astype(F32), axis=0, keepdims=True)

    keep_d = pltpu.make_async_copy(slope, d_hidden_o, keep_sems.at[4])
    keep_d.start()

    def down_tile(i, target):
        f = pl.ds(pl.multiple_of(i * 256, 256), 256)
        for j in range(0, features, 1024):
            target[:, j : j + 1024] = general(act[:, f], gin[:, j : j + 1024], tn_dims).astype(BF)

    through(ff // 256, 256, features, down_tile, down_o)

    keep_normed.wait()
    keep_g.wait()
    keep_d.wait()
    for kind in range(2):
        own_row(kind).wait()
        for m in range(1, nz):
            other_row(kind, flip(z, m), m).wait_send()
            landed(kind, m).wait_recv()
    if gather:
        cots.drain()
        branch_over_y.wait()


def front(gather, split, rows, tokens, nz, many, features, att, ff, operands):
    hbm = pl.BlockSpec(memory_space=pl.ANY)
    vmem = pl.BlockSpec(memory_space=pltpu.VMEM)
    shares = (2, many, features // 4) if gather else (many, features)
    return pl.pallas_call(
        functools.partial(front_kernel, gather, split, rows, tokens),
        out_shape=[
            jax.ShapeDtypeStruct((many, features), BF),
            jax.ShapeDtypeStruct((many, features), BF),
            jax.ShapeDtypeStruct((4, nz * tokens, att), BF),
            jax.ShapeDtypeStruct((many, 128), F32),
            jax.ShapeDtypeStruct((ff, features), BF),
            jax.ShapeDtypeStruct((many, ff), BF),
            jax.ShapeDtypeStruct(shares, BF),
            jax.ShapeDtypeStruct((8, ff), F32),
            jax.ShapeDtypeStruct((ROT // 2, nz * tokens), F32),
            jax.ShapeDtypeStruct((ROT // 2, nz * tokens), F32),
            jax.ShapeDtypeStruct((8, nz * tokens), jnp.int32),
            jax.ShapeDtypeStruct((many // 2, features // 4), BF),
            jax.ShapeDtypeStruct((2, many, features // 4), BF),
        ],
        in_specs=[hbm, vmem, hbm, hbm, vmem, vmem, hbm, vmem, hbm, hbm, vmem, hbm],
        out_specs=[hbm, hbm, hbm, vmem, hbm, hbm, hbm, vmem, vmem, vmem, vmem, hbm, hbm],
        scratch_shapes=[
            pltpu.VMEM((many, features), BF),
            pltpu.VMEM((many, features), BF),
            pltpu.VMEM((3, features, att), BF),
            pltpu.VMEM((att, features), BF),
            pltpu.VMEM((features, ff), BF),
            pltpu.VMEM((ff, features), BF),
            pltpu.VMEM((nz, 4, tokens, att), BF),
            pltpu.VMEM((many, ff), BF),
            pltpu.VMEM((many, ff), BF),
            pltpu.VMEM((2, tokens, features), BF),
            pltpu.SemaphoreType.DMA((rows + 1, 2, 14)),
            pltpu.SemaphoreType.DMA((2, 2, 4)),
            pltpu.SemaphoreType.DMA((6,)),
            pltpu.SemaphoreType.DMA((5,)),
            pltpu.SemaphoreType.DMA((4,)),
            pltpu.SemaphoreType.DMA((2, 2 * many // tokens)),
            pltpu.SemaphoreType.DMA((2,)),
            pltpu.VMEM((2, rows, nz * tokens), jnp.int32),
            pltpu.SemaphoreType.DMA((3,)),
        ],
        compiler_params=pltpu.CompilerParams(
            collective_id=2, has_side_effects=True, vmem_limit_bytes=60 << 20
        ),
        cost_estimate=pl.CostEstimate(
            flops=2 * many * features * (6 * ff + 4 * att), bytes_accessed=100 << 20, transcendentals=0
        ),
        name="front",
    )(*operands)[:12]


def add_rows(target, one, two):
    @pl.loop(0, target.shape[0], step=32)
    def _(r):
        at = pl.ds(pl.multiple_of(r, 32), 32)
        target[at] = (one[at].astype(F32) + two[at].astype(F32)).astype(BF)


class Chain:
    COLUMNS = 256
    SLOTS = {"own": 3, "in": 2, "cross": 2, "sum": 4, "total": 6}
    END_LAG = 5
    MID_LAG = 2
    INWARD = 2
    APART = 5
    ASIDE = 8

    @classmethod
    def layout(cls, arrays):
        chunks, rings = [], {}
        for a, (rows, columns, size, _) in enumerate(arrays):
            size, wide = math.gcd(rows, size), math.gcd(columns, cls.COLUMNS)
            rings[wide] = max(rings.get(wide, 0), size)
            chunks += [(a, r, size, c, wide) for r in range(0, rows, size) for c in range(0, columns, wide)]
        return chunks, rings

    @classmethod
    def scratch(cls, arrays):
        chunks, rings = cls.layout(arrays)
        return [pltpu.VMEM((k, rows, wide), BF) for wide, rows in rings.items() for k in cls.SLOTS.values()] + [
            pltpu.SemaphoreType.DMA((8, len(chunks))),
            pltpu.SemaphoreType.DMA((3, 3)),
            pltpu.SemaphoreType.DMA((len(chunks),)),
        ]

    def __init__(self, arrays, own, outs, landed, crossed, scratch):
        self.arrays, self.own, self.outs, self.landed, self.crossed = arrays, own, outs, landed, crossed
        self.chunks, rings = self.layout(arrays)
        scratch = list(scratch)
        self.rings = {wide: {name: scratch.pop(0) for name in self.SLOTS} for wide in rings}
        self.sems, self.load_sems, self.keep_sem = scratch
        self.n = len(self.chunks)
        self.x, self.z = lax.axis_index("dp"), lax.axis_index("blk")
        self.at_end = (self.z == 0) | (self.z == 3)
        self.inner = jnp.where(self.z == 0, 1, 2)
        self.outer = jnp.where(self.z == 1, 0, 3)

    def send(self, kind, c, src, dst, device):
        return pltpu.make_async_remote_copy(
            src, dst, self.sems.at[2 * kind, c], self.sems.at[2 * kind + 1, c],
            device_id=device, device_id_type=MESH,
        )

    def part(self, refs, c):
        a, r, rows, column, columns = self.chunks[c]
        return refs[a].at[pl.ds(r, rows), pl.ds(column, columns)]

    def final(self, c, half):
        a, r, rows, column, columns = self.chunks[c]
        return self.outs[a].at[half, pl.ds(r, rows), pl.ds(column, columns)]

    def slot(self, name, c):
        _, _, rows, _, columns = self.chunks[c]
        return self.rings[columns][name].at[c % self.SLOTS[name], pl.ds(0, rows)]

    def go_in(self, c):
        return self.send(0, c, self.part(self.own, c), self.part(self.landed, c), {"blk": self.inner})

    def arrive_in(self, c):
        ref = self.part(self.landed, c)
        return self.send(0, c, ref, ref, {"blk": self.outer})

    def go_mid(self, c):
        return self.send(1, c, self.slot("sum", c), self.part(self.crossed, c), {"blk": 3 - self.z})

    def go_out(self, c):
        return self.send(2, c, self.slot("total", c), self.final(c, self.x), {"blk": self.outer})

    def arrive_out(self, c):
        return self.send(2, c, self.final(c, self.x), self.final(c, self.x), {"blk": self.inner})

    def go_x(self, c, end):
        src = self.final(c, self.x) if end else self.slot("total", c)
        return self.send(3, c, src, self.final(c, self.x), {"dp": 1 - self.x})

    def arrive_x(self, c):
        ref = self.final(c, 1 - self.x)
        return self.send(3, c, ref, ref, {"dp": 1 - self.x})

    def load(self, name, refs, c):
        at = self.load_sems.at[list(self.SLOTS).index(name), c % self.SLOTS[name]]
        return pltpu.make_async_copy(self.part(refs, c), self.slot(name, c), at)

    def load_own(self, c):
        return self.load("own", self.own, c)

    def first_of(self, array):
        return [a for a, *_ in self.chunks].index(array)

    def in_hbm(self, c):
        return c < self.n and self.arrays[self.chunks[c][0]][3]

    def keep(self, c):
        return pltpu.make_async_copy(self.slot("total", c), self.final(c, self.x), self.keep_sem.at[c])

    @property
    def steps(self):
        return self.n + self.END_LAG

    def begin(self):
        @pl.when(self.at_end)
        def _():
            for c in range(min(self.INWARD, self.n)):
                self.go_in(c).start()

        @pl.when(jnp.logical_not(self.at_end))
        def _():
            for c in range(2):
                if self.in_hbm(c):
                    self.load_own(c).start()

    def sent(self, c):
        self.go_out(c).wait_send()
        if c < self.n - self.APART:
            self.go_x(c, False).wait_send()
        self.keep(c).wait()

    def step(self, c):
        n, slots = self.n, self.SLOTS

        @pl.when(self.at_end)
        def _():
            if c < n:
                self.go_in(c).wait_send()
                if c + self.INWARD < n:
                    self.go_in(c + self.INWARD).start()
            d = c - self.END_LAG
            if 0 <= d < n:
                self.arrive_out(d).wait_recv()
                if d >= self.ASIDE:
                    self.go_x(d - self.ASIDE, True).wait_send()
                if d < n - self.APART:
                    self.go_x(d, True).start()

        if c >= n + self.MID_LAG:
            return

        @pl.when(jnp.logical_not(self.at_end))
        def _():
            d = c - self.MID_LAG
            crossing = 0 <= d < n
            if c < n:
                if self.in_hbm(c + 2):
                    self.load_own(c + 2).start()
                self.arrive_in(c).wait_recv()
                self.load("in", self.landed, c).start()
            if crossing:
                self.go_mid(d).wait_recv()
                self.load("cross", self.crossed, d).start()
            if c < n:
                if self.in_hbm(c):
                    self.load_own(c).wait()
                    mine = self.slot("own", c)
                else:
                    mine = self.part(self.own, c)
                if c >= slots["sum"]:
                    self.go_mid(c - slots["sum"]).wait_send()
                self.load("in", self.landed, c).wait()
                add_rows(self.slot("sum", c), self.slot("in", c), mine)
                self.go_mid(c).start()
            if crossing:
                if d >= slots["total"]:
                    self.sent(d - slots["total"])
                self.load("cross", self.crossed, d).wait()
                add_rows(self.slot("total", d), self.slot("cross", d), self.slot("sum", d))
                self.go_out(d).start()
                if d < n - self.APART:
                    self.go_x(d, False).start()
                self.keep(d).start()

    def finish(self):
        n, slots = self.n, self.SLOTS

        @pl.when(self.at_end)
        def _():
            for c in range(max(0, n - self.ASIDE), n - self.APART):
                self.go_x(c, True).wait_send()

        @pl.when(jnp.logical_not(self.at_end))
        def _():
            for c in range(max(0, n - slots["sum"]), n):
                self.go_mid(c).wait_send()
            for c in range(max(0, n - slots["total"]), n):
                self.sent(c)

        for c in range(n - self.APART):
            self.arrive_x(c).wait_recv()


def greet(devices):
    barrier = pltpu.get_barrier_semaphore()
    for device in devices:
        pl.semaphore_signal(barrier, inc=1, device_id=device, device_id_type=MESH)
    pl.semaphore_wait(barrier, len(devices))


def turn(source, cos_t, sin_t):
    half = ROT // 2
    front_half, back_half = source[:half], source[half:ROT]
    return jnp.concatenate(
        [front_half * cos_t - back_half * sin_t, back_half * cos_t + front_half * sin_t, source[ROT:]], axis=0
    )


def attention_heads(
    first_head, heads, tile, land, cos_ref, sin_ref, start_ref, out, q_t, k_t, v_t, g_t, q_n, k_n, probs, dk_acc, dv_acc,
    between,
):
    total = land.shape[1]
    steps = total // tile
    scale = HD**-0.5
    hs = range(heads)

    def lanes(h):
        return slice((first_head + h) * HD, (first_head + h + 1) * HD)

    @pl.loop(0, steps)
    def _(i):
        place = pl.ds(pl.multiple_of(i * tile, tile), tile)
        cos_t, sin_t = cos_ref[:, place], sin_ref[:, place]
        for h in hs:
            x = turn(land[0, place, lanes(h)].astype(F32).T, cos_t, sin_t) * scale
            q_t[h, :, place] = x.astype(BF)
            q_n[h, place, :] = x.T.astype(BF)
            x = turn(land[1, place, lanes(h)].astype(F32).T, cos_t, sin_t)
            k_t[h, :, place] = x.astype(BF)
            k_n[h, place, :] = x.T.astype(BF)
            v_t[h, :, place] = land[2, place, lanes(h)].astype(F32).T.astype(BF)
            g_t[h, :, place] = land[3, place, lanes(h)].astype(F32).T.astype(BF)
            dk_acc[h, place, :] = jnp.zeros((tile, HD), F32)
            dv_acc[h, place, :] = jnp.zeros((tile, HD), F32)

    def one_tile(i):
        qs = pl.ds(pl.multiple_of(i * tile, tile), tile)
        start = start_ref[0:1, qs]
        queries = [q_t[h, :, qs] for h in hs]
        queries_n = [q_n[h, qs, :] for h in hs]
        cots = [g_t[h, :, qs] for h in hs]
        cots_n = [land[3, qs, lanes(h)] for h in hs]
        key_at = lax.broadcasted_iota(jnp.int32, (tile, tile), 0)
        query_at = lax.broadcasted_iota(jnp.int32, (tile, tile), 1)

        def score(j, tops, diagonal):
            first = pl.multiple_of(j * tile, tile)
            allowed = key_at >= (start - first)
            if diagonal:
                allowed = allowed & (key_at <= query_at)
            result = []
            for h in hs:
                s = dot32(k_n[h, pl.ds(first, tile), :], queries[h])
                s = jnp.where(allowed, s, NEGATIVE)
                probs[h, pl.ds(first, tile), :] = s
                result.append(jnp.maximum(tops[h], jnp.max(s, axis=0, keepdims=True)))
            return tuple(result)

        tops = tuple(jnp.full((1, tile), NEGATIVE, F32) for _ in hs)
        tops = lax.fori_loop(0, i, lambda j, c: score(j, c, False), tops)
        tops = score(i, tops, True)

        def mix(j, carry):
            sums, mixed = carry
            ks = pl.ds(pl.multiple_of(j * tile, tile), tile)
            new_sums, new_mixed = [], []
            for h in hs:
                p = jnp.exp(probs[h, ks, :] - tops[h])
                probs[h, ks, :] = p
                new_sums.append(sums[h] + jnp.sum(p, axis=0, keepdims=True))
                new_mixed.append(mixed[h] + dot32(v_t[h, :, ks], p.astype(BF)))
            return tuple(new_sums), tuple(new_mixed)

        zeros = tuple(jnp.zeros((1, tile), F32) for _ in hs)
        wide_zeros = tuple(jnp.zeros((HD, tile), F32) for _ in hs)
        sums, mixed = lax.fori_loop(0, i + 1, mix, (zeros, wide_zeros))
        inverse = [1.0 / sums[h] for h in hs]
        mixed = [mixed[h] * inverse[h] for h in hs]
        delta = [jnp.sum(mixed[h] * cots[h].astype(F32), axis=0, keepdims=True) for h in hs]

        def back(j, carry):
            ks = pl.ds(pl.multiple_of(j * tile, tile), tile)
            result = []
            for h in hs:
                p = probs[h, ks, :] * inverse[h]
                dp = dot32(land[2, ks, lanes(h)], cots[h])
                ds = (p * (dp - delta[h])).astype(BF)
                dv_acc[h, ks, :] += dot32(p.astype(BF), cots_n[h])
                dk_acc[h, ks, :] += dot32(ds, queries_n[h])
                result.append(carry[h] + dot32(k_t[h, :, ks], ds))
            return tuple(result)

        dq = lax.fori_loop(0, i + 1, back, wide_zeros)
        cos_t, sin_t = cos_ref[:, qs], sin_ref[:, qs]
        for h in hs:
            out[i, 0, :, lanes(h)] = turn(dq[h] * scale, cos_t, -sin_t).T.astype(BF)
            out[i, 3, :, lanes(h)] = mixed[h].T.astype(BF)

    @pl.loop(0, steps)
    def _(i):
        one_tile(i)
        between(i)

    @pl.loop(0, steps)
    def _(i):
        place = pl.ds(pl.multiple_of(i * tile, tile), tile)
        cos_t, sin_t = cos_ref[:, place], sin_ref[:, place]
        for h in hs:
            out[i, 1, :, lanes(h)] = turn(dk_acc[h, place, :].T, cos_t, -sin_t).T.astype(BF)
            out[i, 2, :, lanes(h)] = dv_acc[h, place, :].astype(BF)


def back_kernel(
    arrays, scatter, split, heads, tokens, land_ref, cos_ref, sin_ref, start_ref, g_ref, normed_ref, wq_ref, wo_ref,
    branch_ff, branch_y, d_hidden_ref, wu_ref, input_ref, grad_ref, stats_ref, gain_ref, out_bias_ref, down_bias_ref,
    ubias_ref, *refs,
):
    x, z, t = lax.axis_index("dp"), lax.axis_index("blk"), lax.axis_index("tensor")
    refs = list(refs)

    def take_refs(n):
        taken = refs[:n]
        del refs[:n]
        return taken

    own = take_refs(1)
    (home,) = take_refs(1)
    outs, landed, crossed = take_refs(4), take_refs(4), take_refs(4)
    up_part, dnorm_ff = take_refs(2)
    home_x, branch_y2, dnorm_y, sum_ff, over_x_ff, cross_ff = take_refs(6) if scatter else [None] * 6
    output_o, input_grad_o, small = take_refs(3) if scatter else [None] * 3
    out, dwo, dwq, load_sems, home_sems, home_keep, stage_sems = take_refs(7)
    give, take, take_y, tile_sems, scatter_sems, cross_sems = take_refs(6) if scatter else [None] * 6
    d_normed, moments, stats, small_in, norm_sems = take_refs(5) if scatter else [None] * 5
    nz, _, _, att = out.shape
    total = nz * tokens
    many, features = normed_ref.shape
    half, width = many // 2, features // 4
    rows = nz // 2
    groups = att // (heads * HD)
    peers = {"x": {"dp": 1 - x}, "y": {"tensor": flip(t, 2)}, "c": {"tensor": flip(t, 1)}}
    greet([{"blk": flip(z, m)} for m in range(1, nz)] + (list(peers.values()) if scatter else [peers["x"]]))
    work = Chain(arrays, own + [up_part, dwo, dwq], outs, landed, crossed, refs)
    work.begin()

    def remote(which, stage, src, dst, to):
        return pltpu.make_async_remote_copy(
            src, dst, scatter_sems.at[0, which, stage], scatter_sems.at[1, which, stage],
            device_id=peers[to], device_id_type=MESH,
        )

    if scatter:
        small[...] = jnp.zeros_like(small)
        ff = ubias_ref.shape[1]
        for r in range(ff // width):
            small[pl.ds(3 + x * (ff // width) + r, 1), :] = ubias_ref[0:1, r * width : (r + 1) * width]
        qkv_row = 3 + 2 * ff // width

    def branch_over_y():
        return remote(0, 0, branch_ff.at[1 - t // 2, pl.ds(half, half)], branch_y2, "y")

    def dnorm_over_y():
        return remote(1, 0, dnorm_ff.at[1 - t // 2], dnorm_y, "y")

    def ff_x(which):
        return remote(which, 1, sum_ff.at[which, pl.ds((1 - x) * half, half)], over_x_ff.at[which], "x")

    def add_ff(which):
        (dnorm_over_y if which else branch_over_y)().wait_recv()
        ours = (branch_ff, dnorm_ff)[which]
        size = half // 4

        def at(k):
            return pl.ds(k * size, size)

        def tile(i, k):
            n = 2 * i + k % 2
            return give.at[n // 4, at(n % 4)]

        def theirs(k):
            if which == 1:
                return dnorm_y.at[at(k)]
            return branch_y.at[at(k)] if k < 4 else branch_y2.at[at(k - 4)]

        def fetch(k):
            return [
                pltpu.make_async_copy(ours.at[t // 2, at(k)], tile(0, k), tile_sems.at[0, k % 2]),
                pltpu.make_async_copy(theirs(k), tile(1, k), tile_sems.at[1, k % 2]),
            ]

        def keep(k):
            return pltpu.make_async_copy(tile(2, k), sum_ff.at[which, at(k)], tile_sems.at[2, k % 2])

        blocks = many // size
        for copy in fetch(0):
            copy.start()
        for k in range(blocks):
            if k + 1 < blocks:
                for copy in fetch(k + 1):
                    copy.start()
            for copy in fetch(k):
                copy.wait()
            if k >= 2:
                keep(k - 2).wait()
            add_rows(tile(2, k), tile(0, k), tile(1, k))
            keep(k).start()
        for k in range(blocks - 2, blocks):
            keep(k).wait()
        ff_x(which).start()

    tn_dims = (((0,), (0,)), ((), ()))
    nt_dims = (((1,), (1,)), ((), ()))
    general = functools.partial(lax.dot_general, preferred_element_type=F32)
    at_step, ready = [0], [work.first_of(2)]

    def step():
        work.step(at_step[0])
        assert at_step[0] + work.INWARD < ready[0]
        at_step[0] += 1

    def spread(d_hidden, weight, normed, stage):
        ff = d_hidden.shape[1]
        part = features // 2
        wide = pl.ds(pl.multiple_of(x * ff, 128), ff)
        loads = [
            pltpu.make_async_copy(d_hidden_ref, d_hidden, load_sems.at[0, 0]),
            pltpu.make_async_copy(wu_ref.at[:, wide] if split else wu_ref, weight, load_sems.at[0, 1]),
        ] + [
            pltpu.make_async_copy(normed_ref.at[:, pl.ds(k * part, part)], normed.at[k], load_sems.at[1, k]) for k in range(2)
        ]
        for copy in loads:
            copy.start()
        loads[0].wait()
        loads[1].wait()

        def value(at, columns):
            return general(d_hidden[at, :], weight[columns, :], nt_dims)

        if scatter:
            core_share(cross_ff, stage, cross_sems, stage_sems, tokens, t, value, dnorm_ff, step)
            dnorm_over_y().start()
        else:
            for r in range(nz):
                at = pl.ds(r * tokens, tokens)
                for columns in range(0, features, 512):
                    stage[0, :, columns : columns + 512] = value(at, pl.ds(columns, 512)).astype(BF)
                copy = pltpu.make_async_copy(stage.at[0], dnorm_ff.at[at], stage_sems.at[0])
                copy.start()
                copy.wait()
        step()

        def keep(k, i):
            rows = pl.ds(pl.multiple_of(k * part + i * 256, 256), 256)
            return pltpu.make_async_copy(
                stage.at[i % 2, pl.ds(0, 256), pl.ds(0, ff)], up_part.at[rows], stage_sems.at[i % 2]
            )

        for k in range(2):
            loads[2 + k].wait()

            @pl.loop(0, part // 256)
            def _(i, k=k):
                @pl.when(i >= 2)
                def _():
                    keep(k, i - 2).wait()

                f = pl.ds(pl.multiple_of(i * 256, 256), 256)
                stage[i % 2, :256, :ff] = general(normed[k, :, f], d_hidden[...], tn_dims).astype(BF)
                keep(k, i).start()

            for i in range(part // 256 - 2, part // 256):
                keep(k, i).wait()
            step()

    if scatter:
        branch_over_y().start()
    pl.run_scoped(
        spread,
        pltpu.VMEM(d_hidden_ref.shape, BF),
        pltpu.VMEM((features, d_hidden_ref.shape[1]), BF),
        pltpu.VMEM((2, many, features // 2), BF),
        pltpu.VMEM((2, tokens, features), BF),
    )

    def lanes(p):
        return pl.ds(p * heads * HD, heads * HD)

    def home_copy(p, m, src, dst):
        return pltpu.make_async_remote_copy(
            src, dst, home_sems.at[0, p, m], home_sems.at[1, p, m], device_id={"blk": flip(z, m)}, device_id_type=MESH
        )

    def go_home(p, m):
        src = out.at[flip(z, m), :, :, lanes(p)]
        dst = home.at[:, z, :, lanes(p)]
        if m == 0:
            return pltpu.make_async_copy(src, dst, home_keep.at[p])
        return home_copy(p, m, src, dst)

    def arrive_home(p, m):
        ref = home.at[:, flip(z, m), :, lanes(p)]
        return home_copy(p, m, ref, ref)

    def attend(land, *scratch):
        load = pltpu.make_async_copy(land_ref, land, load_sems.at[0, 0])
        load.start()
        load.wait()
        for p in range(groups):
            plan = SCHEDULE[p] if p < len(SCHEDULE) else ()
            first = at_step[0]
            at_step[0] += sum(plan)

            def between(i, plan=plan, first=first):
                at = first
                for tile, steps in enumerate(plan):
                    if steps:

                        @pl.when(i == tile)
                        def _(at=at, steps=steps):
                            for c in range(at, at + steps):
                                work.step(c)

                    at += steps

            attention_heads(p * heads, heads, tokens, land, cos_ref, sin_ref, start_ref, out, *scratch, between)
            for m in (2, 3, 1, 0):
                go_home(p, m).start()
            if scatter:
                for which in (0, 1) if groups == 1 else (p,):
                    add_ff(which)

    pl.run_scoped(
        attend,
        pltpu.VMEM((4, total, att), BF),
        *[pltpu.VMEM((heads, HD, total), BF)] * 4,
        *[pltpu.VMEM((heads, total, HD), BF)] * 2,
        pltpu.VMEM((heads, total, tokens), F32),
        *[pltpu.VMEM((heads, total, HD), F32)] * 2,
    )
    def share_home(p):
        src, dst = home.at[:, pl.ds((1 - x) * rows, rows), :, lanes(p)], home_x.at[:, :, :, lanes(p)]
        return remote(p, 2, src, dst, "x")

    def come_home(p):
        for m in range(nz):
            if m == 0:
                go_home(p, m).wait()
            else:
                go_home(p, m).wait_send()
                arrive_home(p, m).wait_recv()
        if scatter:
            share_home(p).start()

    last = work.first_of(2) - work.INWARD - 2
    assert at_step[0] <= last - HOME_APART * (groups - 1)
    while at_step[0] <= last:
        for p in range(groups):
            if at_step[0] == last - HOME_APART * (groups - 1 - p):
                come_home(p)
        step()

    def over_core(which):
        return remote(which, 3, give, take.at[which], "c")

    def over_y(which):
        return remote(which, 4, take.at[which, 1 - t // 2], take_y.at[which], "y")

    def project(stream, hcat, hx, wcat, wo):
        def piece(i, r):
            at = pl.ds(r * tokens, tokens)
            return hcat.at[at, pl.ds(i * att, att)] if split else hcat.at[i, at]

        loads = [
            pltpu.make_async_copy(home.at[i, r], piece(i, r), load_sems.at[i, r])
            for i in (3, 0, 1, 2)
            for r in range(nz)
        ]
        weights = [] if not scatter else [
            pltpu.make_async_copy(
                wq_ref.at[i, :, pl.ds(pl.multiple_of(side * att, 128), att)],
                wcat.at[s, :, pl.ds(i * att, att)],
                load_sems.at[4 + s, i],
            )
            for s, side in enumerate((x, 1 - x))
            for i in range(3)
        ] + [
            pltpu.make_async_copy(wo_ref.at[pl.ds(side * att, att)], wo.at[s], load_sems.at[4 + s, 3])
            for s, side in enumerate((x, 1 - x))
        ]
        part = features // 2

        def streamed(k):
            source = g_ref if k < 2 else normed_ref
            return pltpu.make_async_copy(source.at[:, pl.ds((k % 2) * part, part)], stream.at[k % 2], load_sems.at[6, k % 2])

        for copy in loads[:4] + [streamed(0), streamed(1)] + loads[4:] + (weights if scatter else []):
            copy.start()
        step()
        for copy in loads:
            copy.wait()
        if split:
            attended = hcat[:, 3 * att :]
        else:
            d_qkv, attended = jnp.concatenate([hcat[i] for i in range(3)], axis=1), hcat[3]
        for k in range(2):
            streamed(k).wait()
            for j in range(part // width):
                value = general(attended, stream[k, :, j * width : (j + 1) * width], tn_dims)
                dwo[pl.ds((k * (part // width) + j) * att, att), :] = value.astype(BF)
            streamed(k + 2).start()
        ready[0] = work.first_of(3)
        for k in range(2):
            step()
            streamed(k + 2).wait()

            @pl.loop(0, part // 256)
            def _(j, k=k):
                f = pl.ds(pl.multiple_of(j * 256, 256), 256)
                value = general(stream[k, :, f], hcat[:, : 3 * att] if split else d_qkv, tn_dims).astype(BF)
                for i in range(3):
                    at = pl.multiple_of(i * features + k * part + j * 256, 256)
                    dwq[pl.ds(at, 256), :] = value[:, i * att : (i + 1) * att]

        ready[0] = work.n + work.steps
        if not scatter:
            return
        others = [
            pltpu.make_async_copy(
                home_x.at[i, r], hx.at[pl.ds(r * tokens, tokens), pl.ds(i * att, att)], load_sems.at[i, r]
            )
            for i in range(4)
            for r in range(rows)
        ]
        for p in range(groups):
            share_home(p).wait_recv()
        for copy in others:
            copy.start()
        for copy in weights + others:
            copy.wait()

        def share(which, of_core, target, plus):
            @pl.loop(0, 2 * rows)
            def _(k):
                v = k // rows
                columns = pl.ds(pl.multiple_of((2 * v + of_core) * width, width), width)
                at = pl.ds(pl.multiple_of((k % rows) * tokens, tokens), tokens)
                mine = pl.ds(pl.multiple_of(x * half + (k % rows) * tokens, tokens), tokens)
                if which == 0:
                    value = dot32(hcat[mine, 3 * att :], wo[0, :, columns]) + dot32(hx[at, 3 * att :], wo[1, :, columns])
                else:
                    value = general(hcat[mine, : 3 * att], wcat[0, columns, :], nt_dims)
                    value = value + general(hx[at, : 3 * att], wcat[1, columns, :], nt_dims)
                if plus:
                    value = value + target[v, at, :].astype(F32)
                target[v, at, :] = value.astype(BF)

        sums = jnp.sum(hcat[:, : 3 * att].astype(F32), axis=0, keepdims=True)
        for i in range(3):
            at = pl.ds(pl.multiple_of(x * att, 128), att)
            small[qkv_row + i : qkv_row + i + 1, at] = sums[:, i * att : (i + 1) * att]
        core = t % 2
        share(0, 1 - core, give, False)
        over_core(0).start()
        step()
        over_core(0).wait_send()
        share(1, 1 - core, give, False)
        over_core(1).start()
        step()
        for which in range(2):
            over_core(which).wait_recv()
            share(which, core, take.at[which], True)
            over_y(which).start()
            step()

    pl.run_scoped(
        project,
        pltpu.VMEM((2, many, features // 2), BF),
        pltpu.VMEM((many, 4 * att) if split else (4, many, att), BF),
        pltpu.VMEM((half, 4 * att), BF),
        pltpu.VMEM((2, features, 3 * att), BF),
        pltpu.VMEM((2, att, features), BF),
    )

    def load_to(refs):
        copies = [pltpu.make_async_copy(src, dst, tile_sems.at[i // 2, i % 2]) for i, (src, dst) in enumerate(refs)]
        for copy in copies:
            copy.start()
        for copy in copies:
            copy.wait()

    mine = pl.ds(x * half, half)
    spare = 1 - t // 2

    def total_share(which):
        over_y(which).wait_recv()
        over_y(which).wait_send()
        ff_x(which).wait_recv()
        load_to(
            [
                (sum_ff.at[which, mine], give.at[0]),
                (over_x_ff.at[which], give.at[1]),
                ((input_ref, grad_ref)[which], take.at[which, spare]),
            ]
            + ([(stats_ref.at[mine], stats)] if which else [])
        )

        def value(at):
            ff = give[0, at, :].astype(F32) + give[1, at, :].astype(F32)
            return ff + (take[which, t // 2, at, :].astype(F32) + take_y[which, at, :].astype(F32))

        return value

    def block_at(i):
        return pl.ds(pl.multiple_of(i * 128, 128), 128)

    def save(which):
        return pltpu.make_async_copy(take_y.at[which], (output_o, input_grad_o)[which], home_keep.at[which])

    def norm_copy(k, src, dst, device):
        return pltpu.make_async_remote_copy(
            src, dst, norm_sems.at[0, k], norm_sems.at[1, k], device_id=device, device_id_type=MESH
        )

    def exchange(k):
        return norm_copy(k, moments.at[2 * k], moments.at[2 * k + 1], peers["cy"[k]])

    def output():
        over_core(1).wait_send()
        value = total_share(0)

        @pl.loop(0, half // 128)
        def _(i):
            at = block_at(i)
            total = take[0, spare, at, :].astype(F32) + (value(at) + out_bias_ref[...] + down_bias_ref[...])
            take_y[0, at, :] = total.astype(BF)

        save(0).start()

    def own_gain():
        return gain_ref[:, pl.ds(pl.multiple_of(t * width, width), width)]

    def standardized(at):
        inverse = stats[at, 64:65]
        return (take[0, spare, at, :].astype(F32) - stats[at, 0:1]) * inverse, inverse

    def norm_sums():
        value = total_share(1)

        @pl.loop(0, half // 128)
        def _(i):
            at = block_at(i)
            d = value(at)
            d_normed[at, :] = d
            xhat, _ = standardized(at)
            scaled = d * own_gain()
            one = jnp.sum(scaled, axis=-1, keepdims=True)
            two = jnp.sum(scaled * xhat, axis=-1, keepdims=True)
            lane = lax.broadcasted_iota(jnp.int32, (128, 128), 1)
            moments[0, at, :] = jnp.where(lane < 64, one, two)
            small[0:1, :] += jnp.sum(d * xhat, axis=0, keepdims=True)
            small[1:2, :] += jnp.sum(d, axis=0, keepdims=True)
            small[2:3, :] += jnp.sum(take[1, spare, at, :].astype(F32), axis=0, keepdims=True)

        exchange(0).start()

    def norm_sums_core():
        exchange(0).wait()
        moments[2] = moments[0] + moments[1]
        exchange(1).start()

    def norm_back():
        exchange(1).wait()

        @pl.loop(0, half // 128)
        def _(i):
            at = block_at(i)
            total = (moments[2, at, :] + moments[3, at, :]) * (1.0 / features)
            xhat, inverse = standardized(at)
            scaled = d_normed[at, :] * own_gain()
            back = inverse * (scaled - total[:, 0:1] - xhat * total[:, 64:65])
            take_y[1, at, :] = (take[1, spare, at, :].astype(F32) + back).astype(BF)

        save(1).start()

    def small_sums(k):
        device = ({"dp": 1 - x}, {"blk": flip(z, 1)}, {"blk": flip(z, 2)})[k]
        copy = norm_copy(2 + k, small, small_in.at[k], device)
        copy.start()
        copy.wait()
        small[...] += small_in[k]

    stages = {
        "output": output, "norm_sums": norm_sums, "norm_sums_core": norm_sums_core, "norm_back": norm_back,
        "dp": functools.partial(small_sums, 0), "blk_1": functools.partial(small_sums, 1),
        "blk_2": functools.partial(small_sums, 2),
    }
    later = dict(LATER) if scatter else {}
    while at_step[0] < work.steps:
        for name in later.pop(at_step[0], ()):
            stages[name]()
        step()
    assert not later
    work.finish()
    if scatter:
        for which in range(2):
            ff_x(which).wait_send()
            save(which).wait()
        branch_over_y().wait_send()
        dnorm_over_y().wait_send()
        for p in range(groups):
            share_home(p).wait_send()


def weight_arrays(down, d_hidden, features, att):
    return [
        (*down, 1024, True), (features, d_hidden[1], 1024, True), (4 * att, features // 4, 1024, False),
        (3 * features, att, 512, False),
    ]


def back(
    scatter, split, tokens, land, cos_t, sin_t, start, cotangent, normed, wq, wo, branch_ff, branch_y, d_hidden, wu, down,
    block_input, grad_output, stats, gain, out_bias, down_bias, up_bias_part,
):
    _, total, att = land.shape
    nz = total // tokens
    many, features = normed.shape
    width, half = features // 4, many // 2
    heads = min(2, att // HD)
    groups = att // (heads * HD)
    ff = d_hidden.shape[1]
    arrays = weight_arrays(down.shape, d_hidden.shape, features, att)
    shapes = [a[:2] for a in arrays]
    hbm = pl.BlockSpec(memory_space=pl.ANY)
    vmem = pl.BlockSpec(memory_space=pltpu.VMEM)
    dma = pltpu.SemaphoreType.DMA
    scatter_scratch = [
        pltpu.VMEM((2, half, width), BF),
        pltpu.VMEM((2, 2, half, width), BF),
        pltpu.VMEM((2, half, width), BF),
        dma((3, 2)),
        dma((2, 2, 5)),
        dma((2, 2 * many // tokens)),
        pltpu.VMEM((half, width), F32),
        pltpu.VMEM((4, half, 128), F32),
        pltpu.VMEM((half, 128), F32),
        pltpu.VMEM((3, 16, width), F32),
        dma((2, 5)),
    ]
    scatter_outs = [
        jax.ShapeDtypeStruct((4, nz // 2, tokens, att), BF),
        jax.ShapeDtypeStruct((half, width), BF),
        jax.ShapeDtypeStruct((many, width), BF),
        jax.ShapeDtypeStruct((2, many, width), BF),
        jax.ShapeDtypeStruct((2, half, width), BF),
        jax.ShapeDtypeStruct((2, many, width), BF),
        jax.ShapeDtypeStruct((half, width), BF),
        jax.ShapeDtypeStruct((half, width), BF),
        jax.ShapeDtypeStruct((16, width), F32),
    ]
    results = pl.pallas_call(
        functools.partial(back_kernel, arrays, scatter, split, heads, tokens),
        out_shape=[jax.ShapeDtypeStruct((4, nz, tokens, att), BF)]
        + [jax.ShapeDtypeStruct((2,) + s, BF) for s in shapes]
        + [jax.ShapeDtypeStruct(s, BF) for s in shapes] * 2
        + [jax.ShapeDtypeStruct((features, ff), BF)]
        + [jax.ShapeDtypeStruct((2, many, width) if scatter else (many, features), BF)]
        + (scatter_outs if scatter else []),
        in_specs=[hbm] + [vmem] * 3 + [hbm] * 8 + [hbm] * 3 + [vmem] * 4 + [hbm],
        out_specs=[hbm] * 15 + ([hbm] * 8 + [vmem] if scatter else []),
        scratch_shapes=[
            pltpu.VMEM((nz, 4, tokens, att), BF),
            pltpu.VMEM(shapes[2], BF),
            pltpu.VMEM(shapes[3], BF),
            dma((7, 4)),
            dma((2, groups, nz)),
            dma((max(groups, 2),)),
            dma((4,)),
        ]
        + (scatter_scratch if scatter else [])
        + Chain.scratch(arrays),
        compiler_params=pltpu.CompilerParams(collective_id=3, has_side_effects=True, vmem_limit_bytes=60 << 20),
        cost_estimate=pl.CostEstimate(
            flops=12 * (att // HD) * total * total * HD * 4, bytes_accessed=1 << 29, transcendentals=0
        ),
        name="back",
    )(land, cos_t, sin_t, start, cotangent, normed, wq, wo, branch_ff, branch_y, d_hidden, wu, block_input, grad_output, stats,
      gain, out_bias, down_bias, up_bias_part, down)
    return results[0], results[1:5], results[14], results[21:]


def widen(source, out_shape, block, in_map, out_map, grid):
    def body(source_ref, out_ref):
        out_ref[...] = source_ref[0].astype(F32)

    return pl.pallas_call(
        body,
        out_shape=jax.ShapeDtypeStruct(out_shape, F32),
        grid=grid,
        in_specs=[pl.BlockSpec((1,) + block, in_map)],
        out_specs=pl.BlockSpec(block, out_map),
        compiler_params=pltpu.CompilerParams(vmem_limit_bytes=32 << 20),
        cost_estimate=pl.CostEstimate(flops=0, bytes_accessed=source.size * 6, transcendentals=0),
        name="widen",
    )(source)


def widen_rows(source):
    _, rows, columns = source.shape
    size = min(rows, (1 << 18) // columns)
    steps = rows // size
    return widen(
        source, (2 * rows, columns), (size, columns), lambda i, h: (h, i, 0), lambda i, h: (h * steps + i, 0), (steps, 2)
    )


def widen_columns(source):
    _, rows, columns = source.shape
    if columns % 128:
        return jnp.concatenate([source[0], source[1]], axis=1).astype(F32)
    size = min(rows, (1 << 18) // columns)
    return widen(
        source, (rows, 2 * columns), (size, columns), lambda i, h: (h, i, 0), lambda i, h: (i, h), (rows // size, 2)
    )


def widen_blocks(source):
    _, rows, columns = source.shape
    rows = rows // 4
    return widen(
        source, (2 * rows, 4 * columns), (rows, columns), lambda h, j: (h, j, 0), lambda h, j: (h, j), (2, 4)
    )


def scatter_sum(share):
    whole = lax.psum_scatter(share.astype(BF), "dp", scatter_dimension=0, tiled=True)
    return lax.psum_scatter(whole, "tensor", scatter_dimension=2, tiled=True).astype(F32)


def butterfly(value, axes):
    for axis, size in axes:
        mask = 1
        while mask < size:
            value = value + swap(value, axis, size, mask)
            mask *= 2
    return value


SCHEDULE = ((0, 1, 1, 1), (0, 1, 0, 1))
HOME_APART = 2
LATER = {26: ["output"], 28: ["norm_sums"], 29: ["norm_sums_core"], 31: ["norm_back"], 32: ["dp"], 33: ["blk_1"], 34: ["blk_2"]}


def local(
    nx, nz, nt, block_input, segment_ids, layer_norm_gain, layer_norm_bias, qkv_weight, qkv_bias, out_weight, out_bias,
    up_weight, up_bias, down_weight, down_bias, grad_output,
):
    rows, tokens, width = block_input.shape
    all_rows = nx * rows
    features = nt * width
    many = all_rows * tokens
    x, z, t = lax.axis_index("dp"), lax.axis_index("blk"), lax.axis_index("tensor")
    att = qkv_weight.shape[2] // nx
    ff = up_weight.shape[1] // nx

    split = att % 128 == 0
    gather = nt == 4 and nx == 2 and split
    qkv_whole = jnp.transpose(qkv_weight, (1, 0, 2))
    qkv_half = lax.dynamic_slice_in_dim(qkv_whole, x * att, att, 2)
    out_half = lax.dynamic_slice_in_dim(out_weight, x * att, att, 0)
    if split:
        weights = [qkv_whole, out_weight, up_weight, down_weight]
        first_biases = [qkv_bias.reshape(3, 1, nx * att), up_bias.reshape(1, nx * ff)]
    else:
        up_half = lax.dynamic_slice_in_dim(up_weight, x * ff, ff, 1)
        down_half = lax.dynamic_slice_in_dim(down_weight, x * ff, ff, 0)
        weights = [qkv_half, out_half, up_half, down_half]
        first_biases = [
            lax.dynamic_slice_in_dim(qkv_bias, x * att, att, 1).reshape(3, 1, att),
            lax.dynamic_slice_in_dim(up_bias, x * ff, ff, 0).reshape(1, ff),
        ]

    frequency = np.exp(np.arange(ROT // 2) * (-2.0 / ROT) * ROPE_LOG_BASE).astype(np.float32)[:, None]

    if gather:
        sources = [block_input.reshape(rows * tokens, width), grad_output.reshape(rows * tokens, width)]
    else:
        sources = [lax.all_gather(a, "tensor", axis=2, tiled=True) for a in (block_input, grad_output)]
        sources = [lax.all_gather(a, "dp", axis=0, tiled=True).reshape(many, features) for a in sources]
    normed, cotangent, land, stats, down_part, d_hidden, branch_ff, up_bias_part, cos_t, sin_t, start, branch_y = front(
        gather, split, rows, tokens, nz, many, features, att, ff,
        [
            segment_ids, jnp.asarray(frequency), *sources, layer_norm_gain.reshape(1, features), layer_norm_bias.reshape(1, features), weights[0],
            first_biases[0], weights[1], weights[2], first_biases[1], weights[3],
        ],
    )
    home, sums, d_normed_ff, results = back(
        gather, split, tokens, land, cos_t, sin_t, start, cotangent, normed, weights[0], weights[1], branch_ff, branch_y,
        d_hidden, weights[2], down_part, block_input.reshape(rows * tokens, width),
        grad_output.reshape(rows * tokens, width), stats, layer_norm_gain.reshape(1, features), out_bias.reshape(1, width),
        down_bias.reshape(1, width), up_bias_part,
    )
    down_sum, up_sum, out_sum, qkv_sum = sums
    chunks = Chain.layout(weight_arrays(down_part.shape, d_hidden.shape, features, att))[0][-Chain.APART :]
    first = chunks[0][1]
    last_rows = lax.dynamic_slice(qkv_sum, (x, first, 0), (1, 3 * features - first, att))
    last_rows = lax.ppermute(last_rows, "dp", [(0, 1), (1, 0)])
    qkv_sum = lax.dynamic_update_slice(qkv_sum, last_rows, (1 - x, first, 0))
    if gather:
        block_output, input_grad, small = results
        block_output = block_output.reshape(rows, tokens, width)
        input_grad = input_grad.reshape(rows, tokens, width)
        gain_grad, shift_grad, bias_grad = small[0], small[1], small[2]
        units = nx * ff // width
        up_bias_grad = small[3 : 3 + units].reshape(nx * ff)
        qkv_bias_grad = small[3 + units : 6 + units]
    else:
        home = home.reshape(4, many, att)
        qkv_bias_part = jnp.sum(home[:3].astype(F32), axis=1)
        branch = branch_ff.astype(F32) + dot32(home[3], out_half)
        d_normed = d_normed_ff.astype(F32)
        for i in range(3):
            d_normed = d_normed + dot32(home[i], qkv_half[i].T)
        branch = scatter_sum(branch.reshape(all_rows, tokens, features))
        d_normed = scatter_sum(d_normed.reshape(all_rows, tokens, features))
        block_output = (block_input.astype(F32) + (branch + out_bias + down_bias)).astype(BF)

        stats = lax.dynamic_slice_in_dim(stats, x * rows * tokens, rows * tokens, 0).reshape(rows, tokens, 128)
        own_mean, own_inverse = stats[..., :1], stats[..., 64:65]
        xhat = (block_input.astype(F32) - own_mean) * own_inverse
        gain = lax.dynamic_slice_in_dim(layer_norm_gain, t * width, width, 0)
        scaled = d_normed * gain
        moments = jnp.stack([jnp.sum(scaled, axis=-1), jnp.sum(scaled * xhat, axis=-1)])
        moments = butterfly(moments, [("tensor", nt)]) / features
        first, second = moments[0][..., None], moments[1][..., None]
        input_grad = (
            grad_output.astype(F32) + own_inverse * (scaled - first - xhat * second)
        ).astype(BF)

        def spread(part, whole):
            shape = part.shape[:-1] + (whole,)
            at = (0,) * (part.ndim - 1) + (x * part.shape[-1],)
            return lax.dynamic_update_slice(jnp.zeros(shape, F32), part, at)

        small = [
            jnp.sum(d_normed * xhat, axis=(0, 1)),
            jnp.sum(d_normed, axis=(0, 1)),
            jnp.sum(grad_output.astype(F32), axis=(0, 1)),
            spread(up_bias_part[0], nx * ff),
            spread(qkv_bias_part, nx * att).reshape(-1),
        ]
        packed = butterfly(jnp.concatenate(small), [("dp", nx), ("blk", nz)])
        gain_grad, shift_grad, bias_grad = (packed[i * width : (i + 1) * width] for i in range(3))
        up_bias_grad = packed[3 * width : 3 * width + nx * ff]
        qkv_bias_grad = packed[3 * width + nx * ff :].reshape(3, nx * att)

    down_grad = widen_rows(down_sum)
    up_grad = widen_columns(up_sum)
    out_grad = widen_blocks(out_sum)
    qkv_grad = widen_columns(qkv_sum).reshape(3, features, nx * att)
    qkv_grad = jnp.transpose(qkv_grad, (1, 0, 2))
    return (
        block_output, input_grad, gain_grad, shift_grad, qkv_grad, qkv_bias_grad, out_grad, bias_grad, up_grad,
        up_bias_grad, down_grad, bias_grad,
    )


def solution(mesh):
    in_specs = (
        P("dp", "blk", "tensor"), P("dp", None), P(), P(), P(None, None, "tensor"), P(None, "tensor"), P("tensor", None),
        P("tensor"), P(None, "tensor"), P("tensor"), P("tensor", None), P("tensor"), P("dp", "blk", "tensor"),
    )
    out_specs = (
        P("dp", "blk", "tensor"), P("dp", "blk", "tensor"), P("tensor"), P("tensor"), P(None, None, "tensor"),
        P(None, "tensor"), P("tensor", None), P("tensor"), P(None, "tensor"), P("tensor"), P("tensor", None), P("tensor"),
    )
    body = functools.partial(local, mesh.shape["dp"], mesh.shape["blk"], mesh.shape["tensor"])
    return jax.shard_map(body, mesh=mesh, in_specs=in_specs, out_specs=out_specs, check_vma=False)
```

```python
import functools
import math

import jax
import jax.numpy as jnp
import numpy as np
from jax import lax
from jax.experimental import pallas as pl
from jax.experimental.pallas import tpu as pltpu
from jax.sharding import PartitionSpec as P

HD = 64
ROT = 32
EPSILON = 1e-05
ROPE_LOG_BASE = math.log(10000.0)
NEGATIVE = -1e30
F32 = jnp.float32
BF = jnp.bfloat16
MESH = pl.DeviceIdType.MESH
dot32 = functools.partial(jnp.dot, preferred_element_type=F32)


def swap(value, axis, size, mask):
    return lax.ppermute(value, axis, [(i, i ^ mask) for i in range(size)])


def flip(index, mask):
    if mask == 0:
        return index
    if mask == 1:
        return index + 1 - 2 * (index % 2)
    if mask == 2:
        return (index + 2) % 4
    return 3 - index


def core_share(cross_ref, stage, cross_sems, stage_sems, tokens, t, value, out, between=None):
    _, many, width = out.shape
    blocks = many // tokens
    core = t % 2

    def place(k):
        return pl.ds(pl.multiple_of((k % blocks) * tokens, tokens), tokens)

    def tile(slot, k):
        return stage.at[k % 2, :, pl.ds(slot * width, width)]

    def at(ref, k):
        return ref.at[k // blocks, place(k)]

    def columns(k, of_core):
        return pl.ds(pl.multiple_of((2 * (k // blocks) + of_core) * width, width), width)

    def cross(k, src, dst):
        return pltpu.make_async_remote_copy(
            src, dst, cross_sems.at[0, k], cross_sems.at[1, k], device_id={"tensor": flip(t, 1)}, device_id_type=MESH
        )

    def give(k):
        return cross(k, tile(0, k), at(cross_ref, k))

    def got(k):
        return cross(k, at(cross_ref, k), at(cross_ref, k))

    def fetch(k):
        return pltpu.make_async_copy(at(cross_ref, k), tile(1, k), stage_sems.at[k % 2])

    def keep(k):
        return pltpu.make_async_copy(tile(2, k), at(out, k), stage_sems.at[2 + k % 2])

    @pl.loop(0, 2 * blocks)
    def _(k):
        @pl.when(k >= 2)
        def _():
            give(k - 2).wait_send()

        stage[k % 2, :, :width] = value(place(k), columns(k, 1 - core)).astype(BF)
        give(k).start()

    for k in (2 * blocks - 2, 2 * blocks - 1):
        give(k).wait_send()
    if between:
        between()
    got(0).wait_recv()
    fetch(0).start()

    @pl.loop(0, 2 * blocks)
    def _(k):
        @pl.when(k >= 2)
        def _():
            keep(k - 2).wait()

        @pl.when(k + 1 < 2 * blocks)
        def _():
            got(k + 1).wait_recv()
            fetch(k + 1).start()

        mine = value(place(k), columns(k, core))
        fetch(k).wait()
        stage[k % 2, :, 2 * width : 3 * width] = (mine + stage[k % 2, :, width : 2 * width].astype(F32)).astype(BF)
        keep(k).start()

    for k in (2 * blocks - 2, 2 * blocks - 1):
        keep(k).wait()


def front_kernel(
    gather, split, rows, tokens, segments_ref, frequency_ref, x_own, g_own, gain_ref, shift_ref, wq_ref, bq_ref, wo_ref, wu_ref, bu_ref, wd_ref,
    normed_o, g_o, land_o, stats_o, down_o, d_hidden_o, branch_o, ubias_o, cos_o, sin_o, start_o, branch_y_o, cross_o,
    xin, gin, vq, vo, vu, vd, pay, act, slope, stage, gather_sems, land_sems, load_sems, keep_sems, stage_sems, cross_sems, over_y_sems, segments, segment_sems,
):
    x, z, t = lax.axis_index("dp"), lax.axis_index("blk"), lax.axis_index("tensor")
    many, features = xin.shape
    half = rows * tokens
    width = features // 4
    att = vq.shape[2]
    ff = vu.shape[1]
    nz = pay.shape[0]
    wide = min(512, ff)

    def remote(src, dst, sems, device):
        return pltpu.make_async_remote_copy(
            src, dst, sems[0], sems[1], device_id=device, device_id_type=MESH
        )

    peers = {"x": {"dp": 1 - x}, "y": {"tensor": flip(t, 2)}, "c": {"tensor": flip(t, 1)}}
    barrier = pltpu.get_barrier_semaphore()
    greet = [{"blk": flip(z, m)} for m in range(1, nz)] + (list(peers.values()) if gather else [peers["x"]])
    for device in greet:
        pl.semaphore_signal(barrier, inc=1, device_id=device, device_id_type=MESH)

    loads = [
        pltpu.make_async_copy(
            wq_ref.at[:, :, pl.ds(pl.multiple_of(x * att, 128), att)] if split else wq_ref, vq, load_sems.at[0]
        ),
        pltpu.make_async_copy(
            wu_ref.at[:, pl.ds(pl.multiple_of(x * ff, 128), ff)] if split else wu_ref, vu, load_sems.at[1]
        ),
        pltpu.make_async_copy(wd_ref.at[pl.ds(x * ff, ff)] if split else wd_ref, vd, load_sems.at[2]),
        pltpu.make_async_copy(wo_ref.at[pl.ds(x * att, att)] if split else wo_ref, vo, load_sems.at[3]),
    ]
    if not gather:
        both = [
            pltpu.make_async_copy(x_own, xin, load_sems.at[4]),
            pltpu.make_async_copy(g_own, gin, load_sems.at[5]),
        ]
    else:
        both = [
            pltpu.make_async_copy(
                own,
                buf.at[pl.ds(x * half, half), pl.ds(pl.multiple_of(t * width, 128), width)],
                load_sems.at[4 + i],
            )
            for i, (own, buf) in enumerate([(x_own, xin), (g_own, gin)])
        ]
    both[0].start()
    both[1].start()
    pl.semaphore_wait(barrier, len(greet))

    class Gather:
        def __init__(self, which, own, buf, first, size):
            self.which, self.own, self.buf, self.names = which, own, buf, []
            self.base, self.size = first, size

        def at(self, dx, dt, r):
            return self.buf.at[
                pl.ds(pl.multiple_of((1 - x if dx else x) * half + self.base + r * self.size, self.size), self.size),
                pl.ds(pl.multiple_of(flip(t, dt) * width, 128), width),
            ]

        plan = {
            "x": (0, 0, "x", 1, 0), "y": (0, 0, "y", 0, 2), "c": (0, 0, "c", 0, 1),
            "ex": (1, 0, "c", 1, 1), "ey": (0, 2, "c", 0, 3), "ed": (1, 2, "c", 1, 3),
        }

        def sems(self, kind, r):
            k = 2 * ("x", "y", "c", "d", "ex", "ey", "ed").index(kind) + r
            return gather_sems.at[self.which, 0, k], gather_sems.at[self.which, 1, k]

        def copy(self, kind, r):
            if kind == "d":
                dx, dt, to = (1, 0, "y") if r == 0 else (0, 2, "x")
            else:
                dx, dt, to = self.plan[kind][:3]
            src = dst = self.at(dx, dt, r)
            if kind in "xyc":
                src = self.own.at[pl.ds(self.base + r * self.size, self.size)]
            return remote(src, dst, self.sems(kind, r), peers[to])

        def start(self, kind, r):
            self.names.append((kind, r))
            self.copy(kind, r).start()

        def wait(self, kind, r):
            if kind == "d":
                dx, dt, to = 1, 2, "y"
            else:
                to, dx, dt = self.plan[kind][2:]
            ref = self.at(dx, dt, r)
            remote(ref, ref, self.sems(kind, r), peers[to]).wait_recv()

        def begin(self):
            for kind, r in (("x", 0), ("y", 1), ("x", 1), ("y", 0), ("c", 0), ("c", 1)):
                self.start(kind, r)

        def second(self):
            self.wait("x", 0)
            self.start("d", 0)
            self.start("ex", 0)
            self.wait("y", 1)
            self.start("d", 1)
            self.start("ey", 1)

        def third(self):
            self.wait("x", 1)
            self.start("ex", 1)
            self.wait("y", 0)
            self.start("ey", 0)

        def fourth(self):
            self.wait("d", 0)
            self.start("ed", 0)
            self.wait("d", 1)
            self.start("ed", 1)

        def last(self):
            for kind in ("c", "ex", "ey", "ed"):
                for r in range(2):
                    self.wait(kind, r)

        def drain(self):
            for kind, r in self.names:
                self.copy(kind, r).wait_send()

    ins = [Gather(r, x_own, xin, r * tokens, tokens // 2) for r in range(rows)]
    cots = Gather(rows, g_own, gin, 0, half // 2)
    own_segments = pltpu.make_async_copy(segments_ref, segments.at[x], segment_sems.at[0])
    own_segments.start()
    segments_x = remote(segments_ref, segments.at[x], (segment_sems.at[1], segment_sems.at[2]), peers["x"])
    segments_x.start()
    if gather:
        ins[0].begin()
    for load in loads:
        load.start()

    own_segments.wait()
    segments_x.wait()
    ids = segments[z // rows]
    length = ids.shape[1]
    ids = jnp.sum(jnp.where(lax.broadcasted_iota(jnp.int32, ids.shape, 0) == z % rows, ids, 0), axis=0, keepdims=True)
    ids = jnp.broadcast_to(ids, (8, length))
    at = lax.broadcasted_iota(jnp.int32, (8, length), 1)
    first_of = jnp.where(ids != pltpu.roll(ids, 1, 1), at, 0)
    reach = 1
    while reach < length:
        first_of = jnp.maximum(first_of, jnp.where(at >= reach, pltpu.roll(first_of, reach, 1), 0))
        reach *= 2
    start_o[...] = first_of
    angles = frequency_ref[...] * (at - first_of)[0:1].astype(F32)
    cos_o[...] = jnp.cos(angles)
    sin_o[...] = jnp.sin(angles)

    def place(position):
        return pl.ds(pl.multiple_of(position * tokens, tokens), tokens)

    def normalize(row):
        @pl.loop(0, tokens // 128)
        def _(i):
            at = pl.ds(pl.multiple_of(row * tokens + i * 128, 128), 128)
            v = xin[at, :].astype(F32)
            mean = jnp.sum(v, axis=-1, keepdims=True) * (1.0 / features)
            v = v - mean
            inverse = lax.rsqrt(jnp.sum(v * v, axis=-1, keepdims=True) * (1.0 / features) + EPSILON)
            xin[at, :] = (v * inverse * gain_ref[...] + shift_ref[...]).astype(BF)
            lane = lax.broadcasted_iota(jnp.int32, (128, 128), 1)
            stats_o[at, :] = jnp.where(lane < 64, mean, inverse)

    def parts(kind):
        return pl.ds(0, 3) if kind == 0 else pl.ds(3, 1)

    def sems(kind, m):
        return land_sems.at[0, kind, m], land_sems.at[1, kind, m]

    def own_row(kind):
        return pltpu.make_async_copy(
            pay.at[z, parts(kind)], land_o.at[parts(kind), place(z)], keep_sems.at[2 + kind]
        )

    def other_row(kind, row, m):
        return remote(pay.at[row, parts(kind)], land_o.at[parts(kind), place(z)], sems(kind, m), {"blk": row})

    def send(kind, row):
        @pl.when(z == row)
        def _():
            own_row(kind).start()

        @pl.when(z != row)
        def _():
            other_row(kind, row, flip(z, row)).start()

    def landed(kind, m):
        ref = land_o.at[parts(kind), place(flip(z, m))]
        return remote(ref, ref, sems(kind, m), {"blk": flip(z, m)})

    def project(row):
        @pl.loop(0, 3)
        def _(part):
            lanes = pl.ds(pl.multiple_of(x * att, 128), att) if split else slice(None)
            bias = bq_ref[pl.ds(part, 1), lanes]
            value = dot32(xin[place(row), :], vq[part]) + bias
            pay[row, part] = value.astype(BF)

        send(0, row)

    if gather:
        ins[0].second()
        ins[0].third()
        ins[1].begin()
        ins[0].fourth()
    both[0].wait()
    for r in range(rows):
        if gather:
            ins[r].last()
            ins[r].drain()
        for row in range(r, nz, rows):
            normalize(row)
        if gather and r == 0:
            ins[1].second()
        if r == 0:
            loads[0].wait()
        for row in range(r, nz, rows):
            project(row)
        if gather and r == 0:
            ins[1].third()
            cots.begin()
            ins[1].fourth()
    keep_normed = pltpu.make_async_copy(xin, normed_o, keep_sems.at[0])
    keep_normed.start()
    if gather:
        cots.second()

    loads[1].wait()

    @pl.loop(0, many // tokens)
    def _(i):
        at = place(i)

        @pl.loop(0, ff // wide)
        def _(j):
            columns = pl.ds(pl.multiple_of(j * wide, wide), wide)
            first = x * ff if split else 0
            h = dot32(xin[at, :], vu[:, columns]) + bu_ref[:, pl.ds(pl.multiple_of(first + j * wide, wide), wide)]
            c = math.sqrt(2.0 / math.pi)
            square = h * h
            tanh = jnp.tanh(c * h * (1.0 + 0.044715 * square))
            one = 0.5 * (1.0 + tanh)
            act[at, columns] = (h * one).astype(BF)
            d = one + 0.5 * h * (1.0 - tanh * tanh) * (c * (1.0 + 3 * 0.044715 * square))
            slope[at, columns] = d.astype(BF)

    if gather:
        cots.third()
    nt_dims = (((1,), (1,)), ((), ()))
    tn_dims = (((0,), (0,)), ((), ()))
    general = functools.partial(lax.dot_general, preferred_element_type=F32)

    def through(steps, rows_of, columns_of, make, out):
        def copy(i):
            return pltpu.make_async_copy(
                stage.at[i % 2, pl.ds(0, rows_of), pl.ds(0, columns_of)],
                out.at[pl.ds(pl.multiple_of(i * rows_of, rows_of), rows_of)],
                stage_sems.at[i % 2],
            )

        @pl.loop(0, steps)
        def _(i):
            @pl.when(i >= 2)
            def _():
                copy(i - 2).wait()

            make(i, stage.at[i % 2, pl.ds(0, rows_of), pl.ds(0, columns_of)])
            copy(i).start()

        for i in range(max(0, steps - 2), steps):
            copy(i).wait()

    loads[2].wait()
    if gather:
        core_share(
            cross_o, stage, cross_sems, stage_sems, tokens, t,
            lambda at, columns: dot32(act[at, :], vd[:, columns]), branch_o,
        )
        branch_over_y = remote(
            branch_o.at[1 - t // 2, pl.ds(0, half)], branch_y_o, (over_y_sems.at[0], over_y_sems.at[1]), peers["y"]
        )
        branch_over_y.start()
    else:

        def whole(i, target):
            @pl.loop(0, features // 512)
            def _(j):
                columns = pl.ds(pl.multiple_of(j * 512, 512), 512)
                target[:, columns] = dot32(act[place(i), :], vd[:, columns]).astype(BF)

        through(many // tokens, tokens, features, whole, branch_o)

    if gather:
        cots.fourth()
    both[1].wait()
    if gather:
        cots.last()
    keep_g = pltpu.make_async_copy(gin, g_o, keep_sems.at[1])
    keep_g.start()

    loads[3].wait()
    for row in range(nz):
        pay[row, 3] = general(gin[place(row), :], vo[...], nt_dims).astype(BF)
        send(1, row)

    ubias_o[...] = jnp.zeros_like(ubias_o)

    @pl.loop(0, many // tokens)
    def _(i):
        at = place(i)

        @pl.loop(0, ff // wide)
        def _(j):
            columns = pl.ds(pl.multiple_of(j * wide, wide), wide)
            d = general(gin[at, :], vd[columns, :], nt_dims) * slope[at, columns].astype(F32)
            d = d.astype(BF)
            slope[at, columns] = d
            ubias_o[0:1, columns] += jnp.sum(d.astype(F32), axis=0, keepdims=True)

    keep_d = pltpu.make_async_copy(slope, d_hidden_o, keep_sems.at[4])
    keep_d.start()

    def down_tile(i, target):
        f = pl.ds(pl.multiple_of(i * 256, 256), 256)
        for j in range(0, features, 1024):
            target[:, j : j + 1024] = general(act[:, f], gin[:, j : j + 1024], tn_dims).astype(BF)

    through(ff // 256, 256, features, down_tile, down_o)

    keep_normed.wait()
    keep_g.wait()
    keep_d.wait()
    for kind in range(2):
        own_row(kind).wait()
        for m in range(1, nz):
            other_row(kind, flip(z, m), m).wait_send()
            landed(kind, m).wait_recv()
    if gather:
        cots.drain()
        branch_over_y.wait()


def front(gather, split, rows, tokens, nz, many, features, att, ff, operands):
    hbm = pl.BlockSpec(memory_space=pl.ANY)
    vmem = pl.BlockSpec(memory_space=pltpu.VMEM)
    shares = (2, many, features // 4) if gather else (many, features)
    return pl.pallas_call(
        functools.partial(front_kernel, gather, split, rows, tokens),
        out_shape=[
            jax.ShapeDtypeStruct((many, features), BF),
            jax.ShapeDtypeStruct((many, features), BF),
            jax.ShapeDtypeStruct((4, nz * tokens, att), BF),
            jax.ShapeDtypeStruct((many, 128), F32),
            jax.ShapeDtypeStruct((ff, features), BF),
            jax.ShapeDtypeStruct((many, ff), BF),
            jax.ShapeDtypeStruct(shares, BF),
            jax.ShapeDtypeStruct((8, ff), F32),
            jax.ShapeDtypeStruct((ROT // 2, nz * tokens), F32),
            jax.ShapeDtypeStruct((ROT // 2, nz * tokens), F32),
            jax.ShapeDtypeStruct((8, nz * tokens), jnp.int32),
            jax.ShapeDtypeStruct((many // 2, features // 4), BF),
            jax.ShapeDtypeStruct((2, many, features // 4), BF),
        ],
        in_specs=[hbm, vmem, hbm, hbm, vmem, vmem, hbm, vmem, hbm, hbm, vmem, hbm],
        out_specs=[hbm, hbm, hbm, vmem, hbm, hbm, hbm, vmem, vmem, vmem, vmem, hbm, hbm],
        scratch_shapes=[
            pltpu.VMEM((many, features), BF),
            pltpu.VMEM((many, features), BF),
            pltpu.VMEM((3, features, att), BF),
            pltpu.VMEM((att, features), BF),
            pltpu.VMEM((features, ff), BF),
            pltpu.VMEM((ff, features), BF),
            pltpu.VMEM((nz, 4, tokens, att), BF),
            pltpu.VMEM((many, ff), BF),
            pltpu.VMEM((many, ff), BF),
            pltpu.VMEM((2, tokens, features), BF),
            pltpu.SemaphoreType.DMA((rows + 1, 2, 14)),
            pltpu.SemaphoreType.DMA((2, 2, 4)),
            pltpu.SemaphoreType.DMA((6,)),
            pltpu.SemaphoreType.DMA((5,)),
            pltpu.SemaphoreType.DMA((4,)),
            pltpu.SemaphoreType.DMA((2, 2 * many // tokens)),
            pltpu.SemaphoreType.DMA((2,)),
            pltpu.VMEM((2, rows, nz * tokens), jnp.int32),
            pltpu.SemaphoreType.DMA((3,)),
        ],
        compiler_params=pltpu.CompilerParams(
            collective_id=2, has_side_effects=True, vmem_limit_bytes=60 << 20
        ),
        cost_estimate=pl.CostEstimate(
            flops=2 * many * features * (6 * ff + 4 * att), bytes_accessed=100 << 20, transcendentals=0
        ),
        name="front",
    )(*operands)[:12]


def add_rows(target, one, two):
    @pl.loop(0, target.shape[0], step=32)
    def _(r):
        at = pl.ds(pl.multiple_of(r, 32), 32)
        target[at] = (one[at].astype(F32) + two[at].astype(F32)).astype(BF)


class Chain:
    COLUMNS = 256
    SLOTS = {"own": 3, "in": 2, "cross": 2, "sum": 4, "total": 6}
    END_LAG = 5
    MID_LAG = 2
    INWARD = 2
    APART = 5
    ASIDE = 8

    @classmethod
    def layout(cls, arrays):
        chunks, rings = [], {}
        for a, (rows, columns, size, _) in enumerate(arrays):
            size, wide = math.gcd(rows, size), math.gcd(columns, cls.COLUMNS)
            rings[wide] = max(rings.get(wide, 0), size)
            chunks += [(a, r, size, c, wide) for r in range(0, rows, size) for c in range(0, columns, wide)]
        return chunks, rings

    @classmethod
    def scratch(cls, arrays):
        chunks, rings = cls.layout(arrays)
        return [pltpu.VMEM((k, rows, wide), BF) for wide, rows in rings.items() for k in cls.SLOTS.values()] + [
            pltpu.SemaphoreType.DMA((8, len(chunks))),
            pltpu.SemaphoreType.DMA((3, 3)),
            pltpu.SemaphoreType.DMA((len(chunks),)),
        ]

    def __init__(self, arrays, own, outs, landed, crossed, scratch):
        self.arrays, self.own, self.outs, self.landed, self.crossed = arrays, own, outs, landed, crossed
        self.chunks, rings = self.layout(arrays)
        scratch = list(scratch)
        self.rings = {wide: {name: scratch.pop(0) for name in self.SLOTS} for wide in rings}
        self.sems, self.load_sems, self.keep_sem = scratch
        self.n = len(self.chunks)
        self.x, self.z = lax.axis_index("dp"), lax.axis_index("blk")
        self.at_end = (self.z == 0) | (self.z == 3)
        self.inner = jnp.where(self.z == 0, 1, 2)
        self.outer = jnp.where(self.z == 1, 0, 3)

    def send(self, kind, c, src, dst, device):
        return pltpu.make_async_remote_copy(
            src, dst, self.sems.at[2 * kind, c], self.sems.at[2 * kind + 1, c],
            device_id=device, device_id_type=MESH,
        )

    def part(self, refs, c):
        a, r, rows, column, columns = self.chunks[c]
        return refs[a].at[pl.ds(r, rows), pl.ds(column, columns)]

    def final(self, c, half):
        a, r, rows, column, columns = self.chunks[c]
        return self.outs[a].at[half, pl.ds(r, rows), pl.ds(column, columns)]

    def slot(self, name, c):
        _, _, rows, _, columns = self.chunks[c]
        return self.rings[columns][name].at[c % self.SLOTS[name], pl.ds(0, rows)]

    def go_in(self, c):
        return self.send(0, c, self.part(self.own, c), self.part(self.landed, c), {"blk": self.inner})

    def arrive_in(self, c):
        ref = self.part(self.landed, c)
        return self.send(0, c, ref, ref, {"blk": self.outer})

    def go_mid(self, c):
        return self.send(1, c, self.slot("sum", c), self.part(self.crossed, c), {"blk": 3 - self.z})

    def go_out(self, c):
        return self.send(2, c, self.slot("total", c), self.final(c, self.x), {"blk": self.outer})

    def arrive_out(self, c):
        return self.send(2, c, self.final(c, self.x), self.final(c, self.x), {"blk": self.inner})

    def go_x(self, c, end):
        src = self.final(c, self.x) if end else self.slot("total", c)
        return self.send(3, c, src, self.final(c, self.x), {"dp": 1 - self.x})

    def arrive_x(self, c):
        ref = self.final(c, 1 - self.x)
        return self.send(3, c, ref, ref, {"dp": 1 - self.x})

    def load(self, name, refs, c):
        at = self.load_sems.at[list(self.SLOTS).index(name), c % self.SLOTS[name]]
        return pltpu.make_async_copy(self.part(refs, c), self.slot(name, c), at)

    def load_own(self, c):
        return self.load("own", self.own, c)

    def first_of(self, array):
        return [a for a, *_ in self.chunks].index(array)

    def in_hbm(self, c):
        return c < self.n and self.arrays[self.chunks[c][0]][3]

    def keep(self, c):
        return pltpu.make_async_copy(self.slot("total", c), self.final(c, self.x), self.keep_sem.at[c])

    @property
    def steps(self):
        return self.n + self.END_LAG

    def begin(self):
        @pl.when(self.at_end)
        def _():
            for c in range(min(self.INWARD, self.n)):
                self.go_in(c).start()

        @pl.when(jnp.logical_not(self.at_end))
        def _():
            for c in range(2):
                if self.in_hbm(c):
                    self.load_own(c).start()

    def sent(self, c):
        self.go_out(c).wait_send()
        if c < self.n - self.APART:
            self.go_x(c, False).wait_send()
        self.keep(c).wait()

    def step(self, c):
        n, slots = self.n, self.SLOTS

        @pl.when(self.at_end)
        def _():
            if c < n:
                self.go_in(c).wait_send()
                if c + self.INWARD < n:
                    self.go_in(c + self.INWARD).start()
            d = c - self.END_LAG
            if 0 <= d < n:
                self.arrive_out(d).wait_recv()
                if d >= self.ASIDE:
                    self.go_x(d - self.ASIDE, True).wait_send()
                if d < n - self.APART:
                    self.go_x(d, True).start()

        if c >= n + self.MID_LAG:
            return

        @pl.when(jnp.logical_not(self.at_end))
        def _():
            d = c - self.MID_LAG
            crossing = 0 <= d < n
            if c < n:
                if self.in_hbm(c + 2):
                    self.load_own(c + 2).start()
                self.arrive_in(c).wait_recv()
                self.load("in", self.landed, c).start()
            if crossing:
                self.go_mid(d).wait_recv()
                self.load("cross", self.crossed, d).start()
            if c < n:
                if self.in_hbm(c):
                    self.load_own(c).wait()
                    mine = self.slot("own", c)
                else:
                    mine = self.part(self.own, c)
                if c >= slots["sum"]:
                    self.go_mid(c - slots["sum"]).wait_send()
                self.load("in", self.landed, c).wait()
                add_rows(self.slot("sum", c), self.slot("in", c), mine)
                self.go_mid(c).start()
            if crossing:
                if d >= slots["total"]:
                    self.sent(d - slots["total"])
                self.load("cross", self.crossed, d).wait()
                add_rows(self.slot("total", d), self.slot("cross", d), self.slot("sum", d))
                self.go_out(d).start()
                if d < n - self.APART:
                    self.go_x(d, False).start()
                self.keep(d).start()

    def finish(self):
        n, slots = self.n, self.SLOTS

        @pl.when(self.at_end)
        def _():
            for c in range(max(0, n - self.ASIDE), n - self.APART):
                self.go_x(c, True).wait_send()

        @pl.when(jnp.logical_not(self.at_end))
        def _():
            for c in range(max(0, n - slots["sum"]), n):
                self.go_mid(c).wait_send()
            for c in range(max(0, n - slots["total"]), n):
                self.sent(c)

        for c in range(n - self.APART):
            self.arrive_x(c).wait_recv()


def greet(devices):
    barrier = pltpu.get_barrier_semaphore()
    for device in devices:
        pl.semaphore_signal(barrier, inc=1, device_id=device, device_id_type=MESH)
    pl.semaphore_wait(barrier, len(devices))


def turn(source, cos_t, sin_t):
    half = ROT // 2
    front_half, back_half = source[:half], source[half:ROT]
    return jnp.concatenate(
        [front_half * cos_t - back_half * sin_t, back_half * cos_t + front_half * sin_t, source[ROT:]], axis=0
    )


def attention_heads(
    first_head, heads, tile, land, cos_ref, sin_ref, start_ref, out, q_t, k_t, v_t, g_t, q_n, k_n, probs, dk_acc, dv_acc,
    between,
):
    total = land.shape[1]
    steps = total // tile
    scale = HD**-0.5
    hs = range(heads)

    def lanes(h):
        return slice((first_head + h) * HD, (first_head + h + 1) * HD)

    @pl.loop(0, steps)
    def _(i):
        place = pl.ds(pl.multiple_of(i * tile, tile), tile)
        cos_t, sin_t = cos_ref[:, place], sin_ref[:, place]
        for h in hs:
            x = turn(land[0, place, lanes(h)].astype(F32).T, cos_t, sin_t) * scale
            q_t[h, :, place] = x.astype(BF)
            q_n[h, place, :] = x.T.astype(BF)
            x = turn(land[1, place, lanes(h)].astype(F32).T, cos_t, sin_t)
            k_t[h, :, place] = x.astype(BF)
            k_n[h, place, :] = x.T.astype(BF)
            v_t[h, :, place] = land[2, place, lanes(h)].astype(F32).T.astype(BF)
            g_t[h, :, place] = land[3, place, lanes(h)].astype(F32).T.astype(BF)
            dk_acc[h, place, :] = jnp.zeros((tile, HD), F32)
            dv_acc[h, place, :] = jnp.zeros((tile, HD), F32)

    def one_tile(i):
        qs = pl.ds(pl.multiple_of(i * tile, tile), tile)
        start = start_ref[0:1, qs]
        queries = [q_t[h, :, qs] for h in hs]
        queries_n = [q_n[h, qs, :] for h in hs]
        cots = [g_t[h, :, qs] for h in hs]
        cots_n = [land[3, qs, lanes(h)] for h in hs]
        key_at = lax.broadcasted_iota(jnp.int32, (tile, tile), 0)
        query_at = lax.broadcasted_iota(jnp.int32, (tile, tile), 1)

        def score(j, tops, diagonal):
            first = pl.multiple_of(j * tile, tile)
            allowed = key_at >= (start - first)
            if diagonal:
                allowed = allowed & (key_at <= query_at)
            result = []
            for h in hs:
                s = dot32(k_n[h, pl.ds(first, tile), :], queries[h])
                s = jnp.where(allowed, s, NEGATIVE)
                probs[h, pl.ds(first, tile), :] = s
                result.append(jnp.maximum(tops[h], jnp.max(s, axis=0, keepdims=True)))
            return tuple(result)

        tops = tuple(jnp.full((1, tile), NEGATIVE, F32) for _ in hs)
        tops = lax.fori_loop(0, i, lambda j, c: score(j, c, False), tops)
        tops = score(i, tops, True)

        def mix(j, carry):
            sums, mixed = carry
            ks = pl.ds(pl.multiple_of(j * tile, tile), tile)
            new_sums, new_mixed = [], []
            for h in hs:
                p = jnp.exp(probs[h, ks, :] - tops[h])
                probs[h, ks, :] = p
                new_sums.append(sums[h] + jnp.sum(p, axis=0, keepdims=True))
                new_mixed.append(mixed[h] + dot32(v_t[h, :, ks], p.astype(BF)))
            return tuple(new_sums), tuple(new_mixed)

        zeros = tuple(jnp.zeros((1, tile), F32) for _ in hs)
        wide_zeros = tuple(jnp.zeros((HD, tile), F32) for _ in hs)
        sums, mixed = lax.fori_loop(0, i + 1, mix, (zeros, wide_zeros))
        inverse = [1.0 / sums[h] for h in hs]
        mixed = [mixed[h] * inverse[h] for h in hs]
        delta = [jnp.sum(mixed[h] * cots[h].astype(F32), axis=0, keepdims=True) for h in hs]

        def back(j, carry):
            ks = pl.ds(pl.multiple_of(j * tile, tile), tile)
            result = []
            for h in hs:
                p = probs[h, ks, :] * inverse[h]
                dp = dot32(land[2, ks, lanes(h)], cots[h])
                ds = (p * (dp - delta[h])).astype(BF)
                dv_acc[h, ks, :] += dot32(p.astype(BF), cots_n[h])
                dk_acc[h, ks, :] += dot32(ds, queries_n[h])
                result.append(carry[h] + dot32(k_t[h, :, ks], ds))
            return tuple(result)

        dq = lax.fori_loop(0, i + 1, back, wide_zeros)
        cos_t, sin_t = cos_ref[:, qs], sin_ref[:, qs]
        for h in hs:
            out[i, 0, :, lanes(h)] = turn(dq[h] * scale, cos_t, -sin_t).T.astype(BF)
            out[i, 3, :, lanes(h)] = mixed[h].T.astype(BF)

    @pl.loop(0, steps)
    def _(i):
        one_tile(i)
        between(i)

    @pl.loop(0, steps)
    def _(i):
        place = pl.ds(pl.multiple_of(i * tile, tile), tile)
        cos_t, sin_t = cos_ref[:, place], sin_ref[:, place]
        for h in hs:
            out[i, 1, :, lanes(h)] = turn(dk_acc[h, place, :].T, cos_t, -sin_t).T.astype(BF)
            out[i, 2, :, lanes(h)] = dv_acc[h, place, :].astype(BF)


def back_kernel(
    arrays, scatter, split, heads, tokens, land_ref, cos_ref, sin_ref, start_ref, g_ref, normed_ref, wq_ref, wo_ref,
    branch_ff, branch_y, d_hidden_ref, wu_ref, input_ref, grad_ref, stats_ref, gain_ref, out_bias_ref, down_bias_ref,
    ubias_ref, *refs,
):
    x, z, t = lax.axis_index("dp"), lax.axis_index("blk"), lax.axis_index("tensor")
    refs = list(refs)

    def take_refs(n):
        taken = refs[:n]
        del refs[:n]
        return taken

    own = take_refs(1)
    (home,) = take_refs(1)
    outs, landed, crossed = take_refs(4), take_refs(4), take_refs(4)
    up_part, dnorm_ff = take_refs(2)
    home_x, branch_y2, dnorm_y, sum_ff, over_x_ff, cross_ff = take_refs(6) if scatter else [None] * 6
    output_o, input_grad_o, small = take_refs(3) if scatter else [None] * 3
    out, dwo, dwq, load_sems, home_sems, home_keep, stage_sems = take_refs(7)
    give, take, take_y, tile_sems, scatter_sems, cross_sems = take_refs(6) if scatter else [None] * 6
    d_normed, moments, stats, small_in, norm_sems = take_refs(5) if scatter else [None] * 5
    nz, _, _, att = out.shape
    total = nz * tokens
    many, features = normed_ref.shape
    half, width = many // 2, features // 4
    rows = nz // 2
    groups = att // (heads * HD)
    peers = {"x": {"dp": 1 - x}, "y": {"tensor": flip(t, 2)}, "c": {"tensor": flip(t, 1)}}
    greet([{"blk": flip(z, m)} for m in range(1, nz)] + (list(peers.values()) if scatter else [peers["x"]]))
    work = Chain(arrays, own + [up_part, dwo, dwq], outs, landed, crossed, refs)
    work.begin()

    def remote(which, stage, src, dst, to):
        return pltpu.make_async_remote_copy(
            src, dst, scatter_sems.at[0, which, stage], scatter_sems.at[1, which, stage],
            device_id=peers[to], device_id_type=MESH,
        )

    if scatter:
        small[...] = jnp.zeros_like(small)
        ff = ubias_ref.shape[1]
        for r in range(ff // width):
            small[pl.ds(3 + x * (ff // width) + r, 1), :] = ubias_ref[0:1, r * width : (r + 1) * width]
        qkv_row = 3 + 2 * ff // width

    def branch_over_y():
        return remote(0, 0, branch_ff.at[1 - t // 2, pl.ds(half, half)], branch_y2, "y")

    def dnorm_over_y():
        return remote(1, 0, dnorm_ff.at[1 - t // 2], dnorm_y, "y")

    def ff_x(which):
        return remote(which, 1, sum_ff.at[which, pl.ds((1 - x) * half, half)], over_x_ff.at[which], "x")

    def add_ff(which):
        (dnorm_over_y if which else branch_over_y)().wait_recv()
        ours = (branch_ff, dnorm_ff)[which]
        size = half // 4

        def at(k):
            return pl.ds(k * size, size)

        def tile(i, k):
            n = 2 * i + k % 2
            return give.at[n // 4, at(n % 4)]

        def theirs(k):
            if which == 1:
                return dnorm_y.at[at(k)]
            return branch_y.at[at(k)] if k < 4 else branch_y2.at[at(k - 4)]

        def fetch(k):
            return [
                pltpu.make_async_copy(ours.at[t // 2, at(k)], tile(0, k), tile_sems.at[0, k % 2]),
                pltpu.make_async_copy(theirs(k), tile(1, k), tile_sems.at[1, k % 2]),
            ]

        def keep(k):
            return pltpu.make_async_copy(tile(2, k), sum_ff.at[which, at(k)], tile_sems.at[2, k % 2])

        blocks = many // size
        for copy in fetch(0):
            copy.start()
        for k in range(blocks):
            if k + 1 < blocks:
                for copy in fetch(k + 1):
                    copy.start()
            for copy in fetch(k):
                copy.wait()
            if k >= 2:
                keep(k - 2).wait()
            add_rows(tile(2, k), tile(0, k), tile(1, k))
            keep(k).start()
        for k in range(blocks - 2, blocks):
            keep(k).wait()
        ff_x(which).start()

    tn_dims = (((0,), (0,)), ((), ()))
    nt_dims = (((1,), (1,)), ((), ()))
    general = functools.partial(lax.dot_general, preferred_element_type=F32)
    at_step, ready = [0], [work.first_of(2)]

    def step():
        work.step(at_step[0])
        assert at_step[0] + work.INWARD < ready[0]
        at_step[0] += 1

    def spread(d_hidden, weight, normed, stage):
        ff = d_hidden.shape[1]
        part = features // 2
        wide = pl.ds(pl.multiple_of(x * ff, 128), ff)
        loads = [
            pltpu.make_async_copy(d_hidden_ref, d_hidden, load_sems.at[0, 0]),
            pltpu.make_async_copy(wu_ref.at[:, wide] if split else wu_ref, weight, load_sems.at[0, 1]),
        ] + [
            pltpu.make_async_copy(normed_ref.at[:, pl.ds(k * part, part)], normed.at[k], load_sems.at[1, k]) for k in range(2)
        ]
        for copy in loads:
            copy.start()
        loads[0].wait()
        loads[1].wait()

        def value(at, columns):
            return general(d_hidden[at, :], weight[columns, :], nt_dims)

        if scatter:
            core_share(cross_ff, stage, cross_sems, stage_sems, tokens, t, value, dnorm_ff, step)
            dnorm_over_y().start()
        else:
            for r in range(nz):
                at = pl.ds(r * tokens, tokens)
                for columns in range(0, features, 512):
                    stage[0, :, columns : columns + 512] = value(at, pl.ds(columns, 512)).astype(BF)
                copy = pltpu.make_async_copy(stage.at[0], dnorm_ff.at[at], stage_sems.at[0])
                copy.start()
                copy.wait()
        step()

        def keep(k, i):
            rows = pl.ds(pl.multiple_of(k * part + i * 256, 256), 256)
            return pltpu.make_async_copy(
                stage.at[i % 2, pl.ds(0, 256), pl.ds(0, ff)], up_part.at[rows], stage_sems.at[i % 2]
            )

        for k in range(2):
            loads[2 + k].wait()

            @pl.loop(0, part // 256)
            def _(i, k=k):
                @pl.when(i >= 2)
                def _():
                    keep(k, i - 2).wait()

                f = pl.ds(pl.multiple_of(i * 256, 256), 256)
                stage[i % 2, :256, :ff] = general(normed[k, :, f], d_hidden[...], tn_dims).astype(BF)
                keep(k, i).start()

            for i in range(part // 256 - 2, part // 256):
                keep(k, i).wait()
            step()

    if scatter:
        branch_over_y().start()
    pl.run_scoped(
        spread,
        pltpu.VMEM(d_hidden_ref.shape, BF),
        pltpu.VMEM((features, d_hidden_ref.shape[1]), BF),
        pltpu.VMEM((2, many, features // 2), BF),
        pltpu.VMEM((2, tokens, features), BF),
    )

    def lanes(p):
        return pl.ds(p * heads * HD, heads * HD)

    def home_copy(p, m, src, dst):
        return pltpu.make_async_remote_copy(
            src, dst, home_sems.at[0, p, m], home_sems.at[1, p, m], device_id={"blk": flip(z, m)}, device_id_type=MESH
        )

    def go_home(p, m):
        src = out.at[flip(z, m), :, :, lanes(p)]
        dst = home.at[:, z, :, lanes(p)]
        if m == 0:
            return pltpu.make_async_copy(src, dst, home_keep.at[p])
        return home_copy(p, m, src, dst)

    def arrive_home(p, m):
        ref = home.at[:, flip(z, m), :, lanes(p)]
        return home_copy(p, m, ref, ref)

    def attend(land, *scratch):
        load = pltpu.make_async_copy(land_ref, land, load_sems.at[0, 0])
        load.start()
        load.wait()
        for p in range(groups):
            plan = SCHEDULE[p] if p < len(SCHEDULE) else ()
            first = at_step[0]
            at_step[0] += sum(plan)

            def between(i, plan=plan, first=first):
                at = first
                for tile, steps in enumerate(plan):
                    if steps:

                        @pl.when(i == tile)
                        def _(at=at, steps=steps):
                            for c in range(at, at + steps):
                                work.step(c)

                    at += steps

            attention_heads(p * heads, heads, tokens, land, cos_ref, sin_ref, start_ref, out, *scratch, between)
            for m in (2, 3, 1, 0):
                go_home(p, m).start()
            if scatter:
                for which in (0, 1) if groups == 1 else (p,):
                    add_ff(which)

    pl.run_scoped(
        attend,
        pltpu.VMEM((4, total, att), BF),
        *[pltpu.VMEM((heads, HD, total), BF)] * 4,
        *[pltpu.VMEM((heads, total, HD), BF)] * 2,
        pltpu.VMEM((heads, total, tokens), F32),
        *[pltpu.VMEM((heads, total, HD), F32)] * 2,
    )
    def share_home(p):
        src, dst = home.at[:, pl.ds((1 - x) * rows, rows), :, lanes(p)], home_x.at[:, :, :, lanes(p)]
        return remote(p, 2, src, dst, "x")

    def come_home(p):
        for m in range(nz):
            if m == 0:
                go_home(p, m).wait()
            else:
                go_home(p, m).wait_send()
                arrive_home(p, m).wait_recv()
        if scatter:
            share_home(p).start()

    last = work.first_of(2) - work.INWARD - 2
    assert at_step[0] <= last - HOME_APART * (groups - 1)
    while at_step[0] <= last:
        for p in range(groups):
            if at_step[0] == last - HOME_APART * (groups - 1 - p):
                come_home(p)
        step()

    def over_core(which):
        return remote(which, 3, give, take.at[which], "c")

    def over_y(which):
        return remote(which, 4, take.at[which, 1 - t // 2], take_y.at[which], "y")

    def project(stream, hcat, hx, wcat, wo):
        def piece(i, r):
            at = pl.ds(r * tokens, tokens)
            return hcat.at[at, pl.ds(i * att, att)] if split else hcat.at[i, at]

        loads = [
            pltpu.make_async_copy(home.at[i, r], piece(i, r), load_sems.at[i, r])
            for i in (3, 0, 1, 2)
            for r in range(nz)
        ]
        weights = [] if not scatter else [
            pltpu.make_async_copy(
                wq_ref.at[i, :, pl.ds(pl.multiple_of(side * att, 128), att)],
                wcat.at[s, :, pl.ds(i * att, att)],
                load_sems.at[4 + s, i],
            )
            for s, side in enumerate((x, 1 - x))
            for i in range(3)
        ] + [
            pltpu.make_async_copy(wo_ref.at[pl.ds(side * att, att)], wo.at[s], load_sems.at[4 + s, 3])
            for s, side in enumerate((x, 1 - x))
        ]
        part = features // 2

        def streamed(k):
            source = g_ref if k < 2 else normed_ref
            return pltpu.make_async_copy(source.at[:, pl.ds((k % 2) * part, part)], stream.at[k % 2], load_sems.at[6, k % 2])

        for copy in loads[:4] + [streamed(0), streamed(1)] + loads[4:] + (weights if scatter else []):
            copy.start()
        step()
        for copy in loads:
            copy.wait()
        if split:
            attended = hcat[:, 3 * att :]
        else:
            d_qkv, attended = jnp.concatenate([hcat[i] for i in range(3)], axis=1), hcat[3]
        for k in range(2):
            streamed(k).wait()
            for j in range(part // width):
                value = general(attended, stream[k, :, j * width : (j + 1) * width], tn_dims)
                dwo[pl.ds((k * (part // width) + j) * att, att), :] = value.astype(BF)
            streamed(k + 2).start()
        ready[0] = work.first_of(3)
        for k in range(2):
            step()
            streamed(k + 2).wait()

            @pl.loop(0, part // 256)
            def _(j, k=k):
                f = pl.ds(pl.multiple_of(j * 256, 256), 256)
                value = general(stream[k, :, f], hcat[:, : 3 * att] if split else d_qkv, tn_dims).astype(BF)
                for i in range(3):
                    at = pl.multiple_of(i * features + k * part + j * 256, 256)
                    dwq[pl.ds(at, 256), :] = value[:, i * att : (i + 1) * att]

        ready[0] = work.n + work.steps
        if not scatter:
            return
        others = [
            pltpu.make_async_copy(
                home_x.at[i, r], hx.at[pl.ds(r * tokens, tokens), pl.ds(i * att, att)], load_sems.at[i, r]
            )
            for i in range(4)
            for r in range(rows)
        ]
        for p in range(groups):
            share_home(p).wait_recv()
        for copy in others:
            copy.start()
        for copy in weights + others:
            copy.wait()

        def share(which, of_core, target, plus):
            @pl.loop(0, 2 * rows)
            def _(k):
                v = k // rows
                columns = pl.ds(pl.multiple_of((2 * v + of_core) * width, width), width)
                at = pl.ds(pl.multiple_of((k % rows) * tokens, tokens), tokens)
                mine = pl.ds(pl.multiple_of(x * half + (k % rows) * tokens, tokens), tokens)
                if which == 0:
                    value = dot32(hcat[mine, 3 * att :], wo[0, :, columns]) + dot32(hx[at, 3 * att :], wo[1, :, columns])
                else:
                    value = general(hcat[mine, : 3 * att], wcat[0, columns, :], nt_dims)
                    value = value + general(hx[at, : 3 * att], wcat[1, columns, :], nt_dims)
                if plus:
                    value = value + target[v, at, :].astype(F32)
                target[v, at, :] = value.astype(BF)

        sums = jnp.sum(hcat[:, : 3 * att].astype(F32), axis=0, keepdims=True)
        for i in range(3):
            at = pl.ds(pl.multiple_of(x * att, 128), att)
            small[qkv_row + i : qkv_row + i + 1, at] = sums[:, i * att : (i + 1) * att]
        core = t % 2
        share(0, 1 - core, give, False)
        over_core(0).start()
        step()
        over_core(0).wait_send()
        share(1, 1 - core, give, False)
        over_core(1).start()
        step()
        for which in range(2):
            over_core(which).wait_recv()
            share(which, core, take.at[which], True)
            over_y(which).start()
            step()

    pl.run_scoped(
        project,
        pltpu.VMEM((2, many, features // 2), BF),
        pltpu.VMEM((many, 4 * att) if split else (4, many, att), BF),
        pltpu.VMEM((half, 4 * att), BF),
        pltpu.VMEM((2, features, 3 * att), BF),
        pltpu.VMEM((2, att, features), BF),
    )

    def load_to(refs):
        copies = [pltpu.make_async_copy(src, dst, tile_sems.at[i // 2, i % 2]) for i, (src, dst) in enumerate(refs)]
        for copy in copies:
            copy.start()
        for copy in copies:
            copy.wait()

    mine = pl.ds(x * half, half)
    spare = 1 - t // 2

    def total_share(which):
        over_y(which).wait_recv()
        over_y(which).wait_send()
        ff_x(which).wait_recv()
        load_to(
            [
                (sum_ff.at[which, mine], give.at[0]),
                (over_x_ff.at[which], give.at[1]),
                ((input_ref, grad_ref)[which], take.at[which, spare]),
            ]
            + ([(stats_ref.at[mine], stats)] if which else [])
        )

        def value(at):
            ff = give[0, at, :].astype(F32) + give[1, at, :].astype(F32)
            return ff + (take[which, t // 2, at, :].astype(F32) + take_y[which, at, :].astype(F32))

        return value

    def block_at(i):
        return pl.ds(pl.multiple_of(i * 128, 128), 128)

    def save(which):
        return pltpu.make_async_copy(take_y.at[which], (output_o, input_grad_o)[which], home_keep.at[which])

    def norm_copy(k, src, dst, device):
        return pltpu.make_async_remote_copy(
            src, dst, norm_sems.at[0, k], norm_sems.at[1, k], device_id=device, device_id_type=MESH
        )

    def exchange(k):
        return norm_copy(k, moments.at[2 * k], moments.at[2 * k + 1], peers["cy"[k]])

    def output():
        over_core(1).wait_send()
        value = total_share(0)

        @pl.loop(0, half // 128)
        def _(i):
            at = block_at(i)
            total = take[0, spare, at, :].astype(F32) + (value(at) + out_bias_ref[...] + down_bias_ref[...])
            take_y[0, at, :] = total.astype(BF)

        save(0).start()

    def own_gain():
        return gain_ref[:, pl.ds(pl.multiple_of(t * width, width), width)]

    def standardized(at):
        inverse = stats[at, 64:65]
        return (take[0, spare, at, :].astype(F32) - stats[at, 0:1]) * inverse, inverse

    def norm_sums():
        value = total_share(1)

        @pl.loop(0, half // 128)
        def _(i):
            at = block_at(i)
            d = value(at)
            d_normed[at, :] = d
            xhat, _ = standardized(at)
            scaled = d * own_gain()
            one = jnp.sum(scaled, axis=-1, keepdims=True)
            two = jnp.sum(scaled * xhat, axis=-1, keepdims=True)
            lane = lax.broadcasted_iota(jnp.int32, (128, 128), 1)
            moments[0, at, :] = jnp.where(lane < 64, one, two)
            small[0:1, :] += jnp.sum(d * xhat, axis=0, keepdims=True)
            small[1:2, :] += jnp.sum(d, axis=0, keepdims=True)
            small[2:3, :] += jnp.sum(take[1, spare, at, :].astype(F32), axis=0, keepdims=True)

        exchange(0).start()

    def norm_sums_core():
        exchange(0).wait()
        moments[2] = moments[0] + moments[1]
        exchange(1).start()

    def norm_back():
        exchange(1).wait()

        @pl.loop(0, half // 128)
        def _(i):
            at = block_at(i)
            total = (moments[2, at, :] + moments[3, at, :]) * (1.0 / features)
            xhat, inverse = standardized(at)
            scaled = d_normed[at, :] * own_gain()
            back = inverse * (scaled - total[:, 0:1] - xhat * total[:, 64:65])
            take_y[1, at, :] = (take[1, spare, at, :].astype(F32) + back).astype(BF)

        save(1).start()

    def small_sums(k):
        device = ({"dp": 1 - x}, {"blk": flip(z, 1)}, {"blk": flip(z, 2)})[k]
        copy = norm_copy(2 + k, small, small_in.at[k], device)
        copy.start()
        copy.wait()
        small[...] += small_in[k]

    stages = {
        "output": output, "norm_sums": norm_sums, "norm_sums_core": norm_sums_core, "norm_back": norm_back,
        "dp": functools.partial(small_sums, 0), "blk_1": functools.partial(small_sums, 1),
        "blk_2": functools.partial(small_sums, 2),
    }
    later = dict(LATER) if scatter else {}
    while at_step[0] < work.steps:
        for name in later.pop(at_step[0], ()):
            stages[name]()
        step()
    assert not later
    work.finish()
    if scatter:
        for which in range(2):
            ff_x(which).wait_send()
            save(which).wait()
        branch_over_y().wait_send()
        dnorm_over_y().wait_send()
        for p in range(groups):
            share_home(p).wait_send()


def weight_arrays(down, d_hidden, features, att):
    return [
        (*down, 1024, True), (features, d_hidden[1], 1024, True), (4 * att, features // 4, 1024, False),
        (3 * features, att, 512, False),
    ]


def back(
    scatter, split, tokens, land, cos_t, sin_t, start, cotangent, normed, wq, wo, branch_ff, branch_y, d_hidden, wu, down,
    block_input, grad_output, stats, gain, out_bias, down_bias, up_bias_part,
):
    _, total, att = land.shape
    nz = total // tokens
    many, features = normed.shape
    width, half = features // 4, many // 2
    heads = min(2, att // HD)
    groups = att // (heads * HD)
    ff = d_hidden.shape[1]
    arrays = weight_arrays(down.shape, d_hidden.shape, features, att)
    shapes = [a[:2] for a in arrays]
    hbm = pl.BlockSpec(memory_space=pl.ANY)
    vmem = pl.BlockSpec(memory_space=pltpu.VMEM)
    dma = pltpu.SemaphoreType.DMA
    scatter_scratch = [
        pltpu.VMEM((2, half, width), BF),
        pltpu.VMEM((2, 2, half, width), BF),
        pltpu.VMEM((2, half, width), BF),
        dma((3, 2)),
        dma((2, 2, 5)),
        dma((2, 2 * many // tokens)),
        pltpu.VMEM((half, width), F32),
        pltpu.VMEM((4, half, 128), F32),
        pltpu.VMEM((half, 128), F32),
        pltpu.VMEM((3, 16, width), F32),
        dma((2, 5)),
    ]
    scatter_outs = [
        jax.ShapeDtypeStruct((4, nz // 2, tokens, att), BF),
        jax.ShapeDtypeStruct((half, width), BF),
        jax.ShapeDtypeStruct((many, width), BF),
        jax.ShapeDtypeStruct((2, many, width), BF),
        jax.ShapeDtypeStruct((2, half, width), BF),
        jax.ShapeDtypeStruct((2, many, width), BF),
        jax.ShapeDtypeStruct((half, width), BF),
        jax.ShapeDtypeStruct((half, width), BF),
        jax.ShapeDtypeStruct((16, width), F32),
    ]
    results = pl.pallas_call(
        functools.partial(back_kernel, arrays, scatter, split, heads, tokens),
        out_shape=[jax.ShapeDtypeStruct((4, nz, tokens, att), BF)]
        + [jax.ShapeDtypeStruct((2,) + s, BF) for s in shapes]
        + [jax.ShapeDtypeStruct(s, BF) for s in shapes] * 2
        + [jax.ShapeDtypeStruct((features, ff), BF)]
        + [jax.ShapeDtypeStruct((2, many, width) if scatter else (many, features), BF)]
        + (scatter_outs if scatter else []),
        in_specs=[hbm] + [vmem] * 3 + [hbm] * 8 + [hbm] * 3 + [vmem] * 4 + [hbm],
        out_specs=[hbm] * 15 + ([hbm] * 8 + [vmem] if scatter else []),
        scratch_shapes=[
            pltpu.VMEM((nz, 4, tokens, att), BF),
            pltpu.VMEM(shapes[2], BF),
            pltpu.VMEM(shapes[3], BF),
            dma((7, 4)),
            dma((2, groups, nz)),
            dma((max(groups, 2),)),
            dma((4,)),
        ]
        + (scatter_scratch if scatter else [])
        + Chain.scratch(arrays),
        compiler_params=pltpu.CompilerParams(collective_id=3, has_side_effects=True, vmem_limit_bytes=60 << 20),
        cost_estimate=pl.CostEstimate(
            flops=12 * (att // HD) * total * total * HD * 4, bytes_accessed=1 << 29, transcendentals=0
        ),
        name="back",
    )(land, cos_t, sin_t, start, cotangent, normed, wq, wo, branch_ff, branch_y, d_hidden, wu, block_input, grad_output, stats,
      gain, out_bias, down_bias, up_bias_part, down)
    return results[0], results[1:5], results[14], results[21:]


def widen(source, out_shape, block, in_map, out_map, grid):
    def body(source_ref, out_ref):
        out_ref[...] = source_ref[0].astype(F32)

    return pl.pallas_call(
        body,
        out_shape=jax.ShapeDtypeStruct(out_shape, F32),
        grid=grid,
        in_specs=[pl.BlockSpec((1,) + block, in_map)],
        out_specs=pl.BlockSpec(block, out_map),
        compiler_params=pltpu.CompilerParams(vmem_limit_bytes=32 << 20),
        cost_estimate=pl.CostEstimate(flops=0, bytes_accessed=source.size * 6, transcendentals=0),
        name="widen",
    )(source)


def widen_rows(source):
    _, rows, columns = source.shape
    size = min(rows, (1 << 18) // columns)
    steps = rows // size
    return widen(
        source, (2 * rows, columns), (size, columns), lambda i, h: (h, i, 0), lambda i, h: (h * steps + i, 0), (steps, 2)
    )


def widen_columns(source):
    _, rows, columns = source.shape
    if columns % 128:
        return jnp.concatenate([source[0], source[1]], axis=1).astype(F32)
    size = min(rows, (1 << 18) // columns)
    return widen(
        source, (rows, 2 * columns), (size, columns), lambda i, h: (h, i, 0), lambda i, h: (i, h), (rows // size, 2)
    )


def widen_blocks(source):
    _, rows, columns = source.shape
    rows = rows // 4
    return widen(
        source, (2 * rows, 4 * columns), (rows, columns), lambda h, j: (h, j, 0), lambda h, j: (h, j), (2, 4)
    )


def scatter_sum(share):
    whole = lax.psum_scatter(share.astype(BF), "dp", scatter_dimension=0, tiled=True)
    return lax.psum_scatter(whole, "tensor", scatter_dimension=2, tiled=True).astype(F32)


def butterfly(value, axes):
    for axis, size in axes:
        mask = 1
        while mask < size:
            value = value + swap(value, axis, size, mask)
            mask *= 2
    return value


SCHEDULE = ((0, 1, 1, 1), (0, 1, 0, 1))
HOME_APART = 2
LATER = {26: ["output"], 28: ["norm_sums"], 29: ["norm_sums_core"], 31: ["norm_back"], 32: ["dp"], 33: ["blk_1"], 34: ["blk_2"]}


def local(
    nx, nz, nt, block_input, segment_ids, layer_norm_gain, layer_norm_bias, qkv_weight, qkv_bias, out_weight, out_bias,
    up_weight, up_bias, down_weight, down_bias, grad_output,
):
    rows, tokens, width = block_input.shape
    all_rows = nx * rows
    features = nt * width
    many = all_rows * tokens
    x, z, t = lax.axis_index("dp"), lax.axis_index("blk"), lax.axis_index("tensor")
    att = qkv_weight.shape[2] // nx
    ff = up_weight.shape[1] // nx

    split = att % 128 == 0
    gather = nt == 4 and nx == 2 and split
    qkv_whole = jnp.transpose(qkv_weight, (1, 0, 2))
    qkv_half = lax.dynamic_slice_in_dim(qkv_whole, x * att, att, 2)
    out_half = lax.dynamic_slice_in_dim(out_weight, x * att, att, 0)
    if split:
        weights = [qkv_whole, out_weight, up_weight, down_weight]
        first_biases = [qkv_bias, up_bias.reshape(1, nx * ff)]
    else:
        up_half = lax.dynamic_slice_in_dim(up_weight, x * ff, ff, 1)
        down_half = lax.dynamic_slice_in_dim(down_weight, x * ff, ff, 0)
        weights = [qkv_half, out_half, up_half, down_half]
        first_biases = [
            lax.dynamic_slice_in_dim(qkv_bias, x * att, att, 1),
            lax.dynamic_slice_in_dim(up_bias, x * ff, ff, 0).reshape(1, ff),
        ]

    frequency = np.exp(np.arange(ROT // 2) * (-2.0 / ROT) * ROPE_LOG_BASE).astype(np.float32)[:, None]

    if gather:
        sources = [block_input.reshape(rows * tokens, width), grad_output.reshape(rows * tokens, width)]
    else:
        sources = [lax.all_gather(a, "tensor", axis=2, tiled=True) for a in (block_input, grad_output)]
        sources = [lax.all_gather(a, "dp", axis=0, tiled=True).reshape(many, features) for a in sources]
    normed, cotangent, land, stats, down_part, d_hidden, branch_ff, up_bias_part, cos_t, sin_t, start, branch_y = front(
        gather, split, rows, tokens, nz, many, features, att, ff,
        [
            segment_ids, jnp.asarray(frequency), *sources, layer_norm_gain.reshape(1, features), layer_norm_bias.reshape(1, features), weights[0],
            first_biases[0], weights[1], weights[2], first_biases[1], weights[3],
        ],
    )
    home, sums, d_normed_ff, results = back(
        gather, split, tokens, land, cos_t, sin_t, start, cotangent, normed, weights[0], weights[1], branch_ff, branch_y,
        d_hidden, weights[2], down_part, block_input.reshape(rows * tokens, width),
        grad_output.reshape(rows * tokens, width), stats, layer_norm_gain.reshape(1, features), out_bias.reshape(1, width),
        down_bias.reshape(1, width), up_bias_part,
    )
    down_sum, up_sum, out_sum, qkv_sum = sums
    chunks = Chain.layout(weight_arrays(down_part.shape, d_hidden.shape, features, att))[0][-Chain.APART :]
    first = chunks[0][1]
    last_rows = lax.dynamic_slice(qkv_sum, (x, first, 0), (1, 3 * features - first, att))
    last_rows = lax.ppermute(last_rows, "dp", [(0, 1), (1, 0)])
    qkv_sum = lax.dynamic_update_slice(qkv_sum, last_rows, (1 - x, first, 0))
    if gather:
        block_output, input_grad, small = results
        block_output = block_output.reshape(rows, tokens, width)
        input_grad = input_grad.reshape(rows, tokens, width)
        gain_grad, shift_grad, bias_grad = small[0], small[1], small[2]
        units = nx * ff // width
        up_bias_grad = small[3 : 3 + units].reshape(nx * ff)
        qkv_bias_grad = small[3 + units : 6 + units]
    else:
        home = home.reshape(4, many, att)
        qkv_bias_part = jnp.sum(home[:3].astype(F32), axis=1)
        branch = branch_ff.astype(F32) + dot32(home[3], out_half)
        d_normed = d_normed_ff.astype(F32)
        for i in range(3):
            d_normed = d_normed + dot32(home[i], qkv_half[i].T)
        branch = scatter_sum(branch.reshape(all_rows, tokens, features))
        d_normed = scatter_sum(d_normed.reshape(all_rows, tokens, features))
        block_output = (block_input.astype(F32) + (branch + out_bias + down_bias)).astype(BF)

        stats = lax.dynamic_slice_in_dim(stats, x * rows * tokens, rows * tokens, 0).reshape(rows, tokens, 128)
        own_mean, own_inverse = stats[..., :1], stats[..., 64:65]
        xhat = (block_input.astype(F32) - own_mean) * own_inverse
        gain = lax.dynamic_slice_in_dim(layer_norm_gain, t * width, width, 0)
        scaled = d_normed * gain
        moments = jnp.stack([jnp.sum(scaled, axis=-1), jnp.sum(scaled * xhat, axis=-1)])
        moments = butterfly(moments, [("tensor", nt)]) / features
        first, second = moments[0][..., None], moments[1][..., None]
        input_grad = (
            grad_output.astype(F32) + own_inverse * (scaled - first - xhat * second)
        ).astype(BF)

        def spread(part, whole):
            shape = part.shape[:-1] + (whole,)
            at = (0,) * (part.ndim - 1) + (x * part.shape[-1],)
            return lax.dynamic_update_slice(jnp.zeros(shape, F32), part, at)

        small = [
            jnp.sum(d_normed * xhat, axis=(0, 1)),
            jnp.sum(d_normed, axis=(0, 1)),
            jnp.sum(grad_output.astype(F32), axis=(0, 1)),
            spread(up_bias_part[0], nx * ff),
            spread(qkv_bias_part, nx * att).reshape(-1),
        ]
        packed = butterfly(jnp.concatenate(small), [("dp", nx), ("blk", nz)])
        gain_grad, shift_grad, bias_grad = (packed[i * width : (i + 1) * width] for i in range(3))
        up_bias_grad = packed[3 * width : 3 * width + nx * ff]
        qkv_bias_grad = packed[3 * width + nx * ff :].reshape(3, nx * att)

    down_grad = widen_rows(down_sum)
    up_grad = widen_columns(up_sum)
    out_grad = widen_blocks(out_sum)
    qkv_grad = widen_columns(qkv_sum).reshape(3, features, nx * att)
    qkv_grad = jnp.transpose(qkv_grad, (1, 0, 2))
    return (
        block_output, input_grad, gain_grad, shift_grad, qkv_grad, qkv_bias_grad, out_grad, bias_grad, up_grad,
        up_bias_grad, down_grad, bias_grad,
    )


def solution(mesh):
    in_specs = (
        P("dp", "blk", "tensor"), P("dp", None), P(), P(), P(None, None, "tensor"), P(None, "tensor"), P("tensor", None),
        P("tensor"), P(None, "tensor"), P("tensor"), P("tensor", None), P("tensor"), P("dp", "blk", "tensor"),
    )
    out_specs = (
        P("dp", "blk", "tensor"), P("dp", "blk", "tensor"), P("tensor"), P("tensor"), P(None, None, "tensor"),
        P(None, "tensor"), P("tensor", None), P("tensor"), P(None, "tensor"), P("tensor"), P("tensor", None), P("tensor"),
    )
    body = functools.partial(local, mesh.shape["dp"], mesh.shape["blk"], mesh.shape["tensor"])
    return jax.shard_map(body, mesh=mesh, in_specs=in_specs, out_specs=out_specs, check_vma=False)
```
